128 devices in a mesh: ctx: 32 (over y, x, core), dp: 4 (over z).
Axes of the slice: x: 4, y: 4, z: 4, core: 2. Of those that a mesh axis runs over, the one named last changes fastest.
Arguments:
- tokens: bfloat16 [4, 16384, 2048], P('dp', 'ctx'), may hold values from -6 to 6
- w_query: bfloat16 [2048, 1024], replicated, may hold values from -0.125 to 0.125
- w_key: bfloat16 [2048, 1024], replicated, may hold values from -0.125 to 0.125
- w_value: bfloat16 [2048, 1024], replicated, may hold values from -0.125 to 0.125
- cotangent: bfloat16 [4, 16384, 1024], P('dp', 'ctx'), may hold values from -6 to 6
Outputs:
- attn_out: bfloat16 [4, 16384, 1024], P('dp', 'ctx')
- input_grad: bfloat16 [4, 16384, 2048], P('dp', 'ctx')
- grad_query: float32 [2048, 1024], P(('ctx', 'dp'))
- grad_key: float32 [2048, 1024], P(('ctx', 'dp'))
- grad_value: float32 [2048, 1024], P(('ctx', 'dp'))
The draws below stay inside these ranges and needn't reach their ends.
All inputs are finite; a program needn't handle non-finite values.
Results may differ from the reference program's by a relative error of at most 0.022.
Values may be sent and summed in bfloat16 or wider, within the bound.
No kernel may reach another device: no remote copies, remote signals or barrier semaphores. Data moves between devices by JAX's collectives and lax.ppermute only.
A program may use at most 192 MiB of HBM per device.

```python
import jax
import jax.numpy as jnp
from jax import lax

D = 2048
HEADS = 8
DH = 128
TOK_DEV = 512
SEQ = 16384
SEQS = 4
HD = 1024


def with_spikes(values, stream_key, source, target, shards_of, factor):
    owner, partner = [(jnp.arange(values.shape[dim]) // (values.shape[dim] // shards_of)).reshape([-1 if axis == dim else 1 for axis in range(values.ndim)]) for dim in (source, target)]
    chosen = jax.random.permutation(stream_key, shards_of)[partner]
    strong = (owner == chosen) | (owner == (partner + shards_of // 2) % shards_of)
    return jnp.where(strong, factor * values, values)


def shard_levels(rng, dims, cuts, smallest, largest):
    level = 1.0
    for axis_at, shards_of in cuts:
        draws = jax.random.uniform(jax.random.fold_in(jax.random.fold_in(rng, 6), axis_at), (shards_of,), jnp.float32, smallest / len(cuts), largest / len(cuts))
        level = level * jnp.repeat(jnp.exp(draws), dims[axis_at] // shards_of).reshape((-1,) + (1,) * (len(dims) - 1 - axis_at))
    return level


def noise(own_key, extent, scale, most, shards=(), kind=jnp.bfloat16):
    drawn = scale * jax.random.normal(own_key, extent, jnp.float32)
    if shards:
        drawn = drawn * shard_levels(own_key, extent, shards, -0.22, 0.18)
    return jnp.clip(drawn, -most, most).astype(kind)


def heavy_noise(rng, dims, deviation, limit, shards, heavy, kind=jnp.bfloat16):
    values = deviation * jax.random.normal(rng, dims, jnp.float32)
    if shards:
        values = values * shard_levels(rng, dims, shards, -0.22, 0.18)
    return jnp.clip(with_spikes(values, jax.random.fold_in(rng, 3), *heavy), -limit, limit).astype(kind)


def setup_inputs(seed: int = 0) -> dict:
    splits = jax.random.split(jax.random.key(seed), 6)
    tokens = heavy_noise(splits[0], (SEQS, SEQ, D), 1.0, 6.0, ((0, 4), (1, 32)), (1, 2, 32, 2.75))
    w_query = noise(splits[1], (D, HD), D ** -0.5, 0.125)
    w_key = noise(splits[2], (D, HD), D ** -0.5, 0.125)
    w_value = noise(splits[3], (D, HD), D ** -0.5, 0.125)
    cotangent = noise(splits[4], (SEQS, SEQ, HD), 1.0, 6.0, ((0, 4), (1, 32)))
    return {"tokens": tokens, "w_query": w_query, "w_key": w_key, "w_value": w_value, "cotangent": cotangent}


EPS = 1e-05

def round_trip(value):
    return lax.optimization_barrier(value.astype(jnp.bfloat16)).astype(jnp.float32)

def one_sequence(tokens, cotangent, w_query, w_key, w_value):
    blocks = SEQ // TOK_DEV
    query = jnp.dot(tokens, w_query, preferred_element_type=jnp.float32).astype(jnp.bfloat16)
    key = jnp.dot(tokens, w_key, preferred_element_type=jnp.float32).astype(jnp.bfloat16)
    value = jnp.dot(tokens, w_value, preferred_element_type=jnp.float32).astype(jnp.bfloat16)

    def split(array):
        return array.astype(jnp.float32).reshape(blocks, TOK_DEV, HEADS, DH)
    qb, kb, vb = (split(query), split(key), split(value))
    rows = jnp.arange(TOK_DEV, dtype=jnp.int32)
    causal = (rows[:, None] >= rows[None, :]).astype(jnp.float32)
    state = round_trip(jnp.einsum('ntha,nthb->nhab', kb, vb))
    zero_state = jnp.zeros((1, HEADS, DH, DH), jnp.float32)
    prefix = round_trip(jnp.concatenate([zero_state, jnp.cumsum(state, axis=0)[:-1]], axis=0))
    scores = round_trip(jnp.einsum('ntha,nsha->nhts', qb, kb) * causal)
    mixed = jnp.einsum('nhts,nshb->nthb', scores, vb) + jnp.einsum('ntha,nhab->nthb', qb, prefix)
    inverse = lax.rsqrt(lax.optimization_barrier(jnp.mean(mixed * mixed, axis=-1, keepdims=True)) + EPS)
    normed = mixed * inverse
    attn_out = normed.astype(jnp.bfloat16).reshape(SEQ, HEADS * DH)
    upstream = split(cotangent)
    grad_mixed = round_trip((upstream - normed * lax.optimization_barrier(jnp.mean(upstream * normed, axis=-1, keepdims=True))) * inverse)
    back = round_trip(jnp.einsum('ntha,nthb->nhab', qb, grad_mixed))
    later = jnp.cumsum(back[::-1], axis=0)[::-1]
    suffix = round_trip(jnp.concatenate([later[1:], zero_state], axis=0))
    grad_scores = round_trip(jnp.einsum('nthb,nshb->nhts', grad_mixed, vb) * causal)
    grad_q = jnp.einsum('nhts,nsha->ntha', grad_scores, kb) + jnp.einsum('nthb,nhab->ntha', grad_mixed, prefix)
    grad_k = jnp.einsum('nhts,ntha->nsha', grad_scores, qb) + jnp.einsum('nshb,nhab->nsha', vb, suffix)
    grad_v = jnp.einsum('nhts,nthb->nshb', scores, grad_mixed) + jnp.einsum('nsha,nhab->nshb', kb, suffix)
    grad_q = grad_q.astype(jnp.bfloat16).reshape(SEQ, HEADS * DH)
    grad_k = grad_k.astype(jnp.bfloat16).reshape(SEQ, HEADS * DH)
    grad_v = grad_v.astype(jnp.bfloat16).reshape(SEQ, HEADS * DH)
    input_grad = (jnp.dot(grad_q, w_query.T, preferred_element_type=jnp.float32) + jnp.dot(grad_k, w_key.T, preferred_element_type=jnp.float32) + jnp.dot(grad_v, w_value.T, preferred_element_type=jnp.float32)).astype(jnp.bfloat16)
    combined = jnp.concatenate([grad_q, grad_k, grad_v], axis=1)
    weights = jnp.dot(tokens.T, combined, preferred_element_type=jnp.float32)
    return (attn_out, input_grad, weights)

def reference(tokens, w_query, w_key, w_value, cotangent):

    def run(pair):
        return one_sequence(pair[0], pair[1], w_query, w_key, w_value)
    attn_out, input_grad, weights = lax.map(run, (tokens, cotangent))
    summed = lax.optimization_barrier(jnp.sum(weights, axis=0)) * float(SEQS * SEQ) ** (-0.5)
    width = HEADS * DH
    return (attn_out, input_grad, summed[:, :width], summed[:, width:2 * width], summed[:, 2 * width:])
```

```python
import jax
import jax.numpy as jnp
from jax import lax
from jax.experimental import pallas as pl
from jax.experimental.pallas import tpu as pltpu
from jax.sharding import Mesh
from jax.sharding import PartitionSpec as P

DH = 128
TOK = 512
EPS = 1e-05
CTX = ("y", "x", "c")
CTX_DP = ("y", "x", "c", "z")
CHIPS = ("y", "x", "z")
BF = jnp.bfloat16
F32 = jnp.float32
MB = 1 << 20


def dot(a, b, ca=1, cb=0):
    return lax.dot_general(a, b, (((ca,), (cb,)), ((), ())), preferred_element_type=F32)


def causal(x):
    rows = lax.broadcasted_iota(jnp.int32, x.shape, 0)
    cols = lax.broadcasted_iota(jnp.int32, x.shape, 1)
    return jnp.where(rows >= cols, x, 0.0).astype(BF)


def head(h):
    return slice(h * DH, (h + 1) * DH)


def call(kernel, core, grid, ins, outs, flops, moved):
    return pl.pallas_call(
        kernel,
        out_shape=[jax.ShapeDtypeStruct(s, d) for s, d, _, _ in outs],
        grid_spec=pltpu.PrefetchScalarGridSpec(
            num_scalar_prefetch=1,
            grid=(grid,),
            in_specs=[pl.BlockSpec(b, m) for _, b, m in ins],
            out_specs=[pl.BlockSpec(b, m) for _, _, b, m in outs],
        ),
        compiler_params=pltpu.CompilerParams(
            dimension_semantics=("arbitrary",), vmem_limit_bytes=48 * MB
        ),
        cost_estimate=pl.CostEstimate(flops=flops, bytes_accessed=moved, transcendentals=0),
    )(core, *[a for a, _, _ in ins])


def whole(j, c):
    return (0, 0)


def tall(j, c):
    return (j, 0)


def wide(j, c):
    return (0, j)


def mine(j, c):
    return (0, c[0] * 2 + j)


def project_qkv(core, tok, wq, wk, wv):
    def kernel(c, t, a, b, d, q, k, v, s):
        x = t[...]
        q[...] = dot(x, a[...]).astype(BF)
        kk = dot(x, b[...]).astype(BF)
        vv = dot(x, d[...]).astype(BF)
        k[...] = kk
        v[...] = vv
        for h in range(2):
            s[head(h), :] = dot(kk[:, head(h)], vv[:, head(h)], 0, 0).astype(BF)

    w = (2048, 256)
    return call(
        kernel,
        core,
        2,
        [(tok, (TOK, 2048), whole), (wq, w, mine), (wk, w, mine), (wv, w, mine)],
        [((TOK, 512), BF, (TOK, 256), wide)] * 3 + [((512, DH), BF, (256, DH), tall)],
        3300000000,
        10 * MB,
    )


def project_kv(core, tok, wk, wv, state):
    def kernel(c, t, b, d, so, k, v, s, total):
        x = t[...]
        kk = dot(x, b[...]).astype(BF)
        vv = dot(x, d[...]).astype(BF)
        k[...] = kk
        v[...] = vv
        for h in range(2):
            st = dot(kk[:, head(h)], vv[:, head(h)], 0, 0).astype(BF)
            s[head(h), :] = st
            total[head(h), :] = (st.astype(F32) + so[head(h), :].astype(F32)).astype(BF)

    w = (2048, 256)
    return call(
        kernel,
        core,
        2,
        [(tok, (TOK, 2048), whole), (wk, w, mine), (wv, w, mine), (state, (256, DH), tall)],
        [((TOK, 512), BF, (TOK, 256), wide)] * 2 + [((512, DH), BF, (256, DH), tall)] * 2,
        2200000000,
        7 * MB,
    )


def within(core, tok_o, tok_p, wq, q_o, k_o, v_o, k_p, v_p):
    def kernel(c, to, tp, a, qo, ko, vo, kp, vp, qp, io, ip, tto, ttp):
        qq = dot(tp[...], a[...]).astype(BF)
        qp[...] = qq
        for q, k, v, out in ((qo[...], ko, vo, io), (qq, kp, vp, ip)):
            for h in range(2):
                scores = causal(dot(q[:, head(h)], k[:, head(h)], 1, 1))
                out[:, head(h)] = dot(scores, v[:, head(h)])
        cols = pl.ds(pl.multiple_of(pl.program_id(0) * 1024, 1024), 1024)
        tto[...] = to[:, cols].T
        ttp[...] = tp[:, cols].T

    b = (TOK, 256)
    return call(
        kernel,
        core,
        2,
        [(tok_o, (TOK, 2048), whole), (tok_p, (TOK, 2048), whole), (wq, (2048, 256), mine)]
        + [(t, b, wide) for t in (q_o, k_o, v_o, k_p, v_p)],
        [((TOK, 512), BF, b, wide)]
        + [((TOK, 512), F32, b, wide)] * 2
        + [((2048, TOK), BF, (1024, TOK), tall)] * 2,
        2200000000,
        15 * MB,
    )


def normed(core, i_o, i_p, q_o, q_p, p_o, p_p, cot, cot_p):
    def kernel(c, io, ip, qo, qp, po, pp, co, cp, ao, ap, go, gp, bo, bp, total):
        backs = []
        for i, q, p, ct, a, g, b in ((io, qo, po, co, ao, go, bo), (ip, qp, pp, cp, ap, gp, bp)):
            for h in range(2):
                qh = q[:, head(h)]
                mixed = i[:, head(h)] + dot(qh, p[head(h), :])
                inverse = lax.rsqrt(jnp.mean(mixed * mixed, axis=-1, keepdims=True) + EPS)
                n = mixed * inverse
                up = ct[:, head(h)].astype(F32)
                a[:, head(h)] = n.astype(BF)
                gm = ((up - n * jnp.mean(up * n, axis=-1, keepdims=True)) * inverse).astype(BF)
                g[:, head(h)] = gm
                back = dot(qh, gm, 0, 0).astype(BF)
                b[head(h), :] = back
                backs.append(back.astype(F32))
        for h in range(2):
            total[head(h), :] = (backs[h] + backs[2 + h]).astype(BF)

    b = (TOK, 256)
    s = (256, DH)
    return call(
        kernel,
        core,
        2,
        [(t, b, wide) for t in (i_o, i_p, q_o, q_p)]
        + [(p_o, s, tall), (p_p, s, tall), (cot, b, mine), (cot_p, b, wide)],
        [((TOK, 512), BF, b, wide)] * 4 + [((512, DH), BF, s, tall)] * 3,
        300000000,
        7 * MB,
    )


def grads_within(core, q_o, q_p, k_o, k_p, v_o, v_p, g_o, g_p, p_o, p_p):
    def kernel(c, qo, qp, ko, kp, vo, vp, go, gp, po, pp, dqo, dqp, dko, dkp, dvo, dvp):
        for q, k, v, g, p, dq, dk, dv in (
            (qo, ko, vo, go, po, dqo, dko, dvo),
            (qp, kp, vp, gp, pp, dqp, dkp, dvp),
        ):
            for h in range(2):
                qh, kh, vh, gh = (t[:, head(h)] for t in (q, k, v, g))
                gs = causal(dot(gh, vh, 1, 1))
                dq[:, head(h)] = (dot(gs, kh) + dot(gh, p[head(h), :], 1, 1)).astype(BF)
                dk[:, head(h)] = dot(gs, qh, 0, 0)
                scores = causal(dot(qh, kh, 1, 1))
                dv[:, head(h)] = dot(scores, gh, 0, 0)

    b = (TOK, 256)
    s = (256, DH)
    return call(
        kernel,
        core,
        2,
        [(t, b, wide) for t in (q_o, q_p, k_o, k_p, v_o, v_p, g_o, g_p)]
        + [(p_o, s, tall), (p_p, s, tall)],
        [((TOK, 512), BF, b, wide)] * 2 + [((TOK, 512), F32, b, wide)] * 4,
        2700000000,
        9 * MB,
    )


def grads_after(core, k_o, k_p, v_o, v_p, dk_o, dk_p, dv_o, dv_p, s_o, s_p):
    def kernel(c, ko, kp, vo, vp, ako, akp, avo, avp, so, sp, dko, dkp, dvo, dvp):
        for k, v, ak, av, s, dk, dv in (
            (ko, vo, ako, avo, so, dko, dvo),
            (kp, vp, akp, avp, sp, dkp, dvp),
        ):
            for h in range(2):
                dk[:, head(h)] = (ak[:, head(h)] + dot(v[:, head(h)], s[head(h), :], 1, 1)).astype(BF)
                dv[:, head(h)] = (av[:, head(h)] + dot(k[:, head(h)], s[head(h), :])).astype(BF)

    b = (TOK, 256)
    s = (256, DH)
    return call(
        kernel,
        core,
        2,
        [(t, b, wide) for t in (k_o, k_p, v_o, v_p, dk_o, dk_p, dv_o, dv_p)]
        + [(s_o, s, tall), (s_p, s, tall)],
        [((TOK, 512), BF, b, wide)] * 4,
        200000000,
        8 * MB,
    )


def weight_grad(core, tt_o, tt_p, grads):
    n = len(grads)

    def kernel(c, to, tp, *refs):
        out = refs[-1]
        for m in range(n):
            part = dot(to[...], refs[2 * m][...]) + dot(tp[...], refs[2 * m + 1][...])
            part = part.astype(BF)
            for x in range(4):
                for core_at in range(2):
                    for z in range(4):
                        row = x * 128 + core_at * 64 + z * 16
                        out[0, x, z, core_at * 16 : core_at * 16 + 16, m * 512 : m * 512 + 512] = part[
                            row : row + 16, :
                        ]

    flat = [t for pair in grads for t in pair]
    return call(
        kernel,
        core,
        4,
        [(tt_o, (512, TOK), tall), (tt_p, (512, TOK), tall)]
        + [(t, (TOK, 512), whole) for t in flat],
        [
            (
                (4, 4, 4, 32, n * 512),
                BF,
                (1, 4, 4, 32, n * 512),
                lambda j, c: (j, 0, 0, 0, 0),
            )
        ],
        2200000000 * n,
        (5 + 3 * n) * MB,
    )[0]


def input_part(core, grads, weights, received=None):
    def kernel(c, *refs):
        out = refs[-1]
        total = dot(refs[0][...], refs[3][...], 1, 1)
        total = total + dot(refs[1][...], refs[4][...], 1, 1)
        total = total + dot(refs[2][...], refs[5][...], 1, 1)
        if received is not None:
            total = total + refs[6][...].astype(F32)
        out[...] = total.astype(BF)

    ins = [(g, (TOK, 512), whole) for g in grads]
    ins += [(w, (512, 512), lambda j, c: (j, c[0])) for w in weights]
    if received is not None:
        ins.append((received, (TOK, 512), wide))
    return call(
        kernel, core, 4, ins, [((TOK, 2048), BF, (TOK, 512), wide)], 3300000000, 10 * MB
    )[0]


def shift(v, axis, d):
    n = lax.axis_size(axis)
    return lax.ppermute(v, axis, [(i, (i + d) % n) for i in range(n)])


def swap(v):
    return lax.ppermute(v, "c", [(0, 1), (1, 0)])


def scan_chips(total, reverse):
    before = None
    running = total
    for axis in ("x", "y"):
        at = lax.axis_index(axis)
        inside = jnp.zeros(total.shape, F32)
        row = running.astype(F32)
        for d in (1, 3, 2):
            piece = shift(running, axis, d).astype(F32)
            passed = at + (4 - d) < 4 if reverse else at >= d
            inside = inside + jnp.where(passed, piece, 0.0)
            row = row + piece
        before = inside if before is None else before + inside
        running = row.astype(BF)
    return before


def per_device(tokens, w_query, w_key, w_value, cotangent):
    c = lax.axis_index("c")
    core = c.astype(jnp.int32).reshape(1)
    tok_o = tokens[0]
    cot = cotangent[0]
    tok_p = swap(tok_o)
    cot_p = swap(lax.dynamic_slice(cot, (0, (1 - c) * 512), (TOK, 512)))

    q_o, k_o, v_o, state_o = project_qkv(core, tok_o, w_query, w_key, w_value)
    k_p, v_p, state_p, total = project_kv(core, tok_p, w_key, w_value, state_o)
    before = scan_chips(total, False)
    q_p, i_o, i_p, tt_o, tt_p = within(core, tok_o, tok_p, w_query, q_o, k_o, v_o, k_p, v_p)
    late = c == 1
    p_o = (before + jnp.where(late, state_p.astype(F32), 0.0)).astype(BF)
    p_p = (before + jnp.where(late, 0.0, state_o.astype(F32))).astype(BF)
    a_o, a_p, g_o, g_p, back_o, back_p, total = normed(
        core, i_o, i_p, q_o, q_p, p_o, p_p, cot, cot_p
    )
    after = scan_chips(total, True)
    a_r = swap(a_p)
    dq_o, dq_p, dk_o, dk_p, dv_o, dv_p = grads_within(
        core, q_o, q_p, k_o, k_p, v_o, v_p, g_o, g_p, p_o, p_p
    )
    part_q = weight_grad(core, tt_o, tt_p, [(dq_o, dq_p)])
    s_o = (after + jnp.where(late, 0.0, back_p.astype(F32))).astype(BF)
    s_p = (after + jnp.where(late, back_o.astype(F32), 0.0)).astype(BF)
    dk_o, dk_p, dv_o, dv_p = grads_after(
        core, k_o, k_p, v_o, v_p, dk_o, dk_p, dv_o, dv_p, s_o, s_p
    )
    part_kv = weight_grad(core, tt_o, tt_p, [(dk_o, dk_p), (dv_o, dv_p)])

    def to_owners(part):
        blocks = part.reshape(64, 32, part.shape[-1])
        blocks = lax.all_to_all(blocks, CHIPS, 0, 0, tiled=True)
        return jnp.sum(blocks.astype(F32), axis=0)

    sum_q = to_owners(part_q)
    sum_kv = to_owners(part_kv)
    weights = (w_query, w_key, w_value)
    ig_p = swap(input_part(core, (dq_p, dk_p, dv_p), weights))
    input_grad = input_part(core, (dq_o, dk_o, dv_o), weights, ig_p)
    attn_out = jnp.where(
        late, jnp.concatenate([a_r, a_o], axis=1), jnp.concatenate([a_o, a_r], axis=1)
    )
    summed = jnp.concatenate([sum_q, sum_kv], axis=1) * (65536.0**-0.5)
    own = lax.dynamic_slice(summed, (c * 16, 0), (16, 1536))
    other = lax.dynamic_slice(summed, ((1 - c) * 16, 0), (16, 1536))
    other = swap(other.astype(BF)).astype(F32)

    def joined(k):
        mine_k, other_k = own[:, k * 512 : k * 512 + 512], other[:, k * 512 : k * 512 + 512]
        return jnp.where(
            late,
            jnp.concatenate([other_k, mine_k], axis=1),
            jnp.concatenate([mine_k, other_k], axis=1),
        )

    return (attn_out[None], input_grad[None], joined(0), joined(1), joined(2))


def solution(mesh):
    finer = Mesh(mesh.devices.reshape(4, 4, 2, mesh.shape["dp"]), ("y", "x", "c", "z"))
    return jax.shard_map(
        per_device,
        mesh=finer,
        in_specs=(P("z", CTX, None), P(), P(), P(), P("z", CTX, None)),
        out_specs=(
            P("z", CTX, None),
            P("z", CTX, None),
            P(CTX_DP, None),
            P(CTX_DP, None),
            P(CTX_DP, None),
        ),
        check_vma=False,
    )
```

```python
import jax
import jax.numpy as jnp
from jax import lax
from jax.experimental import pallas as pl
from jax.experimental.pallas import tpu as pltpu
from jax.sharding import Mesh
from jax.sharding import PartitionSpec as P

DH = 128
TOK = 512
EPS = 1e-05
CTX = ("y", "x", "c")
CTX_DP = ("y", "x", "c", "z")
BF = jnp.bfloat16
F32 = jnp.float32
MB = 1 << 20


def dot(a, b, ca=1, cb=0):
    return lax.dot_general(a, b, (((ca,), (cb,)), ((), ())), preferred_element_type=F32)


def causal(x, first=0):
    rows = lax.broadcasted_iota(jnp.int32, x.shape, 0) + first
    cols = lax.broadcasted_iota(jnp.int32, x.shape, 1)
    return jnp.where(rows >= cols, x, 0.0).astype(BF)


def head(h):
    return slice(h * DH, (h + 1) * DH)


def call(kernel, core, grid, ins, outs, flops, moved):
    return pl.pallas_call(
        kernel,
        out_shape=[jax.ShapeDtypeStruct(s, d) for s, d, _, _ in outs],
        grid_spec=pltpu.PrefetchScalarGridSpec(
            num_scalar_prefetch=1,
            grid=(grid,),
            in_specs=[pl.BlockSpec(b, m) for _, b, m in ins],
            out_specs=[pl.BlockSpec(b, m) for _, _, b, m in outs],
        ),
        compiler_params=pltpu.CompilerParams(
            dimension_semantics=("arbitrary",), vmem_limit_bytes=30 * MB
        ),
        cost_estimate=pl.CostEstimate(flops=flops, bytes_accessed=moved, transcendentals=0),
    )(core, *[a for a, _, _ in ins])


def whole(j, c):
    return (0, 0)


def tall(j, c):
    return (j, 0)


def wide(j, c):
    return (0, j)


def mine(j, c):
    return (0, c[0] * 2 + j)


def project_qkv(core, tok, wq, wk, wv):
    def kernel(c, t, a, b, d, q, k, v, s):
        x = t[...]
        q[...] = dot(x, a[...]).astype(BF)
        kk = dot(x, b[...]).astype(BF)
        vv = dot(x, d[...]).astype(BF)
        k[...] = kk
        v[...] = vv
        for h in range(2):
            s[head(h), :] = dot(kk[:, head(h)], vv[:, head(h)], 0, 0).astype(BF)

    w = (2048, 256)
    return call(
        kernel,
        core,
        2,
        [(tok, (TOK, 2048), whole), (wq, w, mine), (wk, w, mine), (wv, w, mine)],
        [((TOK, 512), BF, (TOK, 256), wide)] * 3 + [((512, DH), BF, (256, DH), tall)],
        3300000000,
        10 * MB,
    )


def project_kv(core, tok, wk, wv, state):
    def kernel(c, t, b, d, so, k, v, s, total):
        x = t[...]
        kk = dot(x, b[...]).astype(BF)
        vv = dot(x, d[...]).astype(BF)
        k[...] = kk
        v[...] = vv
        for h in range(2):
            st = dot(kk[:, head(h)], vv[:, head(h)], 0, 0).astype(BF)
            s[head(h), :] = st
            total[head(h), :] = (st.astype(F32) + so[head(h), :].astype(F32)).astype(BF)

    w = (2048, 256)
    return call(
        kernel,
        core,
        2,
        [(tok, (TOK, 2048), whole), (wk, w, mine), (wv, w, mine), (state, (256, DH), tall)],
        [((TOK, 512), BF, (TOK, 256), wide)] * 2 + [((512, DH), BF, (256, DH), tall)] * 2,
        2200000000,
        7 * MB,
    )


def half_rows(x, r):
    return x[r * 256 : r * 256 + 256]


def attend(q, k, r):
    return causal(dot(half_rows(q, r), k[: r * 256 + 256], 1, 1), r * 256)


def rows_down(s0, s1, x):
    first = dot(s0, x[:256], 0, 0) + dot(s1[:, :256], x[256:], 0, 0)
    return first, dot(s1[:, 256:], x[256:], 0, 0)


def within(core, tok_p, wq, q_o, k_o, v_o, k_p, v_p):
    def kernel(c, tp, a, qo, ko, vo, kp, vp, qp, out):
        qq = dot(tp[...], a[...]).astype(BF)
        qp[...] = qq
        for n, (q, k, v) in enumerate(((qo[...], ko, vo), (qq, kp, vp))):
            for h in range(2):
                qh, kh, vh = q[:, head(h)], k[:, head(h)], v[:, head(h)]
                out[n * TOK : n * TOK + 256, head(h)] = dot(attend(qh, kh, 0), vh[:256])
                out[n * TOK + 256 : n * TOK + 512, head(h)] = dot(attend(qh, kh, 1), vh)

    b = (TOK, 256)
    return call(
        kernel,
        core,
        2,
        [(tok_p, (TOK, 2048), whole), (wq, (2048, 256), mine)]
        + [(t, b, wide) for t in (q_o, k_o, v_o, k_p, v_p)],
        [((TOK, 512), BF, b, wide), ((2 * TOK, 512), F32, (2 * TOK, 256), wide)],
        2200000000,
        10 * MB,
    )


def turned(core, tok_o, tok_p):
    def kernel(c, to, tp, out):
        out[:, :TOK] = to[...].T
        out[:, TOK:] = tp[...].T

    return call(
        kernel,
        core,
        4,
        [(tok_o, (TOK, 512), wide), (tok_p, (TOK, 512), wide)],
        [((2048, 2 * TOK), BF, (512, 2 * TOK), tall)],
        1000000,
        8 * MB,
    )[0]


def normed(core, intra, q_o, q_p, p_o, p_p, cot, cot_p):
    def kernel(c, it, qo, qp, po, pp, co, cp, ao, ap, g, bo, bp, total):
        backs = []
        for n, (q, p, ct, a, b) in enumerate(((qo, po, co, ao, bo), (qp, pp, cp, ap, bp))):
            rows = slice(n * TOK, n * TOK + TOK)
            for h in range(2):
                qh = q[:, head(h)]
                mixed = it[rows, head(h)] + dot(qh, p[head(h), :])
                inverse = lax.rsqrt(jnp.mean(mixed * mixed, axis=-1, keepdims=True) + EPS)
                nm = mixed * inverse
                up = ct[:, head(h)].astype(F32)
                a[:, head(h)] = nm.astype(BF)
                gm = ((up - nm * jnp.mean(up * nm, axis=-1, keepdims=True)) * inverse).astype(BF)
                g[rows, head(h)] = gm
                back = dot(qh, gm, 0, 0).astype(BF)
                b[head(h), :] = back
                backs.append(back.astype(F32))
        for h in range(2):
            total[head(h), :] = (backs[h] + backs[2 + h]).astype(BF)

    b = (TOK, 256)
    s = (256, DH)
    return call(
        kernel,
        core,
        2,
        [(intra, (2 * TOK, 256), wide)]
        + [(t, b, wide) for t in (q_o, q_p)]
        + [(p_o, s, tall), (p_p, s, tall), (cot, b, mine), (cot_p, b, wide)],
        [((TOK, 512), BF, b, wide)] * 2
        + [((2 * TOK, 512), BF, (2 * TOK, 256), wide)]
        + [((512, DH), BF, s, tall)] * 3,
        300000000,
        7 * MB,
    )


def grad_q_of(core, k_o, k_p, v_o, v_p, g, p_o, p_p):
    def kernel(c, ko, kp, vo, vp, gr, po, pp, dq):
        for n, (k, v, p) in enumerate(((ko, vo, po), (kp, vp, pp))):
            for h in range(2):
                kh, vh = k[:, head(h)], v[:, head(h)]
                gh = gr[n * TOK : n * TOK + TOK, head(h)]
                past = dot(gh, p[head(h), :], 1, 1)
                for r in range(2):
                    at = n * TOK + r * 256
                    now = dot(attend(gh, vh, r), kh[: r * 256 + 256])
                    dq[at : at + 256, head(h)] = (now + half_rows(past, r)).astype(BF)

    b = (TOK, 256)
    s = (256, DH)
    return call(
        kernel,
        core,
        2,
        [(t, b, wide) for t in (k_o, k_p, v_o, v_p)]
        + [(g, (2 * TOK, 256), wide), (p_o, s, tall), (p_p, s, tall)],
        [((2 * TOK, 512), BF, (2 * TOK, 256), wide)],
        1200000000,
        4 * MB,
    )[0]


def grads_within(core, q_o, q_p, k_o, k_p, v_o, v_p, g):
    def kernel(c, qo, qp, ko, kp, vo, vp, gr, dk, dv):
        for n, (q, k, v) in enumerate(((qo, ko, vo), (qp, kp, vp))):
            for h in range(2):
                qh, kh, vh = q[:, head(h)], k[:, head(h)], v[:, head(h)]
                gh = gr[n * TOK : n * TOK + TOK, head(h)]
                for left, right, x, out in ((gh, vh, qh, dk), (qh, kh, gh, dv)):
                    first, second = rows_down(attend(left, right, 0), attend(left, right, 1), x)
                    out[n * TOK : n * TOK + 256, head(h)] = first
                    out[n * TOK + 256 : n * TOK + 512, head(h)] = second

    b = (TOK, 256)
    return call(
        kernel,
        core,
        2,
        [(t, b, wide) for t in (q_o, q_p, k_o, k_p, v_o, v_p)] + [(g, (2 * TOK, 256), wide)],
        [((2 * TOK, 512), F32, (2 * TOK, 256), wide)] * 2,
        2000000000,
        9 * MB,
    )


def grads_after(core, k_o, k_p, v_o, v_p, dk, dv, s_o, s_p):
    def kernel(c, ko, kp, vo, vp, ak, av, so, sp, ok, ov):
        for n, (k, v, s) in enumerate(((ko, vo, so), (kp, vp, sp))):
            rows = slice(n * TOK, n * TOK + TOK)
            for h in range(2):
                sh = s[head(h), :]
                ok[rows, head(h)] = (ak[rows, head(h)] + dot(v[:, head(h)], sh, 1, 1)).astype(BF)
                ov[rows, head(h)] = (av[rows, head(h)] + dot(k[:, head(h)], sh)).astype(BF)

    b = (TOK, 256)
    s = (256, DH)
    both = (2 * TOK, 256)
    return call(
        kernel,
        core,
        2,
        [(t, b, wide) for t in (k_o, k_p, v_o, v_p)]
        + [(dk, both, wide), (dv, both, wide), (s_o, s, tall), (s_p, s, tall)],
        [((2 * TOK, 512), BF, both, wide)] * 2,
        200000000,
        8 * MB,
    )


def weight_grad(core, tt, grad, first, steps):
    n = len(steps)
    step_at = lambda j: sum(jnp.where(j == i, s, 0) for i, s in enumerate(steps))
    if first == "x":
        block = (4, 1, 8, 16, 2 * TOK)
        at = lambda j, c: (0, (c[2] + step_at(j)) % 4, 0, 0, 0)
    elif first == "y":
        block = (1, 4, 8, 16, 2 * TOK)
        at = lambda j, c: ((c[1] + step_at(j)) % 4, 0, 0, 0, 0)
    else:
        block = (2, 4, 8, 16, 2 * TOK)
        at = lambda j, c: (j, 0, 0, 0, 0)

    def kernel(c, t, g, out):
        rows = block[0] * block[1] * 128
        part = dot(t[...].reshape(rows, 2 * TOK), g[...]).astype(BF)
        j = pl.program_id(0)
        for a in range(block[0]):
            for b in range(block[1]):
                for core_at in range(2):
                    for z in range(4):
                        row = ((a * block[1] + b) * 2 + core_at) * 64 + z * 16
                        piece = part[row : row + 16, :]
                        here = slice(core_at * 16, core_at * 16 + 16)
                        dz = (z - c[3] + 4) % 4
                        if first == "x":
                            out[0, (a - c[1] + 4) % 4, dz, here, :] = piece
                        elif first == "y":
                            out[0, (b - c[2] + 4) % 4, dz, here, :] = piece
                        else:
                            dy = (j * 2 + a - c[1] + 4) % 4
                            out[dz, (b - c[2] + 4) % 4, dy, here, :] = piece

    if first == "z":
        grid, shape, out_block, out_at = 2, (4, 4, 4, 32, 512), (4, 4, 4, 32, 512), None
        out_at = lambda j, c: (0, 0, 0, 0, 0)
    else:
        grid, shape, out_block = n, (n, 4, 4, 32, 512), (1, 4, 4, 32, 512)
        out_at = lambda j, c: (j, 0, 0, 0, 0)
    return call(
        kernel,
        core,
        grid,
        [
            (tt.reshape(4, 4, 8, 16, 2 * TOK), block, at),
            (grad, (2 * TOK, 512), whole),
        ],
        [(shape, BF, out_block, out_at)],
        550000000 * n,
        (1 + 2 * n) * MB,
    )[0]


def input_part(core, slot, grads, weights, received=None):
    def kernel(c, *refs):
        out = refs[-1]
        total = dot(refs[0][...], refs[3][...], 1, 1)
        total = total + dot(refs[1][...], refs[4][...], 1, 1)
        total = total + dot(refs[2][...], refs[5][...], 1, 1)
        if received is not None:
            total = total + refs[6][...].astype(F32)
        out[...] = total.astype(BF)

    ins = [(g, (TOK, 512), lambda j, c: (slot, 0)) for g in grads]
    ins += [(w, (512, 512), lambda j, c: (j, c[0])) for w in weights]
    if received is not None:
        ins.append((received, (TOK, 512), wide))
    return call(
        kernel, core, 4, ins, [((TOK, 2048), BF, (TOK, 512), wide)], 3300000000, 10 * MB
    )[0]


def shift(v, axis, d):
    n = lax.axis_size(axis)
    return lax.ppermute(v, axis, [(i, (i + d) % n) for i in range(n)])


def swap(v):
    return lax.ppermute(v, "c", [(0, 1), (1, 0)])


def scan_axis(running, axis, reverse):
    at = lax.axis_index(axis)
    inside = jnp.zeros(running.shape, F32)
    row = running.astype(F32)
    for d in (1, 3, 2):
        piece = shift(running, axis, d).astype(F32)
        passed = at + (4 - d) < 4 if reverse else at >= d
        inside = inside + jnp.where(passed, piece, 0.0)
        row = row + piece
    return inside, row.astype(BF)


def together(*values):
    return lax.optimization_barrier(values)


def f32_sum(*parts):
    total = parts[0].astype(F32)
    for p in parts[1:]:
        total = total + p.astype(F32)
    return total.astype(BF)


def ring_out(far, axis):
    return shift(far[:2], axis, 1), shift(far[2:], axis, 3)


def ring_near(up, down, came, axis):
    from_left, from_right = came
    up = jnp.concatenate([f32_sum(up[:2], from_left), up[2:]], axis=0)
    down = jnp.concatenate([down[:2], f32_sum(down[2:], from_right)], axis=0)
    return shift(up, axis, 1), shift(down, axis, 3)


def spread(blocks, axis):
    return f32_sum(blocks[0], *[shift(blocks[d], axis, d) for d in (1, 3, 2)])


def per_device(tokens, w_query, w_key, w_value, cotangent):
    c = lax.axis_index("c")
    core = jnp.stack([lax.axis_index(a) for a in ("c", "y", "x", "z")]).astype(jnp.int32)
    tok_o = tokens[0]
    cot = cotangent[0]
    tok_p = swap(tok_o)
    late = c == 1
    cot_p = swap(jnp.where(late, cot[:, :512], cot[:, 512:]))

    q_o, k_o, v_o, state_o = project_qkv(core, tok_o, w_query, w_key, w_value)
    k_p, v_p, state_p, total = project_kv(core, tok_p, w_key, w_value, state_o)
    before, row = scan_axis(total, "x", False)
    q_p, intra = within(core, tok_p, w_query, q_o, k_o, v_o, k_p, v_p)
    row, intra, q_p = together(row, intra, q_p)
    rows_before, _ = scan_axis(row, "y", False)
    tt = turned(core, tok_o, tok_p)
    rows_before, tt = together(rows_before, tt)
    before = before + rows_before
    p_o = (before + jnp.where(late, state_p.astype(F32), 0.0)).astype(BF)
    p_p = (before + jnp.where(late, 0.0, state_o.astype(F32))).astype(BF)
    a_o, a_p, g, back_o, back_p, total = normed(core, intra, q_o, q_p, p_o, p_p, cot, cot_p)
    after, row = scan_axis(total, "x", True)
    dq = grad_q_of(core, k_o, k_p, v_o, v_p, g, p_o, p_p)
    part_q = weight_grad(core, tt, dq, "z", (0, 1, 2, 3))
    row, part_q = together(row, part_q)
    rows_after, _ = scan_axis(row, "y", True)
    came_q = ring_out(part_q[2], "z")
    dk, dv = grads_within(core, q_o, q_p, k_o, k_p, v_o, v_p, g)
    rows_after, dk, dv = together(rows_after, dk, dv)
    after = after + rows_after
    s_o = (after + jnp.where(late, 0.0, back_p.astype(F32))).astype(BF)
    s_p = (after + jnp.where(late, back_o.astype(F32), 0.0)).astype(BF)
    dk, dv = grads_after(core, k_o, k_p, v_o, v_p, dk, dv, s_o, s_p)
    far_k = weight_grad(core, tt, dk, "x", (2,))[0]
    far_v = weight_grad(core, tt, dv, "y", (2,))[0]
    far_k, far_v, *came_q = together(far_k, far_v, *came_q)
    near_q = ring_near(part_q[1], part_q[3], came_q, "z")
    came_k = ring_out(far_k, "x")
    came_v = ring_out(far_v, "y")
    near_k = weight_grad(core, tt, dk, "x", (1, 3, 0))
    near_v = weight_grad(core, tt, dv, "y", (1, 3, 0))
    near_k, near_v, *came = together(near_k, near_v, *came_k, *came_v)
    last_k = ring_near(near_k[0], near_k[1], came[:2], "x")
    last_v = ring_near(near_v[0], near_v[1], came[2:], "y")
    weights = (w_query, w_key, w_value)
    ig_p = input_part(core, 1, (dq, dk, dv), weights)
    ig_p, *last = together(ig_p, *last_k, *last_v, *near_q)
    sum_k = f32_sum(near_k[2], *last[:2])
    sum_v = f32_sum(near_v[2], *last[2:4])
    sum_q = f32_sum(part_q[0], *last[4:])
    sum_k = spread(sum_k, "y")
    sum_vq = spread(jnp.stack([sum_v, sum_q], axis=1), "x")
    ig_r = swap(ig_p)
    a_r = swap(a_p)
    input_grad = input_part(core, 0, (dq, dk, dv), weights, ig_r)
    input_grad, sum_k, sum_vq = together(input_grad, sum_k, sum_vq)
    sum_kv = spread(jnp.concatenate([sum_k, sum_vq[0]], axis=-1), "z")
    sum_q = spread(sum_vq[1], "y")
    attn_out = jnp.where(
        late, jnp.concatenate([a_r, a_o], axis=1), jnp.concatenate([a_o, a_r], axis=1)
    )
    summed = jnp.concatenate([sum_q, sum_kv], axis=1)
    own = jnp.where(late, summed[16:], summed[:16])
    other = swap(jnp.where(late, summed[:16], summed[16:]))
    scale = 65536.0**-0.5
    left = jnp.where(late, other, own).astype(F32) * scale
    right = jnp.where(late, own, other).astype(F32) * scale

    def joined(k):
        cols = slice(k * 512, k * 512 + 512)
        return jnp.concatenate([left[:, cols], right[:, cols]], axis=1)

    return (attn_out[None], input_grad[None], joined(0), joined(1), joined(2))


def solution(mesh):
    finer = Mesh(mesh.devices.reshape(4, 4, 2, mesh.shape["dp"]), ("y", "x", "c", "z"))
    return jax.shard_map(
        per_device,
        mesh=finer,
        in_specs=(P("z", CTX, None), P(), P(), P(), P("z", CTX, None)),
        out_specs=(
            P("z", CTX, None),
            P("z", CTX, None),
            P(CTX_DP, None),
            P(CTX_DP, None),
            P(CTX_DP, None),
        ),
        check_vma=False,
    )
```

```python
import jax
import jax.numpy as jnp
from jax import lax
from jax.experimental import pallas as pl
from jax.experimental.pallas import tpu as pltpu
from jax.sharding import Mesh
from jax.sharding import PartitionSpec as P

DH = 128
TOK = 512
EPS = 1e-05
CTX = ("y", "x", "c")
CTX_DP = ("y", "x", "c", "z")
BF = jnp.bfloat16
F32 = jnp.float32
MB = 1 << 20


def dot(a, b, ca=1, cb=0):
    return lax.dot_general(a, b, (((ca,), (cb,)), ((), ())), preferred_element_type=F32)


def causal(x, turned=False):
    rows = lax.broadcasted_iota(jnp.int32, x.shape, 0)
    cols = lax.broadcasted_iota(jnp.int32, x.shape, 1)
    keep = rows <= cols if turned else rows >= cols
    return jnp.where(keep, x, 0.0).astype(BF)


def head(h):
    return slice(h * DH, (h + 1) * DH)


def call(kernel, core, grid, ins, outs, flops, moved, limit=30):
    return pl.pallas_call(
        kernel,
        out_shape=[jax.ShapeDtypeStruct(s, d) for s, d, _, _ in outs],
        grid_spec=pltpu.PrefetchScalarGridSpec(
            num_scalar_prefetch=1,
            grid=(grid,),
            in_specs=[pl.BlockSpec(b, m) for _, b, m in ins],
            out_specs=[pl.BlockSpec(b, m) for _, _, b, m in outs],
        ),
        compiler_params=pltpu.CompilerParams(
            dimension_semantics=("arbitrary",), vmem_limit_bytes=limit * MB
        ),
        cost_estimate=pl.CostEstimate(flops=flops, bytes_accessed=moved, transcendentals=0),
    )(core, *[a for a, _, _ in ins])


def local(kernel, core, ins, outs, flops, moved):
    vmem = pl.BlockSpec(memory_space=pltpu.VMEM)
    return pl.pallas_call(
        kernel,
        out_shape=[jax.ShapeDtypeStruct(s, d) for s, d in outs],
        in_specs=[pl.BlockSpec(memory_space=pltpu.SMEM)] + [vmem] * len(ins),
        out_specs=[vmem] * len(outs),
        compiler_params=pltpu.CompilerParams(vmem_limit_bytes=30 * MB),
        cost_estimate=pl.CostEstimate(flops=flops, bytes_accessed=moved, transcendentals=0),
    )(core, *ins)


def whole(j, c):
    return (0, 0)


def tall(j, c):
    return (j, 0)


def wide(j, c):
    return (0, j)


def mine(j, c):
    return (0, c[0] * 2 + j)


def project_qkv(core, tok, wq, wk, wv):
    def kernel(c, t, a, b, d, q, k, v, s):
        x = t[...]
        q[...] = dot(x, a[...]).astype(BF)
        kk = dot(x, b[...]).astype(BF)
        vv = dot(x, d[...]).astype(BF)
        k[...] = kk
        v[...] = vv
        for h in range(2):
            s[head(h), :] = dot(kk[:, head(h)], vv[:, head(h)], 0, 0).astype(BF)

    w = (2048, 256)
    return call(
        kernel,
        core,
        2,
        [(tok, (TOK, 2048), whole), (wq, w, mine), (wk, w, mine), (wv, w, mine)],
        [((TOK, 512), BF, (TOK, 256), wide)] * 3 + [((512, DH), BF, (256, DH), tall)],
        3300000000,
        10 * MB,
        56,
    )


def project_kv(core, tok, wk, wv, state):
    def kernel(c, t, b, d, so, k, v, s, total):
        x = t[...]
        kk = dot(x, b[...]).astype(BF)
        vv = dot(x, d[...]).astype(BF)
        k[...] = kk
        v[...] = vv
        for h in range(2):
            st = dot(kk[:, head(h)], vv[:, head(h)], 0, 0).astype(BF)
            s[head(h), :] = st
            total[head(h), :] = (st.astype(F32) + so[head(h), :].astype(F32)).astype(BF)

    w = (2048, 256)
    return call(
        kernel,
        core,
        2,
        [(tok, (TOK, 2048), whole), (wk, w, mine), (wv, w, mine), (state, (256, DH), tall)],
        [((TOK, 512), BF, (TOK, 256), wide)] * 2 + [((512, DH), BF, (256, DH), tall)] * 2,
        2200000000,
        7 * MB,
        54,
    )


LOW = slice(0, 256)
HIGH = slice(256, 512)


def forward_pairs(q, k, v):
    s00 = causal(dot(q[LOW], k[LOW], 1, 1))
    s10 = dot(q[HIGH], k[LOW], 1, 1).astype(BF)
    s11 = causal(dot(q[HIGH], k[HIGH], 1, 1))
    return dot(s00, v[LOW]), dot(s10, v[LOW]) + dot(s11, v[HIGH])


def backward_pairs(q, k, x):
    s00 = causal(dot(k[LOW], q[LOW], 1, 1), True)
    s01 = dot(k[LOW], q[HIGH], 1, 1).astype(BF)
    s11 = causal(dot(k[HIGH], q[HIGH], 1, 1), True)
    return dot(s00, x[LOW]) + dot(s01, x[HIGH]), dot(s11, x[HIGH])


def masked_sum(refs, at, reverse):
    total = None
    for r, d in zip(refs, (1, 3, 2)):
        passed = at + (4 - d) < 4 if reverse else at >= d
        piece = r[...].astype(F32) * jnp.where(passed, 1.0, 0.0)
        total = piece if total is None else total + piece
    return total


def within(core, tok_p, wq, q_o, k_o, v_o, k_p, v_p):
    def kernel(c, tp, a, qo, ko, vo, kp, vp, qp, out):
        qq = dot(tp[...], a[...]).astype(BF)
        qp[...] = qq
        for n, (q, k, v) in enumerate(((qo[...], ko, vo), (qq, kp, vp))):
            for h in range(2):
                low, high = forward_pairs(q[:, head(h)], k[:, head(h)], v[:, head(h)])
                out[n * TOK : n * TOK + 256, head(h)] = low
                out[n * TOK + 256 : n * TOK + 512, head(h)] = high

    b = (TOK, 256)
    return call(
        kernel,
        core,
        2,
        [(tok_p, (TOK, 2048), whole), (wq, (2048, 256), mine)]
        + [(t, b, wide) for t in (q_o, k_o, v_o, k_p, v_p)],
        [((TOK, 512), BF, b, wide), ((2 * TOK, 512), F32, (2 * TOK, 256), wide)],
        2200000000,
        10 * MB,
    )


def turned(core, tok_o, tok_p):
    def kernel(c, to, tp, out):
        out[:, :TOK] = to[...].T
        out[:, TOK:] = tp[...].T

    return call(
        kernel,
        core,
        4,
        [(tok_o, (TOK, 512), wide), (tok_p, (TOK, 512), wide)],
        [((2048, 2 * TOK), BF, (512, 2 * TOK), tall)],
        1000000,
        8 * MB,
    )[0]


def normed(core, intra, q_o, q_p, state_o, state_p, along_x, along_y, cot, cot_p):
    def kernel(c, it, qo, qp, so, sp, x1, x3, x2, y1, y3, y2, co, cp, *outs):
        ao, ap, g, po, pp, bo, bp, total = outs
        before = masked_sum((x1, x3, x2), c[2], False) + masked_sum((y1, y3, y2), c[1], False)
        late = c[0].astype(F32)
        po[...] = (before + sp[...].astype(F32) * late).astype(BF)
        pp[...] = (before + so[...].astype(F32) * (1.0 - late)).astype(BF)
        for h in range(4):
            backs = []
            for n, (q, p, a, b) in enumerate(((qo, po, ao, bo), (qp, pp, ap, bp))):
                rows = slice(n * TOK, n * TOK + TOK)
                qh = q[:, head(h)]
                mixed = it[rows, head(h)] + dot(qh, p[head(h), :])
                inverse = lax.rsqrt(jnp.mean(mixed * mixed, axis=-1, keepdims=True) + EPS)
                nm = mixed * inverse
                if n == 0:
                    up = co[:, pl.ds(pl.multiple_of(c[0] * 512 + h * DH, DH), DH)]
                else:
                    up = cp[:, head(h)]
                up = up.astype(F32)
                a[:, head(h)] = nm.astype(BF)
                gm = ((up - nm * jnp.mean(up * nm, axis=-1, keepdims=True)) * inverse).astype(BF)
                g[rows, head(h)] = gm
                back = dot(qh, gm, 0, 0).astype(BF)
                b[head(h), :] = back
                backs.append(back.astype(F32))
            total[head(h), :] = (backs[0] + backs[1]).astype(BF)

    state = ((512, DH), BF)
    return local(
        kernel,
        core,
        [intra, q_o, q_p, state_o, state_p, *along_x, *along_y, cot, cot_p],
        [((TOK, 512), BF)] * 2 + [((2 * TOK, 512), BF)] + [state] * 5,
        300000000,
        7 * MB,
    )


def grad_q_of(core, k_o, k_p, v_o, v_p, g, p_o, p_p):
    def kernel(c, ko, kp, vo, vp, gr, po, pp, dq):
        for n, (k, v, p) in enumerate(((ko, vo, po), (kp, vp, pp))):
            for h in range(4):
                gh = gr[n * TOK : n * TOK + TOK, head(h)]
                past = dot(gh, p[head(h), :], 1, 1)
                low, high = forward_pairs(gh, v[:, head(h)], k[:, head(h)])
                dq[n * TOK : n * TOK + 256, head(h)] = (low + past[LOW]).astype(BF)
                dq[n * TOK + 256 : n * TOK + 512, head(h)] = (high + past[HIGH]).astype(BF)

    return local(
        kernel,
        core,
        [k_o, k_p, v_o, v_p, g, p_o, p_p],
        [((2 * TOK, 512), BF)],
        1200000000,
        4 * MB,
    )[0]


def grads_within(core, q_o, q_p, k_o, k_p, v_o, v_p, g):
    def kernel(c, qo, qp, ko, kp, vo, vp, gr, dk, dv):
        for n, (q, k, v) in enumerate(((qo, ko, vo), (qp, kp, vp))):
            for h in range(4):
                qh, kh, vh = q[:, head(h)], k[:, head(h)], v[:, head(h)]
                gh = gr[n * TOK : n * TOK + TOK, head(h)]
                for left, right, x, out in ((gh, vh, qh, dk), (qh, kh, gh, dv)):
                    low, high = backward_pairs(left, right, x)
                    out[n * TOK : n * TOK + 256, head(h)] = low
                    out[n * TOK + 256 : n * TOK + 512, head(h)] = high

    return local(
        kernel,
        core,
        [q_o, q_p, k_o, k_p, v_o, v_p, g],
        [((2 * TOK, 512), F32)] * 2,
        2000000000,
        9 * MB,
    )


def grads_after(core, k_o, k_p, v_o, v_p, dk, dv, back_o, back_p, along_x, along_y):
    def kernel(c, ko, kp, vo, vp, ak, av, bo, bp, x1, x3, x2, y1, y3, y2, ok, ov):
        after = masked_sum((x1, x3, x2), c[2], True) + masked_sum((y1, y3, y2), c[1], True)
        late = c[0].astype(F32)
        s_o = (after + bp[...].astype(F32) * (1.0 - late)).astype(BF)
        s_p = (after + bo[...].astype(F32) * late).astype(BF)
        for n, (k, v, s) in enumerate(((ko, vo, s_o), (kp, vp, s_p))):
            rows = slice(n * TOK, n * TOK + TOK)
            for h in range(4):
                sh = s[head(h), :]
                ok[rows, head(h)] = (ak[rows, head(h)] + dot(v[:, head(h)], sh, 1, 1)).astype(BF)
                ov[rows, head(h)] = (av[rows, head(h)] + dot(k[:, head(h)], sh)).astype(BF)

    return local(
        kernel,
        core,
        [k_o, k_p, v_o, v_p, dk, dv, back_o, back_p, *along_x, *along_y],
        [((2 * TOK, 512), BF)] * 2,
        200000000,
        8 * MB,
    )


def weight_grad(core, tt, jobs):
    n = len(jobs)

    def kernel(c, t, *refs):
        for m, (_, axis, step) in enumerate(jobs):
            g, out = refs[m], refs[n + m]
            if axis == "x":
                rows = t[:, (c[2] + step) % 4]
            elif axis == "y":
                rows = t[(c[1] + step) % 4]
            part = dot(rows.reshape(512, 2 * TOK), g[...]).astype(BF)
            for a in range(4):
                at = (a - c[1] + 4) % 4 if axis == "x" else (a - c[2] + 4) % 4
                for core_at in range(2):
                    for z in range(4):
                        row = a * 128 + core_at * 64 + z * 16
                        out[at, (z - c[3] + 4) % 4, core_at * 16 : core_at * 16 + 16, :] = part[
                            row : row + 16, :
                        ]

    return local(
        kernel,
        core,
        [tt.reshape(4, 4, 128, 2 * TOK)] + [g for g, _, _ in jobs],
        [((4, 4, 32, 512), BF)] * n,
        550000000 * n,
        (1 + 2 * n) * MB,
    )


def weight_grad_z(core, tt, grad):
    def kernel(c, t, g, out):
        gr = g[...]
        for y in range(4):
            part = dot(t[y].reshape(512, 2 * TOK), gr).astype(BF)
            dy = (y - c[1] + 4) % 4
            for x in range(4):
                dx = (x - c[2] + 4) % 4
                for core_at in range(2):
                    for z in range(4):
                        row = x * 128 + core_at * 64 + z * 16
                        here = slice(core_at * 16, core_at * 16 + 16)
                        out[(z - c[3] + 4) % 4, dx, dy, here, :] = part[row : row + 16, :]

    return local(
        kernel,
        core,
        [tt.reshape(4, 4, 128, 2 * TOK), grad],
        [((4, 4, 4, 32, 512), BF)],
        2200000000,
        8 * MB,
    )[0]


def assembled(core, sum_q, sum_kv, came):
    def kernel(c, q, kv, r, *outs):
        scale = 65536.0**-0.5
        mine = pl.ds(pl.multiple_of(c[0] * 16, 16), 16)
        here = pl.ds(pl.multiple_of(c[0] * 512, 512), 512)
        there = pl.ds(pl.multiple_of((1 - c[0]) * 512, 512), 512)
        for m, out in enumerate(outs):
            own = q[mine, :] if m == 0 else kv[mine, m * 512 - 512 : m * 512]
            out[:, here] = own.astype(F32) * scale
            out[:, there] = r[:, m * 512 : m * 512 + 512].astype(F32) * scale

    return local(kernel, core, [sum_q, sum_kv, came], [((16, 1024), F32)] * 3, 1000, MB)


def input_part(core, slot, grads, weights, received=None):
    def kernel(c, *refs):
        out = refs[-1]
        total = dot(refs[0][...], refs[3][...], 1, 1)
        total = total + dot(refs[1][...], refs[4][...], 1, 1)
        total = total + dot(refs[2][...], refs[5][...], 1, 1)
        if received is not None:
            total = total + refs[6][...].astype(F32)
        out[...] = total.astype(BF)

    ins = [(g, (TOK, 512), lambda j, c: (slot, 0)) for g in grads]
    ins += [(w, (512, 512), lambda j, c: (j, c[0])) for w in weights]
    if received is not None:
        ins.append((received, (TOK, 512), wide))
    return call(
        kernel, core, 4, ins, [((TOK, 2048), BF, (TOK, 512), wide)], 3300000000, 10 * MB
    )[0]


def shift(v, axis, d):
    n = lax.axis_size(axis)
    return lax.ppermute(v, axis, [(i, (i + d) % n) for i in range(n)])


def swap(v):
    return lax.ppermute(v, "c", [(0, 1), (1, 0)])


def pieces(v, axis):
    return [shift(v, axis, d) for d in (1, 3, 2)]


def together(*values):
    return lax.optimization_barrier(values)


def f32_sum(*parts):
    total = parts[0].astype(F32)
    for p in parts[1:]:
        total = total + p.astype(F32)
    return total.astype(BF)


def ring_out(far, axis):
    return shift(far[:2], axis, 1), shift(far[2:], axis, 3)


def ring_near(up, down, came, axis):
    from_left, from_right = came
    up = jnp.concatenate([f32_sum(up[:2], from_left), up[2:]], axis=0)
    down = jnp.concatenate([down[:2], f32_sum(down[2:], from_right)], axis=0)
    return shift(up, axis, 1), shift(down, axis, 3)


def spread(blocks, axis):
    return f32_sum(blocks[0], *[shift(blocks[d], axis, d) for d in (2, 1, 3)])


def per_device(tokens, w_query, w_key, w_value, cotangent):
    c = lax.axis_index("c")
    core = jnp.stack([lax.axis_index(a) for a in ("c", "y", "x", "z")]).astype(jnp.int32)
    tok_o = tokens[0]
    cot = cotangent[0]
    tok_p = swap(tok_o)
    late = c == 1
    cot_p = swap(jnp.where(late, cot[:, :512], cot[:, 512:]))

    q_o, k_o, v_o, state_o = project_qkv(core, tok_o, w_query, w_key, w_value)
    k_p, v_p, state_p, total = project_kv(core, tok_p, w_key, w_value, state_o)
    along_x = pieces(total, "x")
    q_p, intra = within(core, tok_p, w_query, q_o, k_o, v_o, k_p, v_p)
    row, intra, q_p, tok_t = together(f32_sum(total, *along_x), intra, q_p, tok_o)
    along_y = pieces(row, "y")
    tt = turned(core, tok_t, tok_p)
    *along_y, tt = together(*along_y, tt)
    a_o, a_p, g, p_o, p_p, back_o, back_p, total = normed(
        core, intra, q_o, q_p, state_o, state_p, along_x, along_y, cot, cot_p
    )
    along_x = pieces(total, "x")
    dq = grad_q_of(core, k_o, k_p, v_o, v_p, g, p_o, p_p)
    part_q = weight_grad_z(core, tt, dq)
    row, part_q, g, a_p = together(f32_sum(total, *along_x), part_q, g, a_p)
    along_y = pieces(row, "y")
    came_q = ring_out(part_q[2], "z")
    dk, dv = grads_within(core, q_o, q_p, k_o, k_p, v_o, v_p, g)
    *along_y, dk, dv = together(*along_y, dk, dv)
    dk, dv = grads_after(
        core, k_o, k_p, v_o, v_p, dk, dv, back_o, back_p, along_x, along_y
    )
    far_k, far_v = weight_grad(core, tt, [(dk, "x", 2), (dv, "y", 2)])
    far_k, far_v, dk, dv, *came_q = together(far_k, far_v, dk, dv, *came_q)
    came = [*ring_out(far_k, "x"), *ring_out(far_v, "y")]
    last_q = ring_near(part_q[1], part_q[3], came_q, "z")
    near = weight_grad(core, tt, [(dk, "x", 1), (dk, "x", 3), (dv, "y", 1), (dv, "y", 3)])
    *near, dk, dv, a_p, c0, c1, c2, c3 = together(*near, dk, dv, a_p, *came)
    last = [*ring_near(near[0], near[1], (c0, c1), "x")]
    last += [*ring_near(near[2], near[3], (c2, c3), "y")]
    here_k, here_v = weight_grad(core, tt, [(dk, "x", 0), (dv, "y", 0)])
    weights = (w_query, w_key, w_value)
    ig_p = input_part(core, 1, (dq, dk, dv), weights)
    ig_r = swap(ig_p)
    a_r = swap(a_p)
    attn_out = jnp.where(
        late, jnp.concatenate([a_r, a_o], axis=1), jnp.concatenate([a_o, a_r], axis=1)
    )
    ig_r, here_k, here_v, attn_out, *last = together(
        ig_r, here_k, here_v, attn_out, *last, *last_q
    )
    sum_k = f32_sum(here_k, *last[:2])
    sum_v = f32_sum(here_v, *last[2:4])
    sum_q = f32_sum(part_q[0], *last[4:])
    sum_k = spread(sum_k, "y")
    sum_vq = spread(jnp.stack([sum_v, sum_q], axis=1), "x")
    input_grad = input_part(core, 0, (dq, dk, dv), weights, ig_r)
    input_grad, sum_k, sum_vq = together(input_grad, sum_k, sum_vq)
    sum_kv = spread(jnp.concatenate([sum_k, sum_vq[0]], axis=-1), "z")
    sum_q = spread(sum_vq[1], "y")
    summed = jnp.concatenate([sum_q, sum_kv], axis=1)
    came = swap(jnp.where(late, summed[:16], summed[16:]))
    return (attn_out[None], input_grad[None], *assembled(core, sum_q, sum_kv, came))


def solution(mesh):
    finer = Mesh(mesh.devices.reshape(4, 4, 2, mesh.shape["dp"]), ("y", "x", "c", "z"))
    return jax.shard_map(
        per_device,
        mesh=finer,
        in_specs=(P("z", CTX, None), P(), P(), P(), P("z", CTX, None)),
        out_specs=(
            P("z", CTX, None),
            P("z", CTX, None),
            P(CTX_DP, None),
            P(CTX_DP, None),
            P(CTX_DP, None),
        ),
        check_vma=False,
    )
```

```python
import jax
import jax.numpy as jnp
from jax import lax
from jax.experimental import pallas as pl
from jax.experimental.pallas import tpu as pltpu
from jax.sharding import Mesh
from jax.sharding import PartitionSpec as P

DH = 128
TOK = 512
EPS = 1e-05
CTX = ("y", "x", "c")
CTX_DP = ("y", "x", "c", "z")
BF = jnp.bfloat16
F32 = jnp.float32
MB = 1 << 20


def dot(a, b, ca=1, cb=0):
    return lax.dot_general(a, b, (((ca,), (cb,)), ((), ())), preferred_element_type=F32)


def causal(x, turned=False):
    rows = lax.broadcasted_iota(jnp.int32, x.shape, 0)
    cols = lax.broadcasted_iota(jnp.int32, x.shape, 1)
    keep = rows <= cols if turned else rows >= cols
    return jnp.where(keep, x, 0.0).astype(BF)


def head(h):
    return slice(h * DH, (h + 1) * DH)


def call(kernel, core, grid, ins, outs, flops, moved, limit=20):
    return pl.pallas_call(
        kernel,
        out_shape=[jax.ShapeDtypeStruct(s, d) for s, d, _, _ in outs],
        grid_spec=pltpu.PrefetchScalarGridSpec(
            num_scalar_prefetch=1,
            grid=(grid,),
            in_specs=[pl.BlockSpec(b, m) for _, b, m in ins],
            out_specs=[pl.BlockSpec(b, m) for _, _, b, m in outs],
        ),
        compiler_params=pltpu.CompilerParams(
            dimension_semantics=("arbitrary",), vmem_limit_bytes=limit * MB
        ),
        cost_estimate=pl.CostEstimate(flops=flops, bytes_accessed=moved, transcendentals=0),
    )(core, *[a for a, _, _ in ins])


def local(kernel, core, ins, outs, hbm_in=0, hbm_out=0, scratch=()):
    vmem, hbm = pl.BlockSpec(memory_space=pltpu.VMEM), pl.BlockSpec(memory_space=pltpu.HBM)
    return pl.pallas_call(
        kernel,
        out_shape=[jax.ShapeDtypeStruct(s, d) for s, d in outs],
        in_specs=[pl.BlockSpec(memory_space=pltpu.SMEM)]
        + [vmem] * (len(ins) - hbm_in)
        + [hbm] * hbm_in,
        out_specs=[vmem] * (len(outs) - hbm_out) + [hbm] * hbm_out,
        scratch_shapes=list(scratch),
        compiler_params=pltpu.CompilerParams(vmem_limit_bytes=20 * MB),
        cost_estimate=pl.CostEstimate(flops=1000000, bytes_accessed=1000, transcendentals=0),
    )(core, *ins)


def whole(j, c):
    return (0, 0)


def tall(j, c):
    return (j, 0)


def wide(j, c):
    return (0, j)


def mine(j, c):
    return (0, c[0] * 2 + j)


def project_qkv(core, tok, wq, wk, wv):
    tok, wq, wk, wv = (pltpu.with_memory_space_constraint(t, pltpu.HBM) for t in (tok, wq, wk, wv))

    def kernel(c, t, a, b, d, q, k, v, s, ah, bh, dh, tv, aq, ak, av, sems):
        half = pl.ds(pl.multiple_of(c[0] * 512, 512), 512)
        copies = []
        for i in range(4):
            at = pl.ds(i * 512, 512)
            row = [pltpu.make_async_copy(t.at[:, at], tv.at[:, at], sems.at[i, 0])]
            for n, (src, dst) in enumerate(((b, bh), (d, dh), (a, ah))):
                row.append(pltpu.make_async_copy(src.at[at, half], dst.at[at, :], sems.at[i, n + 1]))
            for copy in row:
                copy.start()
            copies.append(row)
        for i in range(4):
            at = slice(i * 512, i * 512 + 512)
            copies[i][0].wait()
            for n, (w, acc, out) in enumerate(((bh, ak, k), (dh, av, v), (ah, aq, q))):
                copies[i][n + 1].wait()
                part = dot(tv[:, at], w[at, :])
                if i == 0:
                    acc[...] = part
                elif i < 3:
                    acc[...] += part
                else:
                    out[...] = (acc[...] + part).astype(BF)
        for h in range(4):
            s[head(h), :] = dot(k[:, head(h)], v[:, head(h)], 0, 0).astype(BF)

    row, weight = ((TOK, 512), BF), ((2048, 512), BF)
    return local(
        kernel,
        core,
        [tok, wq, wk, wv],
        [row] * 3 + [((512, DH), BF)] + [weight] * 3,
        hbm_in=4,
        scratch=[pltpu.VMEM((TOK, 2048), BF)]
        + [pltpu.VMEM((TOK, 512), F32)] * 3
        + [pltpu.SemaphoreType.DMA((4, 4))],
    )


def project_kv(core, tok, wk, wv, state):
    def kernel(c, t, b, d, so, k, v, s, total):
        k[...] = dot(t[...], b[...]).astype(BF)
        v[...] = dot(t[...], d[...]).astype(BF)
        for h in range(4):
            st = dot(k[:, head(h)], v[:, head(h)], 0, 0).astype(BF)
            s[head(h), :] = st
            total[head(h), :] = (st.astype(F32) + so[head(h), :].astype(F32)).astype(BF)

    return local(
        kernel,
        core,
        [tok, wk, wv, state],
        [((TOK, 512), BF)] * 2 + [((512, DH), BF)] * 2,
    )


LOW = slice(0, 256)
HIGH = slice(256, 512)


def forward_pairs(q, k, v):
    s00 = causal(dot(q[LOW], k[LOW], 1, 1))
    s10 = dot(q[HIGH], k[LOW], 1, 1).astype(BF)
    s11 = causal(dot(q[HIGH], k[HIGH], 1, 1))
    return dot(s00, v[LOW]), dot(s10, v[LOW]) + dot(s11, v[HIGH])


def backward_pairs(q, k, x):
    s00 = causal(dot(k[LOW], q[LOW], 1, 1), True)
    s01 = dot(k[LOW], q[HIGH], 1, 1).astype(BF)
    s11 = causal(dot(k[HIGH], q[HIGH], 1, 1), True)
    return dot(s00, x[LOW]) + dot(s01, x[HIGH]), dot(s11, x[HIGH])


def masked_sum(refs, at, reverse):
    total = None
    for r, d in zip(refs, (1, 3, 2)):
        passed = at + (4 - d) < 4 if reverse else at >= d
        piece = r[...].astype(F32) * jnp.where(passed, 1.0, 0.0)
        total = piece if total is None else total + piece
    return total


def within(core, tok_p, wq, q_o, k_o, v_o, k_p, v_p):
    def kernel(c, tp, a, qo, ko, vo, kp, vp, qp, out):
        qp[...] = dot(tp[...], a[...]).astype(BF)
        for n, (q, k, v) in enumerate(((qo, ko, vo), (qp, kp, vp))):
            for h in range(4):
                low, high = forward_pairs(q[:, head(h)], k[:, head(h)], v[:, head(h)])
                out[n * TOK : n * TOK + 256, head(h)] = low
                out[n * TOK + 256 : n * TOK + 512, head(h)] = high

    return local(
        kernel,
        core,
        [tok_p, wq, q_o, k_o, v_o, k_p, v_p],
        [((TOK, 512), BF), ((2 * TOK, 512), F32)],
    )


def turned(core, tok_o, tok_p):
    def kernel(c, to, tp, out):
        out[:, :TOK] = to[...].T
        out[:, TOK:] = tp[...].T

    return call(
        kernel,
        core,
        4,
        [(tok_o, (TOK, 512), wide), (tok_p, (TOK, 512), wide)],
        [((2048, 2 * TOK), BF, (512, 2 * TOK), tall)],
        1000000,
        8 * MB,
    )[0]


def normed(core, intra, q_o, q_p, state_o, state_p, along_x, along_y, cot, cot_p):
    def kernel(c, it, qo, qp, so, sp, x1, x3, x2, y1, y3, y2, co, cp, *outs):
        ao, ap, g, po, pp, bo, bp, total = outs
        before = masked_sum((x1, x3, x2), c[2], False) + masked_sum((y1, y3, y2), c[1], False)
        late = c[0].astype(F32)
        po[...] = (before + sp[...].astype(F32) * late).astype(BF)
        pp[...] = (before + so[...].astype(F32) * (1.0 - late)).astype(BF)
        for h in range(4):
            backs = []
            for n, (q, p, a, b) in enumerate(((qo, po, ao, bo), (qp, pp, ap, bp))):
                rows = slice(n * TOK, n * TOK + TOK)
                qh = q[:, head(h)]
                mixed = it[rows, head(h)] + dot(qh, p[head(h), :])
                inverse = lax.rsqrt(jnp.mean(mixed * mixed, axis=-1, keepdims=True) + EPS)
                nm = mixed * inverse
                if n == 0:
                    up = co[:, pl.ds(pl.multiple_of(c[0] * 512 + h * DH, DH), DH)]
                else:
                    up = cp[:, head(h)]
                up = up.astype(F32)
                a[:, head(h)] = nm.astype(BF)
                gm = ((up - nm * jnp.mean(up * nm, axis=-1, keepdims=True)) * inverse).astype(BF)
                g[rows, head(h)] = gm
                back = dot(qh, gm, 0, 0).astype(BF)
                b[head(h), :] = back
                backs.append(back.astype(F32))
            total[head(h), :] = (backs[0] + backs[1]).astype(BF)

    state = ((512, DH), BF)
    return local(
        kernel,
        core,
        [intra, q_o, q_p, state_o, state_p, *along_x, *along_y, cot, cot_p],
        [((TOK, 512), BF)] * 2 + [((2 * TOK, 512), BF)] + [state] * 5,
    )


def grad_q_of(core, k_o, k_p, v_o, v_p, g, p_o, p_p):
    def kernel(c, ko, kp, vo, vp, gr, po, pp, dq):
        for n, (k, v, p) in enumerate(((ko, vo, po), (kp, vp, pp))):
            for h in range(4):
                gh = gr[n * TOK : n * TOK + TOK, head(h)]
                past = dot(gh, p[head(h), :], 1, 1)
                low, high = forward_pairs(gh, v[:, head(h)], k[:, head(h)])
                dq[n * TOK : n * TOK + 256, head(h)] = (low + past[LOW]).astype(BF)
                dq[n * TOK + 256 : n * TOK + 512, head(h)] = (high + past[HIGH]).astype(BF)

    return local(
        kernel,
        core,
        [k_o, k_p, v_o, v_p, g, p_o, p_p],
        [((2 * TOK, 512), BF)],
    )[0]


def grads_within(core, q_o, q_p, k_o, k_p, v_o, v_p, g):
    def kernel(c, qo, qp, ko, kp, vo, vp, gr, dk, dv):
        for n, (q, k, v) in enumerate(((qo, ko, vo), (qp, kp, vp))):
            for h in range(4):
                qh, kh, vh = q[:, head(h)], k[:, head(h)], v[:, head(h)]
                gh = gr[n * TOK : n * TOK + TOK, head(h)]
                for left, right, x, out in ((gh, vh, qh, dk), (qh, kh, gh, dv)):
                    low, high = backward_pairs(left, right, x)
                    out[n * TOK : n * TOK + 256, head(h)] = low
                    out[n * TOK + 256 : n * TOK + 512, head(h)] = high

    return local(
        kernel,
        core,
        [q_o, q_p, k_o, k_p, v_o, v_p, g],
        [((2 * TOK, 512), F32)] * 2,
    )


def grads_after(core, k_o, k_p, v_o, v_p, dk, dv, back_o, back_p, along_x, along_y):
    def kernel(c, ko, kp, vo, vp, ak, av, bo, bp, x1, x3, x2, y1, y3, y2, ok, ov):
        after = masked_sum((x1, x3, x2), c[2], True) + masked_sum((y1, y3, y2), c[1], True)
        late = c[0].astype(F32)
        s_o = (after + bp[...].astype(F32) * (1.0 - late)).astype(BF)
        s_p = (after + bo[...].astype(F32) * late).astype(BF)
        for n, (k, v, s) in enumerate(((ko, vo, s_o), (kp, vp, s_p))):
            rows = slice(n * TOK, n * TOK + TOK)
            for h in range(4):
                sh = s[head(h), :]
                ok[rows, head(h)] = (ak[rows, head(h)] + dot(v[:, head(h)], sh, 1, 1)).astype(BF)
                ov[rows, head(h)] = (av[rows, head(h)] + dot(k[:, head(h)], sh)).astype(BF)

    return local(
        kernel,
        core,
        [k_o, k_p, v_o, v_p, dk, dv, back_o, back_p, *along_x, *along_y],
        [((2 * TOK, 512), BF)] * 2,
    )


def weight_grad(core, tt, jobs):
    n = len(jobs)

    def kernel(c, t, *refs):
        for m, (_, axis, step) in enumerate(jobs):
            g, out = refs[m], refs[n + m]
            if axis == "x":
                rows = t[:, (c[2] + step) % 4]
            elif axis == "y":
                rows = t[(c[1] + step) % 4]
            part = dot(rows.reshape(512, 2 * TOK), g[...]).astype(BF)
            for a in range(4):
                at = (a - c[1] + 4) % 4 if axis == "x" else (a - c[2] + 4) % 4
                for core_at in range(2):
                    for z in range(4):
                        row = a * 128 + core_at * 64 + z * 16
                        out[at, (z - c[3] + 4) % 4, core_at * 16 : core_at * 16 + 16, :] = part[
                            row : row + 16, :
                        ]

    return local(
        kernel,
        core,
        [tt.reshape(4, 4, 128, 2 * TOK)] + [g for g, _, _ in jobs],
        [((4, 4, 32, 512), BF)] * n,
    )


def weight_grad_z(core, tt, grad):
    def kernel(c, t, g, out):
        gr = g[...]
        for y in range(4):
            part = dot(t[y].reshape(512, 2 * TOK), gr).astype(BF)
            dy = (y - c[1] + 4) % 4
            for x in range(4):
                dx = (x - c[2] + 4) % 4
                for core_at in range(2):
                    for z in range(4):
                        row = x * 128 + core_at * 64 + z * 16
                        here = slice(core_at * 16, core_at * 16 + 16)
                        out[(z - c[3] + 4) % 4, dx, dy, here, :] = part[row : row + 16, :]

    return local(
        kernel,
        core,
        [tt.reshape(4, 4, 128, 2 * TOK), grad],
        [((4, 4, 4, 32, 512), BF)],
    )[0]


def assembled(core, sum_q, sum_kv, came):
    def kernel(c, q, kv, r, *outs):
        scale = 65536.0**-0.5
        mine = pl.ds(pl.multiple_of(c[0] * 16, 16), 16)
        here = pl.ds(pl.multiple_of(c[0] * 512, 512), 512)
        there = pl.ds(pl.multiple_of((1 - c[0]) * 512, 512), 512)
        for m, out in enumerate(outs):
            own = q[mine, :] if m == 0 else kv[mine, m * 512 - 512 : m * 512]
            out[:, here] = own.astype(F32) * scale
            out[:, there] = r[:, m * 512 : m * 512 + 512].astype(F32) * scale

    return local(kernel, core, [sum_q, sum_kv, came], [((16, 1024), F32)] * 3)


def input_part(core, slot, grads, weights, received=None):
    final = received is not None

    def kernel(c, *refs):
        rows = slice(slot * TOK, slot * TOK + TOK)
        out = refs[7] if final else refs[6]
        copies = []
        for j in range(4):
            at = slice(j * 512, j * 512 + 512)
            total = dot(refs[0][rows, :], refs[3][at, :], 1, 1)
            total = total + dot(refs[1][rows, :], refs[4][at, :], 1, 1)
            total = total + dot(refs[2][rows, :], refs[5][at, :], 1, 1)
            if not final:
                out[:, at] = total.astype(BF)
                continue
            held, sems = refs[8:]
            held[:, at] = (total + refs[6][:, at].astype(F32)).astype(BF)
            cols = pl.ds(j * 512, 512)
            copies.append(pltpu.make_async_copy(held.at[:, cols], out.at[:, cols], sems.at[j]))
            copies[-1].start()
        for copy in copies:
            copy.wait()

    return local(
        kernel,
        core,
        [*grads, *weights] + ([received] if final else []),
        [((TOK, 2048), BF)],
        hbm_out=1 if final else 0,
        scratch=[pltpu.VMEM((TOK, 2048), BF), pltpu.SemaphoreType.DMA((4,))] if final else [],
    )[0]


def shift(v, axis, d):
    n = lax.axis_size(axis)
    return lax.ppermute(v, axis, [(i, (i + d) % n) for i in range(n)])


def swap(v):
    return lax.ppermute(v, "c", [(0, 1), (1, 0)])


def pieces(v, axis):
    return [shift(v, axis, d) for d in (1, 3, 2)]


def together(*values):
    return lax.optimization_barrier(values)


def f32_sum(*parts):
    total = parts[0].astype(F32)
    for p in parts[1:]:
        total = total + p.astype(F32)
    return total.astype(BF)


def ring_out(far, axis):
    return shift(far[:2], axis, 1), shift(far[2:], axis, 3)


def ring_near(up, down, came, axis):
    from_left, from_right = came
    up = jnp.concatenate([f32_sum(up[:2], from_left), up[2:]], axis=0)
    down = jnp.concatenate([down[:2], f32_sum(down[2:], from_right)], axis=0)
    return shift(up, axis, 1), shift(down, axis, 3)


def spread(blocks, axis):
    return f32_sum(blocks[0], *[shift(blocks[d], axis, d) for d in (2, 1, 3)])


def per_device(tokens, w_query, w_key, w_value, cotangent):
    c = lax.axis_index("c")
    core = jnp.stack([lax.axis_index(a) for a in ("c", "y", "x", "z")]).astype(jnp.int32)
    tok_o = tokens[0]
    cot = cotangent[0]
    tok_p = swap(tok_o)
    late = c == 1

    q_o, k_o, v_o, state_o, *weights = project_qkv(core, tok_o, w_query, w_key, w_value)
    k_p, v_p, state_p, total = project_kv(core, tok_p, weights[1], weights[2], state_o)
    along_x = pieces(total, "x")
    q_p, intra = within(core, tok_p, weights[0], q_o, k_o, v_o, k_p, v_p)
    row, intra, q_p, tok_t = together(f32_sum(total, *along_x), intra, q_p, tok_o)
    along_y = pieces(row, "y")
    tt = turned(core, tok_t, tok_p)
    cot_p = swap(jnp.where(late, cot[:, :512], cot[:, 512:]))
    *along_y, tt, cot_p = together(*along_y, tt, cot_p)
    a_o, a_p, g, p_o, p_p, back_o, back_p, total = normed(
        core, intra, q_o, q_p, state_o, state_p, along_x, along_y, cot, cot_p
    )
    along_x = pieces(total, "x")
    a_r = swap(a_p)
    dq = grad_q_of(core, k_o, k_p, v_o, v_p, g, p_o, p_p)
    part_q = weight_grad_z(core, tt, dq)
    row, part_q, g, a_r = together(f32_sum(total, *along_x), part_q, g, a_r)
    along_y = pieces(row, "y")
    came_q = ring_out(part_q[2], "z")
    dk, dv = grads_within(core, q_o, q_p, k_o, k_p, v_o, v_p, g)
    *along_y, dk, dv, c0, c1 = together(*along_y, dk, dv, *came_q)
    last_q = ring_near(part_q[1], part_q[3], (c0, c1), "z")
    dk, dv = grads_after(
        core, k_o, k_p, v_o, v_p, dk, dv, back_o, back_p, along_x, along_y
    )
    far_k, far_v = weight_grad(core, tt, [(dk, "x", 2), (dv, "y", 2)])
    far_k, far_v, dk, dv = together(far_k, far_v, dk, dv)
    came_k, came_v = shift(far_k, "x", 1), shift(far_v, "y", 1)
    near = weight_grad(core, tt, [(dk, "x", 1), (dk, "x", 3), (dv, "y", 1), (dv, "y", 3)])
    ig_r = swap(input_part(core, 1, (dq, dk, dv), weights))
    *near, dk, dv, ig_r, came_k, came_v, q0, q1 = together(
        *near, dk, dv, ig_r, came_k, came_v, *last_q
    )
    last = [shift(f32_sum(near[0], came_k), "x", 1), shift(near[1], "x", 3)]
    last += [shift(f32_sum(near[2], came_v), "y", 1), shift(near[3], "y", 3)]
    sum_q = f32_sum(part_q[0], q0, q1)
    here_k, here_v = weight_grad(core, tt, [(dk, "x", 0), (dv, "y", 0)])
    input_grad = input_part(core, 0, (dq, dk, dv), weights, ig_r)
    attn_out = jnp.where(
        late, jnp.concatenate([a_r, a_o], axis=1), jnp.concatenate([a_o, a_r], axis=1)
    )
    sum_q, here_k, here_v, input_grad, attn_out, *last = together(
        sum_q, here_k, here_v, input_grad, attn_out, *last
    )
    sum_k = f32_sum(here_k, *last[:2])
    sum_v = f32_sum(here_v, *last[2:])
    sum_vq = spread(jnp.stack([sum_v, sum_q], axis=1), "x")
    sum_k = spread(sum_k, "y")
    sum_kv = spread(jnp.concatenate([sum_k, sum_vq[0]], axis=-1), "z")
    sum_q = spread(sum_vq[1], "y")
    summed = jnp.concatenate([sum_q, sum_kv], axis=1)
    came = swap(jnp.where(late, summed[:16], summed[16:]))
    return (attn_out[None], input_grad[None], *assembled(core, sum_q, sum_kv, came))


def solution(mesh):
    finer = Mesh(mesh.devices.reshape(4, 4, 2, mesh.shape["dp"]), ("y", "x", "c", "z"))
    return jax.shard_map(
        per_device,
        mesh=finer,
        in_specs=(P("z", CTX, None), P(), P(), P(), P("z", CTX, None)),
        out_specs=(
            P("z", CTX, None),
            P("z", CTX, None),
            P(CTX_DP, None),
            P(CTX_DP, None),
            P(CTX_DP, None),
        ),
        check_vma=False,
    )
```

```python
import jax
import jax.numpy as jnp
from jax import lax
from jax.experimental import pallas as pl
from jax.experimental.pallas import tpu as pltpu
from jax.sharding import Mesh
from jax.sharding import PartitionSpec as P

DH = 128
TOK = 512
EPS = 1e-05
CTX = ("y", "x", "c")
CTX_DP = ("y", "x", "c", "z")
BF = jnp.bfloat16
F32 = jnp.float32
MB = 1 << 20


def dot(a, b, ca=1, cb=0):
    return lax.dot_general(a, b, (((ca,), (cb,)), ((), ())), preferred_element_type=F32)


def causal(x, turned=False):
    rows = lax.broadcasted_iota(jnp.int32, x.shape, 0)
    cols = lax.broadcasted_iota(jnp.int32, x.shape, 1)
    keep = rows <= cols if turned else rows >= cols
    return jnp.where(keep, x, 0.0).astype(BF)


def head(h):
    return slice(h * DH, (h + 1) * DH)


def call(kernel, core, grid, ins, outs, flops, moved, limit=20):
    return pl.pallas_call(
        kernel,
        out_shape=[jax.ShapeDtypeStruct(s, d) for s, d, _, _ in outs],
        grid_spec=pltpu.PrefetchScalarGridSpec(
            num_scalar_prefetch=1,
            grid=(grid,),
            in_specs=[pl.BlockSpec(b, m) for _, b, m in ins],
            out_specs=[pl.BlockSpec(b, m) for _, _, b, m in outs],
        ),
        compiler_params=pltpu.CompilerParams(
            dimension_semantics=("arbitrary",), vmem_limit_bytes=limit * MB
        ),
        cost_estimate=pl.CostEstimate(flops=flops, bytes_accessed=moved, transcendentals=0),
    )(core, *[a for a, _, _ in ins])


def local(kernel, core, ins, outs, hbm_in=0, hbm_out=0, scratch=()):
    vmem, hbm = pl.BlockSpec(memory_space=pltpu.VMEM), pl.BlockSpec(memory_space=pltpu.HBM)
    return pl.pallas_call(
        kernel,
        out_shape=[jax.ShapeDtypeStruct(s, d) for s, d in outs],
        in_specs=[pl.BlockSpec(memory_space=pltpu.SMEM)]
        + [vmem] * (len(ins) - hbm_in)
        + [hbm] * hbm_in,
        out_specs=[vmem] * (len(outs) - hbm_out) + [hbm] * hbm_out,
        scratch_shapes=list(scratch),
        compiler_params=pltpu.CompilerParams(vmem_limit_bytes=20 * MB),
        cost_estimate=pl.CostEstimate(flops=1000000, bytes_accessed=1000, transcendentals=0),
    )(core, *ins)


def whole(j, c):
    return (0, 0)


def tall(j, c):
    return (j, 0)


def wide(j, c):
    return (0, j)


def mine(j, c):
    return (0, c[0] * 2 + j)


def project_qkv(core, tok, wq, wk, wv):
    tok, wq, wk, wv = (pltpu.with_memory_space_constraint(t, pltpu.HBM) for t in (tok, wq, wk, wv))

    def kernel(c, t, a, b, d, q, k, v, s, ah, bh, dh, tv, sems):
        copies = [pltpu.make_async_copy(t, tv, sems.at[6])]
        copies[0].start()
        order = ((b, bh, k), (d, dh, v), (a, ah, q))
        for i in range(6):
            src, dst, _ = order[i // 2]
            cols = pl.ds(pl.multiple_of(c[0] * 512 + i % 2 * 256, 256), 256)
            at = pl.ds(i % 2 * 256, 256)
            copies.append(pltpu.make_async_copy(src.at[:, cols], dst.at[:, at], sems.at[i]))
            copies[-1].start()
        copies[0].wait()
        for i in range(6):
            _, w, out = order[i // 2]
            at = slice(i % 2 * 256, i % 2 * 256 + 256)
            copies[i + 1].wait()
            out[:, at] = dot(tv[...], w[:, at]).astype(BF)
        for h in range(4):
            s[head(h), :] = dot(k[:, head(h)], v[:, head(h)], 0, 0).astype(BF)

    row, weight = ((TOK, 512), BF), ((2048, 512), BF)
    return local(
        kernel,
        core,
        [tok, wq, wk, wv],
        [row] * 3 + [((512, DH), BF)] + [weight] * 3,
        hbm_in=4,
        scratch=[pltpu.VMEM((TOK, 2048), BF), pltpu.SemaphoreType.DMA((7,))],
    )


def project_kv(core, tok, wk, wv, state):
    def kernel(c, t, b, d, so, k, v, s, total):
        k[...] = dot(t[...], b[...]).astype(BF)
        v[...] = dot(t[...], d[...]).astype(BF)
        for h in range(4):
            st = dot(k[:, head(h)], v[:, head(h)], 0, 0).astype(BF)
            s[head(h), :] = st
            total[head(h), :] = (st.astype(F32) + so[head(h), :].astype(F32)).astype(BF)

    return local(
        kernel,
        core,
        [tok, wk, wv, state],
        [((TOK, 512), BF)] * 2 + [((512, DH), BF)] * 2,
    )


LOW = slice(0, 256)
HIGH = slice(256, 512)


def forward_pairs(q, k, v):
    s00 = causal(dot(q[LOW], k[LOW], 1, 1))
    s10 = dot(q[HIGH], k[LOW], 1, 1).astype(BF)
    s11 = causal(dot(q[HIGH], k[HIGH], 1, 1))
    return dot(s00, v[LOW]), dot(s10, v[LOW]) + dot(s11, v[HIGH])


def backward_pairs(q, k, x):
    s00 = causal(dot(k[LOW], q[LOW], 1, 1), True)
    s01 = dot(k[LOW], q[HIGH], 1, 1).astype(BF)
    s11 = causal(dot(k[HIGH], q[HIGH], 1, 1), True)
    return dot(s00, x[LOW]) + dot(s01, x[HIGH]), dot(s11, x[HIGH])


def masked_sum(refs, at, reverse):
    total = None
    for r, d in zip(refs, (1, 3, 2)):
        passed = at + (4 - d) < 4 if reverse else at >= d
        piece = r[...].astype(F32) * jnp.where(passed, 1.0, 0.0)
        total = piece if total is None else total + piece
    return total


def within(core, tok_p, wq, q_o, k_o, v_o, k_p, v_p):
    def kernel(c, tp, a, qo, ko, vo, kp, vp, qp, out):
        qp[...] = dot(tp[...], a[...]).astype(BF)
        for n, (q, k, v) in enumerate(((qo, ko, vo), (qp, kp, vp))):
            for h in range(4):
                low, high = forward_pairs(q[:, head(h)], k[:, head(h)], v[:, head(h)])
                out[n * TOK : n * TOK + 256, head(h)] = low
                out[n * TOK + 256 : n * TOK + 512, head(h)] = high

    return local(
        kernel,
        core,
        [tok_p, wq, q_o, k_o, v_o, k_p, v_p],
        [((TOK, 512), BF), ((2 * TOK, 512), F32)],
    )


def turned(core, tok_o, tok_p):
    def kernel(c, to, tp, out):
        out[:, :TOK] = to[...].T
        out[:, TOK:] = tp[...].T

    return call(
        kernel,
        core,
        4,
        [(tok_o, (TOK, 512), wide), (tok_p, (TOK, 512), wide)],
        [((2048, 2 * TOK), BF, (512, 2 * TOK), tall)],
        1000000,
        8 * MB,
    )[0]


def normed(core, intra, q_o, q_p, state_o, state_p, along_x, along_y, cot, cot_p):
    def kernel(c, it, qo, qp, so, sp, x1, x3, x2, y1, y3, y2, co, cp, *outs):
        ao, ap, g, po, pp, bo, bp, total = outs
        before = masked_sum((x1, x3, x2), c[2], False) + masked_sum((y1, y3, y2), c[1], False)
        late = c[0].astype(F32)
        po[...] = (before + sp[...].astype(F32) * late).astype(BF)
        pp[...] = (before + so[...].astype(F32) * (1.0 - late)).astype(BF)
        for h in range(4):
            backs = []
            for n, (q, p, a, b) in enumerate(((qo, po, ao, bo), (qp, pp, ap, bp))):
                rows = slice(n * TOK, n * TOK + TOK)
                qh = q[:, head(h)]
                mixed = it[rows, head(h)] + dot(qh, p[head(h), :])
                inverse = lax.rsqrt(jnp.mean(mixed * mixed, axis=-1, keepdims=True) + EPS)
                nm = mixed * inverse
                if n == 0:
                    up = co[:, pl.ds(pl.multiple_of(c[0] * 512 + h * DH, DH), DH)]
                else:
                    up = cp[:, head(h)]
                up = up.astype(F32)
                a[:, head(h)] = nm.astype(BF)
                gm = ((up - nm * jnp.mean(up * nm, axis=-1, keepdims=True)) * inverse).astype(BF)
                g[rows, head(h)] = gm
                back = dot(qh, gm, 0, 0).astype(BF)
                b[head(h), :] = back
                backs.append(back.astype(F32))
            total[head(h), :] = (backs[0] + backs[1]).astype(BF)

    state = ((512, DH), BF)
    return local(
        kernel,
        core,
        [intra, q_o, q_p, state_o, state_p, *along_x, *along_y, cot, cot_p],
        [((TOK, 512), BF)] * 2 + [((2 * TOK, 512), BF)] + [state] * 5,
    )


def grad_q_of(core, k_o, k_p, v_o, v_p, g, p_o, p_p):
    def kernel(c, ko, kp, vo, vp, gr, po, pp, dq):
        for n, (k, v, p) in enumerate(((ko, vo, po), (kp, vp, pp))):
            for h in range(4):
                gh = gr[n * TOK : n * TOK + TOK, head(h)]
                past = dot(gh, p[head(h), :], 1, 1)
                low, high = forward_pairs(gh, v[:, head(h)], k[:, head(h)])
                dq[n * TOK : n * TOK + 256, head(h)] = (low + past[LOW]).astype(BF)
                dq[n * TOK + 256 : n * TOK + 512, head(h)] = (high + past[HIGH]).astype(BF)

    return local(
        kernel,
        core,
        [k_o, k_p, v_o, v_p, g, p_o, p_p],
        [((2 * TOK, 512), BF)],
    )[0]


def grads_within(core, q_o, q_p, k_o, k_p, v_o, v_p, g):
    def kernel(c, qo, qp, ko, kp, vo, vp, gr, dk, dv):
        for n, (q, k, v) in enumerate(((qo, ko, vo), (qp, kp, vp))):
            for h in range(4):
                qh, kh, vh = q[:, head(h)], k[:, head(h)], v[:, head(h)]
                gh = gr[n * TOK : n * TOK + TOK, head(h)]
                for left, right, x, out in ((gh, vh, qh, dk), (qh, kh, gh, dv)):
                    low, high = backward_pairs(left, right, x)
                    out[n * TOK : n * TOK + 256, head(h)] = low
                    out[n * TOK + 256 : n * TOK + 512, head(h)] = high

    return local(
        kernel,
        core,
        [q_o, q_p, k_o, k_p, v_o, v_p, g],
        [((2 * TOK, 512), F32)] * 2,
    )


def grads_after(core, k_o, k_p, v_o, v_p, dk, dv, back_o, back_p, along_x, along_y):
    def kernel(c, ko, kp, vo, vp, ak, av, bo, bp, x1, x3, x2, y1, y3, y2, ok, ov):
        after = masked_sum((x1, x3, x2), c[2], True) + masked_sum((y1, y3, y2), c[1], True)
        late = c[0].astype(F32)
        s_o = (after + bp[...].astype(F32) * (1.0 - late)).astype(BF)
        s_p = (after + bo[...].astype(F32) * late).astype(BF)
        for n, (k, v, s) in enumerate(((ko, vo, s_o), (kp, vp, s_p))):
            rows = slice(n * TOK, n * TOK + TOK)
            for h in range(4):
                sh = s[head(h), :]
                ok[rows, head(h)] = (ak[rows, head(h)] + dot(v[:, head(h)], sh, 1, 1)).astype(BF)
                ov[rows, head(h)] = (av[rows, head(h)] + dot(k[:, head(h)], sh)).astype(BF)

    return local(
        kernel,
        core,
        [k_o, k_p, v_o, v_p, dk, dv, back_o, back_p, *along_x, *along_y],
        [((2 * TOK, 512), BF)] * 2,
    )


def weight_grad(core, tt, jobs):
    n = len(jobs)

    def kernel(c, t, *refs):
        for m, (_, axis, step) in enumerate(jobs):
            g, out = refs[m], refs[n + m]
            if axis == "x":
                rows = t[:, (c[2] + step) % 4]
            elif axis == "y":
                rows = t[(c[1] + step) % 4]
            part = dot(rows.reshape(512, 2 * TOK), g[...]).astype(BF)
            for a in range(4):
                at = (a - c[1] + 4) % 4 if axis == "x" else (a - c[2] + 4) % 4
                for core_at in range(2):
                    for z in range(4):
                        row = a * 128 + core_at * 64 + z * 16
                        out[at, (z - c[3] + 4) % 4, core_at * 16 : core_at * 16 + 16, :] = part[
                            row : row + 16, :
                        ]

    return local(
        kernel,
        core,
        [tt.reshape(4, 4, 128, 2 * TOK)] + [g for g, _, _ in jobs],
        [((4, 4, 32, 512), BF)] * n,
    )


def weight_grad_z(core, tt, grad):
    def kernel(c, t, g, out):
        gr = g[...]
        for y in range(4):
            part = dot(t[y].reshape(512, 2 * TOK), gr).astype(BF)
            dy = (y - c[1] + 4) % 4
            for x in range(4):
                dx = (x - c[2] + 4) % 4
                for core_at in range(2):
                    for z in range(4):
                        row = x * 128 + core_at * 64 + z * 16
                        here = slice(core_at * 16, core_at * 16 + 16)
                        out[(z - c[3] + 4) % 4, dx, dy, here, :] = part[row : row + 16, :]

    return local(
        kernel,
        core,
        [tt.reshape(4, 4, 128, 2 * TOK), grad],
        [((4, 4, 4, 32, 512), BF)],
    )[0]


def assembled(core, sum_q, sum_kv, came):
    def kernel(c, q, kv, r, *outs):
        scale = 65536.0**-0.5
        mine = pl.ds(pl.multiple_of(c[0] * 16, 16), 16)
        here = pl.ds(pl.multiple_of(c[0] * 512, 512), 512)
        there = pl.ds(pl.multiple_of((1 - c[0]) * 512, 512), 512)
        for m, out in enumerate(outs):
            own = q[mine, :] if m == 0 else kv[mine, m * 512 - 512 : m * 512]
            out[:, here] = own.astype(F32) * scale
            out[:, there] = r[:, m * 512 : m * 512 + 512].astype(F32) * scale

    return local(kernel, core, [sum_q, sum_kv, came], [((16, 1024), F32)] * 3)


def input_part(core, slot, grads, weights, received=None):
    final = received is not None

    def kernel(c, *refs):
        rows = slice(slot * TOK, slot * TOK + TOK)
        out = refs[7] if final else refs[6]
        copies = []
        for j in range(4):
            at = slice(j * 512, j * 512 + 512)
            total = dot(refs[0][rows, :], refs[3][at, :], 1, 1)
            total = total + dot(refs[1][rows, :], refs[4][at, :], 1, 1)
            total = total + dot(refs[2][rows, :], refs[5][at, :], 1, 1)
            if not final:
                out[:, at] = total.astype(BF)
                continue
            held, sems = refs[8:]
            held[:, at] = (total + refs[6][:, at].astype(F32)).astype(BF)
            cols = pl.ds(j * 512, 512)
            copies.append(pltpu.make_async_copy(held.at[:, cols], out.at[:, cols], sems.at[j]))
            copies[-1].start()
        for copy in copies:
            copy.wait()

    return local(
        kernel,
        core,
        [*grads, *weights] + ([received] if final else []),
        [((TOK, 2048), BF)],
        hbm_out=1 if final else 0,
        scratch=[pltpu.VMEM((TOK, 2048), BF), pltpu.SemaphoreType.DMA((4,))] if final else [],
    )[0]


def shift(v, axis, d):
    n = lax.axis_size(axis)
    return lax.ppermute(v, axis, [(i, (i + d) % n) for i in range(n)])


def swap(v):
    return lax.ppermute(v, "c", [(0, 1), (1, 0)])


def pieces(v, axis):
    return [shift(v, axis, d) for d in (1, 3, 2)]


def together(*values):
    return lax.optimization_barrier(values)


def f32_sum(*parts):
    total = parts[0].astype(F32)
    for p in parts[1:]:
        total = total + p.astype(F32)
    return total.astype(BF)


def ring_out(far, axis):
    return shift(far[:2], axis, 1), shift(far[2:], axis, 3)


def ring_near(up, down, came, axis):
    from_left, from_right = came
    up = jnp.concatenate([f32_sum(up[:2], from_left), up[2:]], axis=0)
    down = jnp.concatenate([down[:2], f32_sum(down[2:], from_right)], axis=0)
    return shift(up, axis, 1), shift(down, axis, 3)


def spread(blocks, axis):
    return f32_sum(blocks[0], *[shift(blocks[d], axis, d) for d in (2, 1, 3)])


def per_device(tokens, w_query, w_key, w_value, cotangent):
    c = lax.axis_index("c")
    core = jnp.stack([lax.axis_index(a) for a in ("c", "y", "x", "z")]).astype(jnp.int32)
    tok_o = tokens[0]
    cot = cotangent[0]
    tok_p = swap(tok_o)
    late = c == 1

    q_o, k_o, v_o, state_o, *weights = project_qkv(core, tok_o, w_query, w_key, w_value)
    k_p, v_p, state_p, total = project_kv(core, tok_p, weights[1], weights[2], state_o)
    along_x = pieces(total, "x")
    q_p, intra = within(core, tok_p, weights[0], q_o, k_o, v_o, k_p, v_p)
    row, intra, q_p, tok_t = together(f32_sum(total, *along_x), intra, q_p, tok_o)
    along_y = pieces(row, "y")
    tt = turned(core, tok_t, tok_p)
    cot_p = swap(jnp.where(late, cot[:, :512], cot[:, 512:]))
    *along_y, tt, cot_p = together(*along_y, tt, cot_p)
    a_o, a_p, g, p_o, p_p, back_o, back_p, total = normed(
        core, intra, q_o, q_p, state_o, state_p, along_x, along_y, cot, cot_p
    )
    along_x = pieces(total, "x")
    a_r = swap(a_p)
    dq = grad_q_of(core, k_o, k_p, v_o, v_p, g, p_o, p_p)
    part_q = weight_grad_z(core, tt, dq)
    row, part_q, g, a_r = together(f32_sum(total, *along_x), part_q, g, a_r)
    along_y = pieces(row, "y")
    came_q = ring_out(part_q[2], "z")
    dk, dv = grads_within(core, q_o, q_p, k_o, k_p, v_o, v_p, g)
    *along_y, dk, dv, c0, c1 = together(*along_y, dk, dv, *came_q)
    last_q = ring_near(part_q[1], part_q[3], (c0, c1), "z")
    dk, dv = grads_after(
        core, k_o, k_p, v_o, v_p, dk, dv, back_o, back_p, along_x, along_y
    )
    far_k, far_v = weight_grad(core, tt, [(dk, "x", 2), (dv, "y", 2)])
    far_k, far_v, dk, dv = together(far_k, far_v, dk, dv)
    came_k, came_v = shift(far_k, "x", 1), shift(far_v, "y", 1)
    near = weight_grad(core, tt, [(dk, "x", 1), (dk, "x", 3), (dv, "y", 1), (dv, "y", 3)])
    here_k, here_v = weight_grad(core, tt, [(dk, "x", 0), (dv, "y", 0)])
    attn_out = jnp.where(
        late, jnp.concatenate([a_r, a_o], axis=1), jnp.concatenate([a_o, a_r], axis=1)
    )
    ig_p = input_part(core, 1, (dq, dk, dv), weights)
    *near, dk, dv, here_k, here_v, ig_p, attn_out, came_k, came_v, q0, q1 = together(
        *near, dk, dv, here_k, here_v, ig_p, attn_out, came_k, came_v, *last_q
    )
    sum_q = f32_sum(part_q[0], q0, q1)
    up_k = jnp.concatenate([f32_sum(near[0], came_k), sum_q[2:3]], axis=0)
    last = [shift(up_k, "x", 1), shift(near[1], "x", 3)]
    last += [shift(f32_sum(near[2], came_v), "y", 1), shift(near[3], "y", 3)]
    ig_r = swap(ig_p)
    input_grad = input_part(core, 0, (dq, dk, dv), weights, ig_r)
    sum_q, input_grad, *last = together(sum_q, input_grad, *last)
    sum_k = f32_sum(here_k, last[0][:4], last[1])
    sum_v = f32_sum(here_v, *last[2:])
    up = jnp.stack([sum_v[1], f32_sum(sum_q[1], last[0][4])])
    down = jnp.stack([sum_v[3], sum_q[3]])
    up, down, far = shift(up, "x", 1), shift(down, "x", 3), shift(sum_v[2], "x", 2)
    sum_k = spread(sum_k, "y")
    sum_v = f32_sum(sum_v[0], up[0], down[0], far)
    sum_q = f32_sum(sum_q[0], up[1], down[1])
    sum_kv = spread(jnp.concatenate([sum_k, sum_v], axis=-1), "z")
    sum_q = spread(sum_q, "y")
    summed = jnp.concatenate([sum_q, sum_kv], axis=1)
    came = swap(jnp.where(late, summed[:16], summed[16:]))
    return (attn_out[None], input_grad[None], *assembled(core, sum_q, sum_kv, came))


def solution(mesh):
    finer = Mesh(mesh.devices.reshape(4, 4, 2, mesh.shape["dp"]), ("y", "x", "c", "z"))
    return jax.shard_map(
        per_device,
        mesh=finer,
        in_specs=(P("z", CTX, None), P(), P(), P(), P("z", CTX, None)),
        out_specs=(
            P("z", CTX, None),
            P("z", CTX, None),
            P(CTX_DP, None),
            P(CTX_DP, None),
            P(CTX_DP, None),
        ),
        check_vma=False,
    )
```

```python
import jax
import jax.numpy as jnp
from jax import lax
from jax.experimental import pallas as pl
from jax.experimental.pallas import tpu as pltpu
from jax.sharding import Mesh
from jax.sharding import PartitionSpec as P

DH = 128
TOK = 512
EPS = 1e-05
CTX = ("y", "x", "c")
CTX_DP = ("y", "x", "c", "z")
BF = jnp.bfloat16
F32 = jnp.float32
MB = 1 << 20


def dot(a, b, ca=1, cb=0):
    return lax.dot_general(a, b, (((ca,), (cb,)), ((), ())), preferred_element_type=F32)


def causal(x, turned=False):
    rows = lax.broadcasted_iota(jnp.int32, x.shape, 0)
    cols = lax.broadcasted_iota(jnp.int32, x.shape, 1)
    keep = rows <= cols if turned else rows >= cols
    return jnp.where(keep, x, 0.0).astype(BF)


def head(h):
    return slice(h * DH, (h + 1) * DH)


def call(kernel, core, grid, ins, outs, flops, moved, limit=20):
    return pl.pallas_call(
        kernel,
        out_shape=[jax.ShapeDtypeStruct(s, d) for s, d, _, _ in outs],
        grid_spec=pltpu.PrefetchScalarGridSpec(
            num_scalar_prefetch=1,
            grid=(grid,),
            in_specs=[pl.BlockSpec(b, m) for _, b, m in ins],
            out_specs=[pl.BlockSpec(b, m) for _, _, b, m in outs],
        ),
        compiler_params=pltpu.CompilerParams(
            dimension_semantics=("arbitrary",), vmem_limit_bytes=limit * MB
        ),
        cost_estimate=pl.CostEstimate(flops=flops, bytes_accessed=moved, transcendentals=0),
    )(core, *[a for a, _, _ in ins])


def local(kernel, core, ins, outs, hbm_in=0, hbm_out=0, scratch=()):
    vmem, hbm = pl.BlockSpec(memory_space=pltpu.VMEM), pl.BlockSpec(memory_space=pltpu.HBM)
    return pl.pallas_call(
        kernel,
        out_shape=[jax.ShapeDtypeStruct(s, d) for s, d in outs],
        in_specs=[pl.BlockSpec(memory_space=pltpu.SMEM)]
        + [vmem] * (len(ins) - hbm_in)
        + [hbm] * hbm_in,
        out_specs=[vmem] * (len(outs) - hbm_out) + [hbm] * hbm_out,
        scratch_shapes=list(scratch),
        compiler_params=pltpu.CompilerParams(vmem_limit_bytes=20 * MB),
        cost_estimate=pl.CostEstimate(flops=1000000, bytes_accessed=1000, transcendentals=0),
    )(core, *ins)


def whole(j, c):
    return (0, 0)


def tall(j, c):
    return (j, 0)


def wide(j, c):
    return (0, j)


def mine(j, c):
    return (0, c[0] * 2 + j)


def in_hbm(*arrays):
    return [pltpu.with_memory_space_constraint(t, pltpu.HBM) for t in arrays]


def half_of(which):
    return pl.ds(pl.multiple_of(which * 512, 512), 512)


def project_own(core, tok, wk, wv):
    def kernel(c, t, b, d, k, v, s, bh, dh, tv, sems):
        copies = [pltpu.make_async_copy(t, tv, sems.at[0])]
        copies.append(pltpu.make_async_copy(b.at[:, half_of(c[0])], bh, sems.at[1]))
        copies.append(pltpu.make_async_copy(d.at[:, half_of(c[0])], dh, sems.at[2]))
        for copy in copies:
            copy.start()
        copies[0].wait()
        copies[1].wait()
        k[...] = dot(tv[...], bh[...]).astype(BF)
        copies[2].wait()
        v[...] = dot(tv[...], dh[...]).astype(BF)
        for h in range(4):
            s[head(h), :] = dot(k[:, head(h)], v[:, head(h)], 0, 0).astype(BF)

    row, weight = ((TOK, 512), BF), ((2048, 512), BF)
    return local(
        kernel,
        core,
        in_hbm(tok, wk, wv),
        [row] * 2 + [((512, DH), BF)] + [weight] * 2,
        hbm_in=3,
        scratch=[pltpu.VMEM((TOK, 2048), BF), pltpu.SemaphoreType.DMA((3,))],
    )


def project_partner(core, tok, wk, wv, state, wq, cot):
    def kernel(c, t, b, d, so, a, ct, k, v, s, total, ah, mine_ct, other_ct, sems):
        copies = [
            pltpu.make_async_copy(a.at[:, half_of(c[0])], ah, sems.at[0]),
            pltpu.make_async_copy(ct.at[:, half_of(1 - c[0])], other_ct, sems.at[1]),
            pltpu.make_async_copy(ct.at[:, half_of(c[0])], mine_ct, sems.at[2]),
        ]
        for copy in copies:
            copy.start()
        k[...] = dot(t[...], b[...]).astype(BF)
        v[...] = dot(t[...], d[...]).astype(BF)
        for h in range(4):
            st = dot(k[:, head(h)], v[:, head(h)], 0, 0).astype(BF)
            s[head(h), :] = st
            total[head(h), :] = (st.astype(F32) + so[head(h), :].astype(F32)).astype(BF)
        for copy in copies:
            copy.wait()

    row = ((TOK, 512), BF)
    return local(
        kernel,
        core,
        [tok, wk, wv, state, *in_hbm(wq, cot)],
        [row] * 2 + [((512, DH), BF)] * 2 + [((2048, 512), BF)] + [row] * 2,
        hbm_in=2,
        scratch=[pltpu.SemaphoreType.DMA((3,))],
    )


LOW = slice(0, 256)
HIGH = slice(256, 512)


def forward_pairs(q, k, v):
    s00 = causal(dot(q[LOW], k[LOW], 1, 1))
    s10 = dot(q[HIGH], k[LOW], 1, 1).astype(BF)
    s11 = causal(dot(q[HIGH], k[HIGH], 1, 1))
    return dot(s00, v[LOW]), dot(s10, v[LOW]) + dot(s11, v[HIGH])


def backward_pairs(q, k, x):
    s00 = causal(dot(k[LOW], q[LOW], 1, 1), True)
    s01 = dot(k[LOW], q[HIGH], 1, 1).astype(BF)
    s11 = causal(dot(k[HIGH], q[HIGH], 1, 1), True)
    return dot(s00, x[LOW]) + dot(s01, x[HIGH]), dot(s11, x[HIGH])


def masked_sum(refs, at, reverse):
    total = None
    for r, d in zip(refs, (1, 3, 2)):
        passed = at + (4 - d) < 4 if reverse else at >= d
        piece = r[...].astype(F32) * jnp.where(passed, 1.0, 0.0)
        total = piece if total is None else total + piece
    return total


def within(core, tok_o, tok_p, wq, k_o, v_o, k_p, v_p):
    def kernel(c, to, tp, a, ko, vo, kp, vp, qo, qp, out):
        qo[...] = dot(to[...], a[...]).astype(BF)
        qp[...] = dot(tp[...], a[...]).astype(BF)
        for n, (q, k, v) in enumerate(((qo, ko, vo), (qp, kp, vp))):
            for h in range(4):
                low, high = forward_pairs(q[:, head(h)], k[:, head(h)], v[:, head(h)])
                out[n * TOK : n * TOK + 256, head(h)] = low
                out[n * TOK + 256 : n * TOK + 512, head(h)] = high

    return local(
        kernel,
        core,
        [tok_o, tok_p, wq, k_o, v_o, k_p, v_p],
        [((TOK, 512), BF)] * 2 + [((2 * TOK, 512), F32)],
    )


def turned(core, tok_o, tok_p):
    def kernel(c, to, tp, out):
        out[:, :TOK] = to[...].T
        out[:, TOK:] = tp[...].T

    return call(
        kernel,
        core,
        4,
        [(tok_o, (TOK, 512), wide), (tok_p, (TOK, 512), wide)],
        [((2048, 2 * TOK), BF, (512, 2 * TOK), tall)],
        1000000,
        8 * MB,
    )[0]


def normed(core, intra, q_o, q_p, state_o, state_p, along_x, along_y, cot, cot_p):
    def kernel(c, it, qo, qp, so, sp, x1, x3, x2, y1, y3, y2, co, cp, *outs):
        ao, ap, g, po, pp, bo, bp, total = outs
        before = masked_sum((x1, x3, x2), c[2], False) + masked_sum((y1, y3, y2), c[1], False)
        late = c[0].astype(F32)
        po[...] = (before + sp[...].astype(F32) * late).astype(BF)
        pp[...] = (before + so[...].astype(F32) * (1.0 - late)).astype(BF)
        for h in range(4):
            backs = []
            for n, (q, p, a, b) in enumerate(((qo, po, ao, bo), (qp, pp, ap, bp))):
                rows = slice(n * TOK, n * TOK + TOK)
                qh = q[:, head(h)]
                mixed = it[rows, head(h)] + dot(qh, p[head(h), :])
                inverse = lax.rsqrt(jnp.mean(mixed * mixed, axis=-1, keepdims=True) + EPS)
                nm = mixed * inverse
                up = (co if n == 0 else cp)[:, head(h)].astype(F32)
                a[:, head(h)] = nm.astype(BF)
                gm = ((up - nm * jnp.mean(up * nm, axis=-1, keepdims=True)) * inverse).astype(BF)
                g[rows, head(h)] = gm
                back = dot(qh, gm, 0, 0).astype(BF)
                b[head(h), :] = back
                backs.append(back.astype(F32))
            total[head(h), :] = (backs[0] + backs[1]).astype(BF)

    state = ((512, DH), BF)
    return local(
        kernel,
        core,
        [intra, q_o, q_p, state_o, state_p, *along_x, *along_y, cot, cot_p],
        [((TOK, 512), BF)] * 2 + [((2 * TOK, 512), BF)] + [state] * 5,
    )


def grad_q_of(core, k_o, k_p, v_o, v_p, g, p_o, p_p):
    def kernel(c, ko, kp, vo, vp, gr, po, pp, dq):
        for n, (k, v, p) in enumerate(((ko, vo, po), (kp, vp, pp))):
            for h in range(4):
                gh = gr[n * TOK : n * TOK + TOK, head(h)]
                past = dot(gh, p[head(h), :], 1, 1)
                low, high = forward_pairs(gh, v[:, head(h)], k[:, head(h)])
                dq[n * TOK : n * TOK + 256, head(h)] = (low + past[LOW]).astype(BF)
                dq[n * TOK + 256 : n * TOK + 512, head(h)] = (high + past[HIGH]).astype(BF)

    return local(
        kernel,
        core,
        [k_o, k_p, v_o, v_p, g, p_o, p_p],
        [((2 * TOK, 512), BF)],
    )[0]


def grads_within(core, q_o, q_p, k_o, k_p, v_o, v_p, g):
    def kernel(c, qo, qp, ko, kp, vo, vp, gr, dk, dv):
        for n, (q, k, v) in enumerate(((qo, ko, vo), (qp, kp, vp))):
            for h in range(4):
                qh, kh, vh = q[:, head(h)], k[:, head(h)], v[:, head(h)]
                gh = gr[n * TOK : n * TOK + TOK, head(h)]
                for left, right, x, out in ((gh, vh, qh, dk), (qh, kh, gh, dv)):
                    low, high = backward_pairs(left, right, x)
                    out[n * TOK : n * TOK + 256, head(h)] = low
                    out[n * TOK + 256 : n * TOK + 512, head(h)] = high

    return local(
        kernel,
        core,
        [q_o, q_p, k_o, k_p, v_o, v_p, g],
        [((2 * TOK, 512), F32)] * 2,
    )


def grads_after(core, k_o, k_p, v_o, v_p, dk, dv, back_o, back_p, along_x, along_y):
    def kernel(c, ko, kp, vo, vp, ak, av, bo, bp, x1, x3, x2, y1, y3, y2, ok, ov):
        after = masked_sum((x1, x3, x2), c[2], True) + masked_sum((y1, y3, y2), c[1], True)
        late = c[0].astype(F32)
        s_o = (after + bp[...].astype(F32) * (1.0 - late)).astype(BF)
        s_p = (after + bo[...].astype(F32) * late).astype(BF)
        for n, (k, v, s) in enumerate(((ko, vo, s_o), (kp, vp, s_p))):
            rows = slice(n * TOK, n * TOK + TOK)
            for h in range(4):
                sh = s[head(h), :]
                ok[rows, head(h)] = (ak[rows, head(h)] + dot(v[:, head(h)], sh, 1, 1)).astype(BF)
                ov[rows, head(h)] = (av[rows, head(h)] + dot(k[:, head(h)], sh)).astype(BF)

    return local(
        kernel,
        core,
        [k_o, k_p, v_o, v_p, dk, dv, back_o, back_p, *along_x, *along_y],
        [((2 * TOK, 512), BF)] * 2,
    )


def weight_grad(core, tt, jobs):
    n = len(jobs)

    def kernel(c, t, *refs):
        for m, (_, axis, step) in enumerate(jobs):
            g, out = refs[m], refs[n + m]
            if axis == "x":
                rows = t[:, (c[2] + step) % 4]
            elif axis == "y":
                rows = t[(c[1] + step) % 4]
            part = dot(rows.reshape(512, 2 * TOK), g[...]).astype(BF)
            for a in range(4):
                at = (a - c[1] + 4) % 4 if axis == "x" else (a - c[2] + 4) % 4
                for core_at in range(2):
                    for z in range(4):
                        row = a * 128 + core_at * 64 + z * 16
                        out[at, (z - c[3] + 4) % 4, core_at * 16 : core_at * 16 + 16, :] = part[
                            row : row + 16, :
                        ]

    return local(
        kernel,
        core,
        [tt.reshape(4, 4, 128, 2 * TOK)] + [g for g, _, _ in jobs],
        [((4, 4, 32, 512), BF)] * n,
    )


def weight_grad_all(core, tt, grad):
    def kernel(c, t, g, out):
        gr = g[...]
        for y in range(4):
            part = dot(t[y].reshape(512, 2 * TOK), gr).astype(BF)
            dy = (y - c[1] + 4) % 4
            for x in range(4):
                dx = (x - c[2] + 4) % 4
                for core_at in range(2):
                    for z in range(4):
                        row = x * 128 + core_at * 64 + z * 16
                        here = slice(core_at * 16, core_at * 16 + 16)
                        out[dx, dy, (z - c[3] + 4) % 4, here, :] = part[row : row + 16, :]

    return local(
        kernel,
        core,
        [tt.reshape(4, 4, 128, 2 * TOK), grad],
        [((4, 4, 4, 32, 512), BF)],
    )[0]


def joined_heads(core, own, received):
    def kernel(c, o, r, out, sems):
        copies = [
            pltpu.make_async_copy(o, out.at[:, half_of(c[0])], sems.at[0]),
            pltpu.make_async_copy(r, out.at[:, half_of(1 - c[0])], sems.at[1]),
        ]
        for copy in copies:
            copy.start()
        for copy in copies:
            copy.wait()

    return local(
        kernel,
        core,
        [own, received],
        [((TOK, 1024), BF)],
        hbm_out=1,
        scratch=[pltpu.SemaphoreType.DMA((2,))],
    )[0]


def assembled(core, summed, came):
    def kernel(c, qkv, r, *outs):
        scale = 65536.0**-0.5
        mine = pl.ds(pl.multiple_of(c[0] * 16, 16), 16)
        here = pl.ds(pl.multiple_of(c[0] * 512, 512), 512)
        there = pl.ds(pl.multiple_of((1 - c[0]) * 512, 512), 512)
        for m, out in enumerate(outs):
            out[:, here] = qkv[mine, m * 512 : m * 512 + 512].astype(F32) * scale
            out[:, there] = r[:, m * 512 : m * 512 + 512].astype(F32) * scale

    return local(kernel, core, [summed, came], [((16, 1024), F32)] * 3)


def input_part(core, slot, grads, weights, received=None):
    final = received is not None

    def kernel(c, *refs):
        rows = slice(slot * TOK, slot * TOK + TOK)
        out = refs[7] if final else refs[6]
        copies = []
        for j in range(4):
            at = slice(j * 512, j * 512 + 512)
            total = dot(refs[0][rows, :], refs[3][at, :], 1, 1)
            total = total + dot(refs[1][rows, :], refs[4][at, :], 1, 1)
            total = total + dot(refs[2][rows, :], refs[5][at, :], 1, 1)
            if not final:
                out[:, at] = total.astype(BF)
                continue
            held, sems = refs[8:]
            held[:, at] = (total + refs[6][:, at].astype(F32)).astype(BF)
            cols = pl.ds(j * 512, 512)
            copies.append(pltpu.make_async_copy(held.at[:, cols], out.at[:, cols], sems.at[j]))
            copies[-1].start()
        for copy in copies:
            copy.wait()

    return local(
        kernel,
        core,
        [*grads, *weights] + ([received] if final else []),
        [((TOK, 2048), BF)],
        hbm_out=1 if final else 0,
        scratch=[pltpu.VMEM((TOK, 2048), BF), pltpu.SemaphoreType.DMA((4,))] if final else [],
    )[0]


def shift(v, axis, d):
    n = lax.axis_size(axis)
    return lax.ppermute(v, axis, [(i, (i + d) % n) for i in range(n)])


def swap(v):
    return lax.ppermute(v, "c", [(0, 1), (1, 0)])


def pieces(v, axis):
    return [shift(v, axis, d) for d in (1, 3, 2)]


def together(*values):
    return lax.optimization_barrier(values)


def f32_sum(*parts):
    total = parts[0].astype(F32)
    for p in parts[1:]:
        total = total + p.astype(F32)
    return total.astype(BF)


def ring_out(far, axis):
    return shift(far[:2], axis, 1), shift(far[2:], axis, 3)


def ring_near(up, down, came, axis):
    from_left, from_right = came
    up = jnp.concatenate([f32_sum(up[:2], from_left), up[2:]], axis=0)
    down = jnp.concatenate([down[:2], f32_sum(down[2:], from_right)], axis=0)
    return shift(up, axis, 1), shift(down, axis, 3)


def spread(blocks, axis):
    return f32_sum(blocks[0], *[shift(blocks[d], axis, d) for d in (2, 1, 3)])


def per_device(tokens, w_query, w_key, w_value, cotangent):
    c = lax.axis_index("c")
    core = jnp.stack([lax.axis_index(a) for a in ("c", "y", "x", "z")]).astype(jnp.int32)
    tok_o = tokens[0]
    tok_p = swap(tok_o)
    late = c == 1

    k_o, v_o, state_o, w_k, w_v = project_own(core, tok_o, w_key, w_value)
    k_p, v_p, state_p, total, w_q, cot, cot_s = project_partner(
        core, tok_p, w_k, w_v, state_o, w_query, cotangent[0]
    )
    weights = (w_q, w_k, w_v)
    along_x = pieces(total, "x")
    cot_p = swap(cot_s)
    q_o, q_p, intra = within(core, tok_o, tok_p, w_q, k_o, v_o, k_p, v_p)
    row, intra, q_o, q_p, tok_t, cot_p = together(
        f32_sum(total, *along_x), intra, q_o, q_p, tok_o, cot_p
    )
    along_y = pieces(row, "y")
    tt = turned(core, tok_t, tok_p)
    *along_y, tt = together(*along_y, tt)
    a_o, a_p, g, p_o, p_p, back_o, back_p, total = normed(
        core, intra, q_o, q_p, state_o, state_p, along_x, along_y, cot, cot_p
    )
    along_x = pieces(total, "x")
    a_r = swap(a_p)
    dq = grad_q_of(core, k_o, k_p, v_o, v_p, g, p_o, p_p)
    part_q = weight_grad_all(core, tt, dq)
    row, part_q, g, a_r = together(f32_sum(total, *along_x), part_q, g, a_r)
    along_y = pieces(row, "y")
    came_q = ring_out(part_q[2], "x")
    dk, dv = grads_within(core, q_o, q_p, k_o, k_p, v_o, v_p, g)
    *along_y, dk, dv, c0, c1 = together(*along_y, dk, dv, *came_q)
    last_q = ring_near(part_q[1], part_q[3], (c0, c1), "x")
    dk, dv = grads_after(
        core, k_o, k_p, v_o, v_p, dk, dv, back_o, back_p, along_x, along_y
    )
    far_k, far_v = weight_grad(core, tt, [(dk, "x", 2), (dv, "y", 2)])
    far_k, far_v, dk, dv = together(far_k, far_v, dk, dv)
    came_k, came_v = ring_out(far_k, "x"), shift(far_v, "y", 1)
    near = weight_grad(core, tt, [(dk, "x", 1), (dk, "x", 3), (dv, "y", 1), (dv, "y", 3)])
    here_k, here_v = weight_grad(core, tt, [(dk, "x", 0), (dv, "y", 0)])
    attn_out = joined_heads(core, a_o, a_r)
    ig_p = input_part(core, 1, (dq, dk, dv), weights)
    *near, dk, dv, here_k, here_v, ig_p, attn_out, k0, k1, came_v, q0, q1 = together(
        *near, dk, dv, here_k, here_v, ig_p, attn_out, *came_k, came_v, *last_q
    )
    last_k = ring_near(near[0], near[1], (k0, k1), "x")
    sum_q = f32_sum(part_q[0], q0, q1)
    flat = (16, 32, 512)
    up = jnp.concatenate([f32_sum(near[2], came_v).reshape(flat), sum_q[2, :2]], axis=0)
    down = jnp.concatenate([near[3].reshape(flat), sum_q[2, 2:]], axis=0)
    last_v = [shift(up, "y", 1), shift(down, "y", 3)]
    ig_r = swap(ig_p)
    input_grad = input_part(core, 0, (dq, dk, dv), weights, ig_r)
    sum_q, input_grad, k0, k1, v0, v1 = together(sum_q, input_grad, *last_k, *last_v)
    sum_k = f32_sum(here_k, k0, k1)
    sum_v = f32_sum(here_v.reshape(flat), v0[:16], v1[:16]).reshape(4, 4, 32, 512)
    up_q = jnp.concatenate([f32_sum(sum_q[1, :2], v0[16:]), sum_q[1, 2:]], axis=0)
    down_q = jnp.concatenate([sum_q[3, :2], f32_sum(sum_q[3, 2:], v1[16:])], axis=0)
    up, down = jnp.stack([sum_k[1], up_q]), jnp.stack([sum_k[3], down_q])
    up, down, far = shift(up, "y", 1), shift(down, "y", 3), shift(sum_k[2], "y", 2)
    sum_v = spread(sum_v, "x")
    sum_k = f32_sum(sum_k[0], up[0], down[0], far)
    sum_q = f32_sum(sum_q[0], up[1], down[1])
    summed = spread(jnp.concatenate([sum_q, sum_k, sum_v], axis=-1), "z")
    came = swap(jnp.where(late, summed[:16], summed[16:]))
    return (attn_out[None], input_grad[None], *assembled(core, summed, came))


def solution(mesh):
    finer = Mesh(mesh.devices.reshape(4, 4, 2, mesh.shape["dp"]), ("y", "x", "c", "z"))
    return jax.shard_map(
        per_device,
        mesh=finer,
        in_specs=(P("z", CTX, None), P(), P(), P(), P("z", CTX, None)),
        out_specs=(
            P("z", CTX, None),
            P("z", CTX, None),
            P(CTX_DP, None),
            P(CTX_DP, None),
            P(CTX_DP, None),
        ),
        check_vma=False,
    )
```

```python
import jax
import jax.numpy as jnp
from jax import lax
from jax.experimental import pallas as pl
from jax.experimental.pallas import tpu as pltpu
from jax.sharding import Mesh
from jax.sharding import PartitionSpec as P

DH = 128
TOK = 512
EPS = 1e-05
CTX = ("y", "x", "c")
CTX_DP = ("y", "x", "c", "z")
BF = jnp.bfloat16
F32 = jnp.float32
MB = 1 << 20


def dot(a, b, ca=1, cb=0):
    return lax.dot_general(a, b, (((ca,), (cb,)), ((), ())), preferred_element_type=F32)


def causal(x, turned=False):
    rows = lax.broadcasted_iota(jnp.int32, x.shape, 0)
    cols = lax.broadcasted_iota(jnp.int32, x.shape, 1)
    keep = rows <= cols if turned else rows >= cols
    return jnp.where(keep, x, 0.0).astype(BF)


def head(h):
    if isinstance(h, int):
        return slice(h * DH, (h + 1) * DH)
    return pl.ds(pl.multiple_of(h * DH, DH), DH)


def each_head(body):
    def step(h, carry):
        body(h)
        return carry

    lax.fori_loop(0, 4, step, 0)


def call(kernel, core, grid, ins, outs, flops, moved, limit=20):
    return pl.pallas_call(
        kernel,
        out_shape=[jax.ShapeDtypeStruct(s, d) for s, d, _, _ in outs],
        grid_spec=pltpu.PrefetchScalarGridSpec(
            num_scalar_prefetch=1,
            grid=(grid,),
            in_specs=[pl.BlockSpec(b, m) for _, b, m in ins],
            out_specs=[pl.BlockSpec(b, m) for _, _, b, m in outs],
        ),
        compiler_params=pltpu.CompilerParams(
            dimension_semantics=("arbitrary",), vmem_limit_bytes=limit * MB
        ),
        cost_estimate=pl.CostEstimate(flops=flops, bytes_accessed=moved, transcendentals=0),
    )(core, *[a for a, _, _ in ins])


def local(kernel, core, ins, outs, hbm_in=0, hbm_out=0, scratch=()):
    vmem, hbm = pl.BlockSpec(memory_space=pltpu.VMEM), pl.BlockSpec(memory_space=pltpu.HBM)
    return pl.pallas_call(
        kernel,
        out_shape=[jax.ShapeDtypeStruct(s, d) for s, d in outs],
        in_specs=[pl.BlockSpec(memory_space=pltpu.SMEM)]
        + [vmem] * (len(ins) - hbm_in)
        + [hbm] * hbm_in,
        out_specs=[vmem] * (len(outs) - hbm_out) + [hbm] * hbm_out,
        scratch_shapes=list(scratch),
        compiler_params=pltpu.CompilerParams(vmem_limit_bytes=20 * MB),
        cost_estimate=pl.CostEstimate(flops=1000000, bytes_accessed=1000, transcendentals=0),
    )(core, *ins)


def whole(j, c):
    return (0, 0)


def tall(j, c):
    return (j, 0)


def wide(j, c):
    return (0, j)


def mine(j, c):
    return (0, c[0] * 2 + j)


def in_hbm(*arrays):
    return [pltpu.with_memory_space_constraint(t, pltpu.HBM) for t in arrays]


def half_of(which):
    return pl.ds(pl.multiple_of(which * 512, 512), 512)


def project_own(core, tok, wk, wv):
    def kernel(c, t, b, d, k, v, s, bh, dh, tv, sems):
        copies = [pltpu.make_async_copy(t, tv, sems.at[0])]
        copies.append(pltpu.make_async_copy(b.at[:, half_of(c[0])], bh, sems.at[1]))
        copies.append(pltpu.make_async_copy(d.at[:, half_of(c[0])], dh, sems.at[2]))
        for copy in copies:
            copy.start()
        copies[0].wait()
        copies[1].wait()
        k[...] = dot(tv[...], bh[...]).astype(BF)
        copies[2].wait()
        v[...] = dot(tv[...], dh[...]).astype(BF)
        for h in range(4):
            s[head(h), :] = dot(k[:, head(h)], v[:, head(h)], 0, 0).astype(BF)

    row, weight = ((TOK, 512), BF), ((2048, 512), BF)
    return local(
        kernel,
        core,
        in_hbm(tok, wk, wv),
        [row] * 2 + [((512, DH), BF)] + [weight] * 2,
        hbm_in=3,
        scratch=[pltpu.VMEM((TOK, 2048), BF), pltpu.SemaphoreType.DMA((3,))],
    )


def project_partner(core, tok, wk, wv, state, wq):
    def kernel(c, t, b, d, so, a, k, v, s, total, ah, sem):
        copy = pltpu.make_async_copy(a.at[:, half_of(c[0])], ah, sem)
        copy.start()
        k[...] = dot(t[...], b[...]).astype(BF)
        v[...] = dot(t[...], d[...]).astype(BF)
        for h in range(4):
            st = dot(k[:, head(h)], v[:, head(h)], 0, 0).astype(BF)
            s[head(h), :] = st
            total[head(h), :] = (st.astype(F32) + so[head(h), :].astype(F32)).astype(BF)
        copy.wait()

    row = ((TOK, 512), BF)
    return local(
        kernel,
        core,
        [tok, wk, wv, state, *in_hbm(wq)],
        [row] * 2 + [((512, DH), BF)] * 2 + [((2048, 512), BF)],
        hbm_in=1,
        scratch=[pltpu.SemaphoreType.DMA],
    )


LOW = slice(0, 256)
HIGH = slice(256, 512)


def forward_pairs(q, k, v):
    s00 = causal(dot(q[LOW], k[LOW], 1, 1))
    s10 = dot(q[HIGH], k[LOW], 1, 1).astype(BF)
    s11 = causal(dot(q[HIGH], k[HIGH], 1, 1))
    return dot(s00, v[LOW]), dot(s10, v[LOW]) + dot(s11, v[HIGH])


def backward_pairs(q, k, x):
    s00 = causal(dot(k[LOW], q[LOW], 1, 1), True)
    s01 = dot(k[LOW], q[HIGH], 1, 1).astype(BF)
    s11 = causal(dot(k[HIGH], q[HIGH], 1, 1), True)
    return dot(s00, x[LOW]) + dot(s01, x[HIGH]), dot(s11, x[HIGH])


def masked_sum(refs, at, reverse):
    total = None
    for r, d in zip(refs, (1, 3, 2)):
        passed = at + (4 - d) < 4 if reverse else at >= d
        piece = r[...].astype(F32) * jnp.where(passed, 1.0, 0.0)
        total = piece if total is None else total + piece
    return total


def within(core, tok_o, tok_p, wq, k_o, v_o, k_p, v_p, cot):
    def kernel(c, to, tp, a, ko, vo, kp, vp, ct, qo, qp, out, mine_ct, other_ct, sems):
        copies = [
            pltpu.make_async_copy(ct.at[:, half_of(1 - c[0])], other_ct, sems.at[0]),
            pltpu.make_async_copy(ct.at[:, half_of(c[0])], mine_ct, sems.at[1]),
        ]
        for copy in copies:
            copy.start()
        qo[...] = dot(to[...], a[...]).astype(BF)
        qp[...] = dot(tp[...], a[...]).astype(BF)

        @each_head
        def _(h):
            for n, (q, k, v) in enumerate(((qo, ko, vo), (qp, kp, vp))):
                low, high = forward_pairs(q[:, head(h)], k[:, head(h)], v[:, head(h)])
                out[n * TOK : n * TOK + 256, head(h)] = low
                out[n * TOK + 256 : n * TOK + 512, head(h)] = high

        for copy in copies:
            copy.wait()

    return local(
        kernel,
        core,
        [tok_o, tok_p, wq, k_o, v_o, k_p, v_p, *in_hbm(cot)],
        [((TOK, 512), BF)] * 2 + [((2 * TOK, 512), F32)] + [((TOK, 512), BF)] * 2,
        hbm_in=1,
        scratch=[pltpu.SemaphoreType.DMA((2,))],
    )


def turned(core, tok_o, tok_p):
    def kernel(c, to, tp, out):
        out[:, :TOK] = to[...].T
        out[:, TOK:] = tp[...].T

    return call(
        kernel,
        core,
        4,
        [(tok_o, (TOK, 512), wide), (tok_p, (TOK, 512), wide)],
        [((2048, 2 * TOK), BF, (512, 2 * TOK), tall)],
        1000000,
        8 * MB,
    )[0]


def normed(core, intra, q_o, q_p, state_o, state_p, along_x, along_y, cot, cot_p):
    def kernel(c, it, qo, qp, so, sp, x1, x3, x2, y1, y3, y2, co, cp, *outs):
        ao, ap, g, po, pp, bo, bp, total = outs
        before = masked_sum((x1, x3, x2), c[2], False) + masked_sum((y1, y3, y2), c[1], False)
        late = c[0].astype(F32)
        po[...] = (before + sp[...].astype(F32) * late).astype(BF)
        pp[...] = (before + so[...].astype(F32) * (1.0 - late)).astype(BF)

        @each_head
        def _(h):
            backs = []
            for n, (q, p, a, b) in enumerate(((qo, po, ao, bo), (qp, pp, ap, bp))):
                rows = slice(n * TOK, n * TOK + TOK)
                qh = q[:, head(h)]
                mixed = it[rows, head(h)] + dot(qh, p[head(h), :])
                inverse = lax.rsqrt(jnp.mean(mixed * mixed, axis=-1, keepdims=True) + EPS)
                nm = mixed * inverse
                up = (co if n == 0 else cp)[:, head(h)].astype(F32)
                a[:, head(h)] = nm.astype(BF)
                gm = ((up - nm * jnp.mean(up * nm, axis=-1, keepdims=True)) * inverse).astype(BF)
                g[rows, head(h)] = gm
                back = dot(qh, gm, 0, 0).astype(BF)
                b[head(h), :] = back
                backs.append(back.astype(F32))
            total[head(h), :] = (backs[0] + backs[1]).astype(BF)

    state = ((512, DH), BF)
    return local(
        kernel,
        core,
        [intra, q_o, q_p, state_o, state_p, *along_x, *along_y, cot, cot_p],
        [((TOK, 512), BF)] * 2 + [((2 * TOK, 512), BF)] + [state] * 5,
    )


def grad_q_of(core, k_o, k_p, v_o, v_p, g, p_o, p_p):
    def kernel(c, ko, kp, vo, vp, gr, po, pp, dq):
        @each_head
        def _(h):
            for n, (k, v, p) in enumerate(((ko, vo, po), (kp, vp, pp))):
                gh = gr[n * TOK : n * TOK + TOK, head(h)]
                past = dot(gh, p[head(h), :], 1, 1)
                low, high = forward_pairs(gh, v[:, head(h)], k[:, head(h)])
                dq[n * TOK : n * TOK + 256, head(h)] = (low + past[LOW]).astype(BF)
                dq[n * TOK + 256 : n * TOK + 512, head(h)] = (high + past[HIGH]).astype(BF)

    return local(
        kernel,
        core,
        [k_o, k_p, v_o, v_p, g, p_o, p_p],
        [((2 * TOK, 512), BF)],
    )[0]


def grads_within(core, q_o, q_p, k_o, k_p, v_o, v_p, g):
    def kernel(c, qo, qp, ko, kp, vo, vp, gr, dk, dv):
        @each_head
        def _(h):
            for n, (q, k, v) in enumerate(((qo, ko, vo), (qp, kp, vp))):
                qh, kh, vh = q[:, head(h)], k[:, head(h)], v[:, head(h)]
                gh = gr[n * TOK : n * TOK + TOK, head(h)]
                for left, right, x, out in ((gh, vh, qh, dk), (qh, kh, gh, dv)):
                    low, high = backward_pairs(left, right, x)
                    out[n * TOK : n * TOK + 256, head(h)] = low
                    out[n * TOK + 256 : n * TOK + 512, head(h)] = high

    return local(
        kernel,
        core,
        [q_o, q_p, k_o, k_p, v_o, v_p, g],
        [((2 * TOK, 512), F32)] * 2,
    )


def grads_after(core, k_o, k_p, v_o, v_p, dk, dv, back_o, back_p, along_x, along_y):
    def kernel(c, ko, kp, vo, vp, ak, av, bo, bp, x1, x3, x2, y1, y3, y2, ok, ov):
        after = masked_sum((x1, x3, x2), c[2], True) + masked_sum((y1, y3, y2), c[1], True)
        late = c[0].astype(F32)
        s_o = (after + bp[...].astype(F32) * (1.0 - late)).astype(BF)
        s_p = (after + bo[...].astype(F32) * late).astype(BF)
        for n, (k, v, s) in enumerate(((ko, vo, s_o), (kp, vp, s_p))):
            rows = slice(n * TOK, n * TOK + TOK)
            for h in range(4):
                sh = s[head(h), :]
                ok[rows, head(h)] = (ak[rows, head(h)] + dot(v[:, head(h)], sh, 1, 1)).astype(BF)
                ov[rows, head(h)] = (av[rows, head(h)] + dot(k[:, head(h)], sh)).astype(BF)

    return local(
        kernel,
        core,
        [k_o, k_p, v_o, v_p, dk, dv, back_o, back_p, *along_x, *along_y],
        [((2 * TOK, 512), BF)] * 2,
    )


def weight_grad(core, tt, jobs):
    n = len(jobs)

    def kernel(c, t, *refs):
        for m, (_, axis, step) in enumerate(jobs):
            g, out = refs[m], refs[n + m]
            if axis == "x":
                rows = t[:, (c[2] + step) % 4]
            elif axis == "y":
                rows = t[(c[1] + step) % 4]
            part = dot(rows.reshape(512, 2 * TOK), g[...]).astype(BF)
            for a in range(4):
                at = (a - c[1] + 4) % 4 if axis == "x" else (a - c[2] + 4) % 4
                for core_at in range(2):
                    for z in range(4):
                        row = a * 128 + core_at * 64 + z * 16
                        out[at, (z - c[3] + 4) % 4, core_at * 16 : core_at * 16 + 16, :] = part[
                            row : row + 16, :
                        ]

    return local(
        kernel,
        core,
        [tt.reshape(4, 4, 128, 2 * TOK)] + [g for g, _, _ in jobs],
        [((4, 4, 32, 512), BF)] * n,
    )


def weight_grad_all(core, tt, grad):
    def kernel(c, t, g, out):
        def at_y(y, carry):
            part = dot(t[y].reshape(512, 2 * TOK), g[...]).astype(BF)
            dy = (y - c[1] + 4) % 4
            for x in range(4):
                dx = (x - c[2] + 4) % 4
                for core_at in range(2):
                    for z in range(4):
                        row = x * 128 + core_at * 64 + z * 16
                        here = slice(core_at * 16, core_at * 16 + 16)
                        out[dx, dy, (z - c[3] + 4) % 4, here, :] = part[row : row + 16, :]
            return carry

        lax.fori_loop(0, 4, at_y, 0)

    return local(
        kernel,
        core,
        [tt.reshape(4, 4, 128, 2 * TOK), grad],
        [((4, 4, 4, 32, 512), BF)],
    )[0]


def joined_heads(core, own, received):
    def kernel(c, o, r, out, sems):
        copies = [
            pltpu.make_async_copy(o, out.at[:, half_of(c[0])], sems.at[0]),
            pltpu.make_async_copy(r, out.at[:, half_of(1 - c[0])], sems.at[1]),
        ]
        for copy in copies:
            copy.start()
        for copy in copies:
            copy.wait()

    return local(
        kernel,
        core,
        [own, received],
        [((TOK, 1024), BF)],
        hbm_out=1,
        scratch=[pltpu.SemaphoreType.DMA((2,))],
    )[0]


def assembled(core, summed, came):
    def kernel(c, qkv, r, *outs):
        scale = 65536.0**-0.5
        mine = pl.ds(pl.multiple_of(c[0] * 16, 16), 16)
        here = pl.ds(pl.multiple_of(c[0] * 512, 512), 512)
        there = pl.ds(pl.multiple_of((1 - c[0]) * 512, 512), 512)
        for m, out in enumerate(outs):
            out[:, here] = qkv[mine, m * 512 : m * 512 + 512].astype(F32) * scale
            out[:, there] = r[:, m * 512 : m * 512 + 512].astype(F32) * scale

    return local(kernel, core, [summed, came], [((16, 1024), F32)] * 3)


def input_part(core, slot, grads, weights, received=None):
    final = received is not None

    def kernel(c, *refs):
        rows = slice(slot * TOK, slot * TOK + TOK)
        out = refs[7] if final else refs[6]
        def columns(j, carry):
            at = pl.ds(pl.multiple_of(j * 512, 512), 512)
            total = dot(refs[0][rows, :], refs[3][at, :], 1, 1)
            total = total + dot(refs[1][rows, :], refs[4][at, :], 1, 1)
            total = total + dot(refs[2][rows, :], refs[5][at, :], 1, 1)
            if final:
                held, sems = refs[8:]
                held[:, at] = (total + refs[6][:, at].astype(F32)).astype(BF)
                pltpu.make_async_copy(held.at[:, at], out.at[:, at], sems.at[j]).start()
            else:
                out[:, at] = total.astype(BF)
            return carry

        lax.fori_loop(0, 4, columns, 0)
        if final:
            held, sems = refs[8:]
            for j in range(4):
                at = pl.ds(j * 512, 512)
                pltpu.make_async_copy(held.at[:, at], out.at[:, at], sems.at[j]).wait()

    return local(
        kernel,
        core,
        [*grads, *weights] + ([received] if final else []),
        [((TOK, 2048), BF)],
        hbm_out=1 if final else 0,
        scratch=[pltpu.VMEM((TOK, 2048), BF), pltpu.SemaphoreType.DMA((4,))] if final else [],
    )[0]


def shift(v, axis, d):
    n = lax.axis_size(axis)
    return lax.ppermute(v, axis, [(i, (i + d) % n) for i in range(n)])


def swap(v):
    return lax.ppermute(v, "c", [(0, 1), (1, 0)])


def pieces(v, axis):
    return [shift(v, axis, d) for d in (1, 3, 2)]


def together(*values):
    return lax.optimization_barrier(values)


def f32_sum(*parts):
    total = parts[0].astype(F32)
    for p in parts[1:]:
        total = total + p.astype(F32)
    return total.astype(BF)


def ring_out(far, axis):
    return shift(far[:2], axis, 1), shift(far[2:], axis, 3)


def ring_near(up, down, came, axis):
    from_left, from_right = came
    up = jnp.concatenate([f32_sum(up[:2], from_left), up[2:]], axis=0)
    down = jnp.concatenate([down[:2], f32_sum(down[2:], from_right)], axis=0)
    return shift(up, axis, 1), shift(down, axis, 3)


def spread(blocks, axis):
    return f32_sum(blocks[0], *[shift(blocks[d], axis, d) for d in (2, 1, 3)])


def per_device(tokens, w_query, w_key, w_value, cotangent):
    c = lax.axis_index("c")
    core = jnp.stack([lax.axis_index(a) for a in ("c", "y", "x", "z")]).astype(jnp.int32)
    tok_o = tokens[0]
    tok_p = swap(tok_o)
    late = c == 1

    k_o, v_o, state_o, w_k, w_v = project_own(core, tok_o, w_key, w_value)
    k_p, v_p, state_p, total, w_q = project_partner(core, tok_p, w_k, w_v, state_o, w_query)
    weights = (w_q, w_k, w_v)
    along_x = pieces(total, "x")
    q_o, q_p, intra, cot, cot_s = within(
        core, tok_o, tok_p, w_q, k_o, v_o, k_p, v_p, cotangent[0]
    )
    row, intra, q_o, q_p, tok_t, cot_s = together(
        f32_sum(total, *along_x), intra, q_o, q_p, tok_o, cot_s
    )
    along_y = pieces(row, "y")
    cot_p = swap(cot_s)
    tt = turned(core, tok_t, tok_p)
    *along_y, tt, cot_p = together(*along_y, tt, cot_p)
    a_o, a_p, g, p_o, p_p, back_o, back_p, total = normed(
        core, intra, q_o, q_p, state_o, state_p, along_x, along_y, cot, cot_p
    )
    along_x = pieces(total, "x")
    a_r = swap(a_p)
    dq = grad_q_of(core, k_o, k_p, v_o, v_p, g, p_o, p_p)
    part_q = weight_grad_all(core, tt, dq)
    row, part_q, g, a_r = together(f32_sum(total, *along_x), part_q, g, a_r)
    along_y = pieces(row, "y")
    came_q = ring_out(part_q[2], "x")
    dk, dv = grads_within(core, q_o, q_p, k_o, k_p, v_o, v_p, g)
    *along_y, dk, dv, c0, c1 = together(*along_y, dk, dv, *came_q)
    last_q = ring_near(part_q[1], part_q[3], (c0, c1), "x")
    dk, dv = grads_after(
        core, k_o, k_p, v_o, v_p, dk, dv, back_o, back_p, along_x, along_y
    )
    far_k, far_v = weight_grad(core, tt, [(dk, "x", 2), (dv, "y", 2)])
    far_k, far_v, dk, dv = together(far_k, far_v, dk, dv)
    came_k, came_v = ring_out(far_k, "x"), shift(far_v, "y", 1)
    near = weight_grad(core, tt, [(dk, "x", 1), (dk, "x", 3), (dv, "y", 1), (dv, "y", 3)])
    here_k, here_v = weight_grad(core, tt, [(dk, "x", 0), (dv, "y", 0)])
    attn_out = joined_heads(core, a_o, a_r)
    ig_p = input_part(core, 1, (dq, dk, dv), weights)
    *near, dk, dv, here_k, here_v, ig_p, attn_out, k0, k1, came_v, q0, q1 = together(
        *near, dk, dv, here_k, here_v, ig_p, attn_out, *came_k, came_v, *last_q
    )
    last_k = ring_near(near[0], near[1], (k0, k1), "x")
    sum_q = f32_sum(part_q[0], q0, q1)
    flat = (16, 32, 512)
    up = jnp.concatenate([f32_sum(near[2], came_v).reshape(flat), sum_q[2, :2]], axis=0)
    down = jnp.concatenate([near[3].reshape(flat), sum_q[2, 2:]], axis=0)
    last_v = [shift(up, "y", 1), shift(down, "y", 3)]
    ig_r = swap(ig_p)
    input_grad = input_part(core, 0, (dq, dk, dv), weights, ig_r)
    sum_q, input_grad, k0, k1, v0, v1 = together(sum_q, input_grad, *last_k, *last_v)
    sum_k = f32_sum(here_k, k0, k1)
    sum_v = f32_sum(here_v.reshape(flat), v0[:16], v1[:16]).reshape(4, 4, 32, 512)
    up_q = jnp.concatenate([f32_sum(sum_q[1, :2], v0[16:]), sum_q[1, 2:]], axis=0)
    down_q = jnp.concatenate([sum_q[3, :2], f32_sum(sum_q[3, 2:], v1[16:])], axis=0)
    up, down = jnp.stack([sum_k[1], up_q]), jnp.stack([sum_k[3], down_q])
    up, down, far = shift(up, "y", 1), shift(down, "y", 3), shift(sum_k[2], "y", 2)
    sum_v = spread(sum_v, "x")
    sum_k = f32_sum(sum_k[0], up[0], down[0], far)
    sum_q = f32_sum(sum_q[0], up[1], down[1])
    summed = spread(jnp.concatenate([sum_q, sum_k, sum_v], axis=-1), "z")
    came = swap(jnp.where(late, summed[:16], summed[16:]))
    return (attn_out[None], input_grad[None], *assembled(core, summed, came))


def solution(mesh):
    finer = Mesh(mesh.devices.reshape(4, 4, 2, mesh.shape["dp"]), ("y", "x", "c", "z"))
    return jax.shard_map(
        per_device,
        mesh=finer,
        in_specs=(P("z", CTX, None), P(), P(), P(), P("z", CTX, None)),
        out_specs=(
            P("z", CTX, None),
            P("z", CTX, None),
            P(CTX_DP, None),
            P(CTX_DP, None),
            P(CTX_DP, None),
        ),
        check_vma=False,
    )
```

```python
import jax
import jax.numpy as jnp
from jax import lax
from jax.experimental import pallas as pl
from jax.experimental.pallas import tpu as pltpu
from jax.sharding import Mesh
from jax.sharding import PartitionSpec as P

DH = 128
TOK = 512
EPS = 1e-05
CTX = ("y", "x", "c")
CTX_DP = ("y", "x", "c", "z")
BF = jnp.bfloat16
F32 = jnp.float32
MB = 1 << 20


def dot(a, b, ca=1, cb=0):
    return lax.dot_general(a, b, (((ca,), (cb,)), ((), ())), preferred_element_type=F32)


def causal(x, turned=False):
    rows = lax.broadcasted_iota(jnp.int32, x.shape, 0)
    cols = lax.broadcasted_iota(jnp.int32, x.shape, 1)
    keep = rows <= cols if turned else rows >= cols
    return jnp.where(keep, x, 0.0).astype(BF)


def head(h):
    if isinstance(h, int):
        return slice(h * DH, (h + 1) * DH)
    return pl.ds(pl.multiple_of(h * DH, DH), DH)


def each_head(body):
    for h in range(4):
        body(h)


def looped_head(body):
    def step(h, carry):
        body(h)
        return carry

    lax.fori_loop(0, 4, step, 0)


def call(kernel, core, grid, ins, outs, flops, moved, limit=20):
    return pl.pallas_call(
        kernel,
        out_shape=[jax.ShapeDtypeStruct(s, d) for s, d, _, _ in outs],
        grid_spec=pltpu.PrefetchScalarGridSpec(
            num_scalar_prefetch=1,
            grid=(grid,),
            in_specs=[pl.BlockSpec(b, m) for _, b, m in ins],
            out_specs=[pl.BlockSpec(b, m) for _, _, b, m in outs],
        ),
        compiler_params=pltpu.CompilerParams(
            dimension_semantics=("arbitrary",), vmem_limit_bytes=limit * MB
        ),
        cost_estimate=pl.CostEstimate(flops=flops, bytes_accessed=moved, transcendentals=0),
    )(core, *[a for a, _, _ in ins])


def local(kernel, core, ins, outs, hbm_in=0, hbm_out=0, scratch=()):
    vmem, hbm = pl.BlockSpec(memory_space=pltpu.VMEM), pl.BlockSpec(memory_space=pltpu.HBM)
    return pl.pallas_call(
        kernel,
        out_shape=[jax.ShapeDtypeStruct(s, d) for s, d in outs],
        in_specs=[pl.BlockSpec(memory_space=pltpu.SMEM)]
        + [vmem] * (len(ins) - hbm_in)
        + [hbm] * hbm_in,
        out_specs=[vmem] * (len(outs) - hbm_out) + [hbm] * hbm_out,
        scratch_shapes=list(scratch),
        compiler_params=pltpu.CompilerParams(vmem_limit_bytes=20 * MB),
        cost_estimate=pl.CostEstimate(flops=1000000, bytes_accessed=1000, transcendentals=0),
    )(core, *ins)


def whole(j, c):
    return (0, 0)


def tall(j, c):
    return (j, 0)


def wide(j, c):
    return (0, j)


def mine(j, c):
    return (0, c[0] * 2 + j)


def in_hbm(*arrays):
    return [pltpu.with_memory_space_constraint(t, pltpu.HBM) for t in arrays]


def half_of(which):
    return pl.ds(pl.multiple_of(which * 512, 512), 512)


def project_own(core, tok, wk, wv):
    def kernel(c, t, b, d, k, v, s, bh, dh, tv, sems):
        copies = [[], [], []]
        for i in range(4):
            rows, part = pl.ds(i * 512, 512), pl.ds(i * 128, 128)
            copies[0].append(pltpu.make_async_copy(t.at[part], tv.at[part], sems.at[0, i]))
            for n, (src, dst) in enumerate(((b, bh), (d, dh))):
                half = src.at[rows, half_of(c[0])]
                copies[n + 1].append(pltpu.make_async_copy(half, dst.at[rows], sems.at[n + 1, i]))
        for copy in sum(copies, []):
            copy.start()
        for copy in copies[0]:
            copy.wait()
        for n, (w, out) in enumerate(((bh, k), (dh, v))):
            for copy in copies[n + 1]:
                copy.wait()
            out[...] = dot(tv[...], w[...]).astype(BF)
        for h in range(4):
            s[head(h), :] = dot(k[:, head(h)], v[:, head(h)], 0, 0).astype(BF)

    row, weight = ((TOK, 512), BF), ((2048, 512), BF)
    return local(
        kernel,
        core,
        in_hbm(tok, wk, wv),
        [row] * 2 + [((512, DH), BF)] + [weight] * 2,
        hbm_in=3,
        scratch=[pltpu.VMEM((TOK, 2048), BF), pltpu.SemaphoreType.DMA((3, 4))],
    )


def project_partner(core, tok, wk, wv, state, wq):
    def kernel(c, t, b, d, so, a, k, v, s, total, ah, sem):
        copy = pltpu.make_async_copy(a.at[:, half_of(c[0])], ah, sem)
        copy.start()
        k[...] = dot(t[...], b[...]).astype(BF)
        v[...] = dot(t[...], d[...]).astype(BF)
        for h in range(4):
            st = dot(k[:, head(h)], v[:, head(h)], 0, 0).astype(BF)
            s[head(h), :] = st
            total[head(h), :] = (st.astype(F32) + so[head(h), :].astype(F32)).astype(BF)
        copy.wait()

    row = ((TOK, 512), BF)
    return local(
        kernel,
        core,
        [tok, wk, wv, state, *in_hbm(wq)],
        [row] * 2 + [((512, DH), BF)] * 2 + [((2048, 512), BF)],
        hbm_in=1,
        scratch=[pltpu.SemaphoreType.DMA],
    )


LOW = slice(0, 256)
HIGH = slice(256, 512)


def forward_pairs(q, k, v):
    s00 = causal(dot(q[LOW], k[LOW], 1, 1))
    s10 = dot(q[HIGH], k[LOW], 1, 1).astype(BF)
    s11 = causal(dot(q[HIGH], k[HIGH], 1, 1))
    return dot(s00, v[LOW]), dot(s10, v[LOW]) + dot(s11, v[HIGH])


def backward_pairs(q, k, x):
    s00 = causal(dot(k[LOW], q[LOW], 1, 1), True)
    s01 = dot(k[LOW], q[HIGH], 1, 1).astype(BF)
    s11 = causal(dot(k[HIGH], q[HIGH], 1, 1), True)
    return dot(s00, x[LOW]) + dot(s01, x[HIGH]), dot(s11, x[HIGH])


def masked_sum(refs, at, reverse):
    total = None
    for r, d in zip(refs, (1, 3, 2)):
        passed = at + (4 - d) < 4 if reverse else at >= d
        piece = r[...].astype(F32) * jnp.where(passed, 1.0, 0.0)
        total = piece if total is None else total + piece
    return total


def within(core, tok_o, tok_p, wq, k_o, v_o, k_p, v_p, cot):
    def kernel(c, to, tp, a, ko, vo, kp, vp, ct, qo, qp, out, mine_ct, other_ct, sems):
        copies = [
            pltpu.make_async_copy(ct.at[:, half_of(1 - c[0])], other_ct, sems.at[0]),
            pltpu.make_async_copy(ct.at[:, half_of(c[0])], mine_ct, sems.at[1]),
        ]
        for copy in copies:
            copy.start()
        qo[...] = dot(to[...], a[...]).astype(BF)
        qp[...] = dot(tp[...], a[...]).astype(BF)

        @each_head
        def _(h):
            for n, (q, k, v) in enumerate(((qo, ko, vo), (qp, kp, vp))):
                low, high = forward_pairs(q[:, head(h)], k[:, head(h)], v[:, head(h)])
                out[n * TOK : n * TOK + 256, head(h)] = low
                out[n * TOK + 256 : n * TOK + 512, head(h)] = high

        for copy in copies:
            copy.wait()

    return local(
        kernel,
        core,
        [tok_o, tok_p, wq, k_o, v_o, k_p, v_p, *in_hbm(cot)],
        [((TOK, 512), BF)] * 2 + [((2 * TOK, 512), F32)] + [((TOK, 512), BF)] * 2,
        hbm_in=1,
        scratch=[pltpu.SemaphoreType.DMA((2,))],
    )


def turned(core, tok_o, tok_p):
    def kernel(c, to, tp, out):
        out[:, :TOK] = to[...].T
        out[:, TOK:] = tp[...].T

    return call(
        kernel,
        core,
        4,
        [(tok_o, (TOK, 512), wide), (tok_p, (TOK, 512), wide)],
        [((2048, 2 * TOK), BF, (512, 2 * TOK), tall)],
        1000000,
        8 * MB,
    )[0]


def normed(core, intra, q_o, q_p, state_o, state_p, along_x, along_y, cot, cot_p):
    def kernel(c, it, qo, qp, so, sp, x1, x3, x2, y1, y3, y2, co, cp, *outs):
        ao, ap, g, po, pp, bo, bp, total = outs
        before = masked_sum((x1, x3, x2), c[2], False) + masked_sum((y1, y3, y2), c[1], False)
        late = c[0].astype(F32)
        po[...] = (before + sp[...].astype(F32) * late).astype(BF)
        pp[...] = (before + so[...].astype(F32) * (1.0 - late)).astype(BF)

        @each_head
        def _(h):
            backs = []
            for n, (q, p, a, b) in enumerate(((qo, po, ao, bo), (qp, pp, ap, bp))):
                rows = slice(n * TOK, n * TOK + TOK)
                qh = q[:, head(h)]
                mixed = it[rows, head(h)] + dot(qh, p[head(h), :])
                inverse = lax.rsqrt(jnp.mean(mixed * mixed, axis=-1, keepdims=True) + EPS)
                nm = mixed * inverse
                up = (co if n == 0 else cp)[:, head(h)].astype(F32)
                a[:, head(h)] = nm.astype(BF)
                gm = ((up - nm * jnp.mean(up * nm, axis=-1, keepdims=True)) * inverse).astype(BF)
                g[rows, head(h)] = gm
                back = dot(qh, gm, 0, 0).astype(BF)
                b[head(h), :] = back
                backs.append(back.astype(F32))
            total[head(h), :] = (backs[0] + backs[1]).astype(BF)

    state = ((512, DH), BF)
    return local(
        kernel,
        core,
        [intra, q_o, q_p, state_o, state_p, *along_x, *along_y, cot, cot_p],
        [((TOK, 512), BF)] * 2 + [((2 * TOK, 512), BF)] + [state] * 5,
    )


def grad_q_of(core, k_o, k_p, v_o, v_p, g, p_o, p_p):
    def kernel(c, ko, kp, vo, vp, gr, po, pp, dq):
        @each_head
        def _(h):
            for n, (k, v, p) in enumerate(((ko, vo, po), (kp, vp, pp))):
                gh = gr[n * TOK : n * TOK + TOK, head(h)]
                past = dot(gh, p[head(h), :], 1, 1)
                low, high = forward_pairs(gh, v[:, head(h)], k[:, head(h)])
                dq[n * TOK : n * TOK + 256, head(h)] = (low + past[LOW]).astype(BF)
                dq[n * TOK + 256 : n * TOK + 512, head(h)] = (high + past[HIGH]).astype(BF)

    return local(
        kernel,
        core,
        [k_o, k_p, v_o, v_p, g, p_o, p_p],
        [((2 * TOK, 512), BF)],
    )[0]


def grads_within(core, q_o, q_p, k_o, k_p, v_o, v_p, g):
    def kernel(c, qo, qp, ko, kp, vo, vp, gr, dk, dv):
        @looped_head
        def _(h):
            for n, (q, k, v) in enumerate(((qo, ko, vo), (qp, kp, vp))):
                qh, kh, vh = q[:, head(h)], k[:, head(h)], v[:, head(h)]
                gh = gr[n * TOK : n * TOK + TOK, head(h)]
                for left, right, x, out in ((gh, vh, qh, dk), (qh, kh, gh, dv)):
                    low, high = backward_pairs(left, right, x)
                    out[n * TOK : n * TOK + 256, head(h)] = low
                    out[n * TOK + 256 : n * TOK + 512, head(h)] = high

    return local(
        kernel,
        core,
        [q_o, q_p, k_o, k_p, v_o, v_p, g],
        [((2 * TOK, 512), F32)] * 2,
    )


def grads_after(core, k_o, k_p, v_o, v_p, dk, dv, back_o, back_p, along_x, along_y):
    def kernel(c, ko, kp, vo, vp, ak, av, bo, bp, x1, x3, x2, y1, y3, y2, ok, ov):
        after = masked_sum((x1, x3, x2), c[2], True) + masked_sum((y1, y3, y2), c[1], True)
        late = c[0].astype(F32)
        s_o = (after + bp[...].astype(F32) * (1.0 - late)).astype(BF)
        s_p = (after + bo[...].astype(F32) * late).astype(BF)
        for n, (k, v, s) in enumerate(((ko, vo, s_o), (kp, vp, s_p))):
            rows = slice(n * TOK, n * TOK + TOK)
            for h in range(4):
                sh = s[head(h), :]
                ok[rows, head(h)] = (ak[rows, head(h)] + dot(v[:, head(h)], sh, 1, 1)).astype(BF)
                ov[rows, head(h)] = (av[rows, head(h)] + dot(k[:, head(h)], sh)).astype(BF)

    return local(
        kernel,
        core,
        [k_o, k_p, v_o, v_p, dk, dv, back_o, back_p, *along_x, *along_y],
        [((2 * TOK, 512), BF)] * 2,
    )


def weight_grad(core, tt, jobs):
    n = len(jobs)

    def kernel(c, t, *refs):
        for m, (_, axis, step) in enumerate(jobs):
            g, out = refs[m], refs[n + m]
            if axis == "x":
                rows = t[:, (c[2] + step) % 4]
            elif axis == "y":
                rows = t[(c[1] + step) % 4]
            part = dot(rows.reshape(512, 2 * TOK), g[...]).astype(BF)
            for a in range(4):
                near = (a - c[1] + 4) % 4 if axis == "x" else (a - c[2] + 4) % 4
                for core_at in range(2):
                    for z in range(4):
                        row = a * 128 + core_at * 64 + z * 16
                        here = slice(core_at * 16, core_at * 16 + 16)
                        out[near, (z - c[3] + 4) % 4, here, :] = part[row : row + 16, :]

    return local(
        kernel,
        core,
        [tt.reshape(4, 4, 128, 2 * TOK)] + [g for g, _, _ in jobs],
        [((4, 4, 32, 512), BF)] * n,
    )


def weight_grad_all(core, tt, grad):
    def kernel(c, t, g, out):
        def at_y(y, carry):
            part = dot(t[y].reshape(512, 2 * TOK), g[...]).astype(BF)
            dy = (y - c[1] + 4) % 4
            for x in range(4):
                dx = (x - c[2] + 4) % 4
                for core_at in range(2):
                    for z in range(4):
                        row = x * 128 + core_at * 64 + z * 16
                        here = slice(core_at * 16, core_at * 16 + 16)
                        out[dx, dy, (z - c[3] + 4) % 4, here, :] = part[row : row + 16, :]
            return carry

        lax.fori_loop(0, 4, at_y, 0)

    return local(
        kernel,
        core,
        [tt.reshape(4, 4, 128, 2 * TOK), grad],
        [((4, 4, 4, 32, 512), BF)],
    )[0]


def joined_heads(core, own, received):
    def kernel(c, o, r, out, sems):
        copies = [
            pltpu.make_async_copy(o, out.at[:, half_of(c[0])], sems.at[0]),
            pltpu.make_async_copy(r, out.at[:, half_of(1 - c[0])], sems.at[1]),
        ]
        for copy in copies:
            copy.start()
        for copy in copies:
            copy.wait()

    return local(
        kernel,
        core,
        [own, received],
        [((TOK, 1024), BF)],
        hbm_out=1,
        scratch=[pltpu.SemaphoreType.DMA((2,))],
    )[0]


def assembled(core, summed, came):
    def kernel(c, qkv, r, *outs):
        scale = 65536.0**-0.5
        mine = pl.ds(pl.multiple_of(c[0] * 16, 16), 16)
        here = pl.ds(pl.multiple_of(c[0] * 512, 512), 512)
        there = pl.ds(pl.multiple_of((1 - c[0]) * 512, 512), 512)
        for m, out in enumerate(outs):
            out[:, here] = qkv[mine, m * 512 : m * 512 + 512].astype(F32) * scale
            out[:, there] = r[:, m * 512 : m * 512 + 512].astype(F32) * scale

    return local(kernel, core, [summed, came], [((16, 1024), F32)] * 3)


def input_part(core, slot, grads, weights, received=None):
    final = received is not None

    def kernel(c, *refs):
        rows = slice(slot * TOK, slot * TOK + TOK)
        out = refs[7] if final else refs[6]
        def columns(j, carry):
            at = pl.ds(pl.multiple_of(j * 512, 512), 512)
            total = dot(refs[0][rows, :], refs[3][at, :], 1, 1)
            total = total + dot(refs[1][rows, :], refs[4][at, :], 1, 1)
            total = total + dot(refs[2][rows, :], refs[5][at, :], 1, 1)
            if final:
                held, sems = refs[8:]
                held[:, at] = (total + refs[6][:, at].astype(F32)).astype(BF)
                pltpu.make_async_copy(held.at[:, at], out.at[:, at], sems.at[j]).start()
            else:
                out[:, at] = total.astype(BF)
            return carry

        lax.fori_loop(0, 4, columns, 0)
        if final:
            held, sems = refs[8:]
            for j in range(4):
                at = pl.ds(j * 512, 512)
                pltpu.make_async_copy(held.at[:, at], out.at[:, at], sems.at[j]).wait()

    return local(
        kernel,
        core,
        [*grads, *weights] + ([received] if final else []),
        [((TOK, 2048), BF)],
        hbm_out=1 if final else 0,
        scratch=[pltpu.VMEM((TOK, 2048), BF), pltpu.SemaphoreType.DMA((4,))] if final else [],
    )[0]


def shift(v, axis, d):
    n = lax.axis_size(axis)
    return lax.ppermute(v, axis, [(i, (i + d) % n) for i in range(n)])


def swap(v):
    return lax.ppermute(v, "c", [(0, 1), (1, 0)])


def pieces(v, axis):
    return [shift(v, axis, d) for d in (1, 3, 2)]


def together(*values):
    return lax.optimization_barrier(values)


def f32_sum(*parts):
    total = parts[0].astype(F32)
    for p in parts[1:]:
        total = total + p.astype(F32)
    return total.astype(BF)


def ring_out(far, axis):
    return shift(far[:2], axis, 1), shift(far[2:], axis, 3)


def ring_near(up, down, came, axis):
    from_left, from_right = came
    up = jnp.concatenate([f32_sum(up[:2], from_left), up[2:]], axis=0)
    down = jnp.concatenate([down[:2], f32_sum(down[2:], from_right)], axis=0)
    return shift(up, axis, 1), shift(down, axis, 3)


def spread(blocks, axis):
    return f32_sum(blocks[0], *[shift(blocks[d], axis, d) for d in (2, 1, 3)])


def per_device(tokens, w_query, w_key, w_value, cotangent):
    c = lax.axis_index("c")
    core = jnp.stack([lax.axis_index(a) for a in ("c", "y", "x", "z")]).astype(jnp.int32)
    tok_o = tokens[0]
    tok_p = swap(tok_o)
    late = c == 1

    k_o, v_o, state_o, w_k, w_v = project_own(core, tok_o, w_key, w_value)
    k_p, v_p, state_p, total, w_q = project_partner(core, tok_p, w_k, w_v, state_o, w_query)
    weights = (w_q, w_k, w_v)
    along_x = pieces(total, "x")
    q_o, q_p, intra, cot, cot_s = within(
        core, tok_o, tok_p, w_q, k_o, v_o, k_p, v_p, cotangent[0]
    )
    row, intra, q_o, q_p, tok_t, cot_s = together(
        f32_sum(total, *along_x), intra, q_o, q_p, tok_o, cot_s
    )
    along_y = pieces(row, "y")
    cot_p = swap(cot_s)
    tt = turned(core, tok_t, tok_p)
    *along_y, tt, cot_p = together(*along_y, tt, cot_p)
    a_o, a_p, g, p_o, p_p, back_o, back_p, total = normed(
        core, intra, q_o, q_p, state_o, state_p, along_x, along_y, cot, cot_p
    )
    along_x = pieces(total, "x")
    a_r = swap(a_p)
    dq = grad_q_of(core, k_o, k_p, v_o, v_p, g, p_o, p_p)
    part_q = weight_grad_all(core, tt, dq)
    row, part_q, g, a_r = together(f32_sum(total, *along_x), part_q, g, a_r)
    along_y = pieces(row, "y")
    came_q = ring_out(part_q[2], "x")
    dk, dv = grads_within(core, q_o, q_p, k_o, k_p, v_o, v_p, g)
    *along_y, dk, dv, c0, c1 = together(*along_y, dk, dv, *came_q)
    last_q = ring_near(part_q[1], part_q[3], (c0, c1), "x")
    dk, dv = grads_after(
        core, k_o, k_p, v_o, v_p, dk, dv, back_o, back_p, along_x, along_y
    )
    far_k, far_v = weight_grad(core, tt, [(dk, "x", 2), (dv, "y", 2)])
    far_k, far_v, dk, dv = together(far_k, far_v, dk, dv)
    came_k, came_v = ring_out(far_k, "x"), shift(far_v, "y", 1)
    near = weight_grad(core, tt, [(dk, "x", 1), (dk, "x", 3), (dv, "y", 1), (dv, "y", 3)])
    here_k, here_v = weight_grad(core, tt, [(dk, "x", 0), (dv, "y", 0)])
    ig_p = input_part(core, 1, (dq, dk, dv), weights)
    *near, dk, dv, here_k, here_v, ig_p, a_o, k0, k1, came_v, q0, q1 = together(
        *near, dk, dv, here_k, here_v, ig_p, a_o, *came_k, came_v, *last_q
    )
    last_k = ring_near(near[0], near[1], (k0, k1), "x")
    sum_q = f32_sum(part_q[0], q0, q1)
    flat = (16, 32, 512)
    up = jnp.concatenate([f32_sum(near[2], came_v).reshape(flat), sum_q[2, :2]], axis=0)
    down = jnp.concatenate([near[3].reshape(flat), sum_q[2, 2:]], axis=0)
    last_v = [shift(up, "y", 1), shift(down, "y", 3)]
    ig_r = swap(ig_p)
    attn_out = joined_heads(core, a_o, a_r)
    input_grad = input_part(core, 0, (dq, dk, dv), weights, ig_r)
    sum_q, input_grad, attn_out, k0, k1, v0, v1 = together(
        sum_q, input_grad, attn_out, *last_k, *last_v
    )
    sum_k = f32_sum(here_k, k0, k1)
    sum_v = f32_sum(here_v.reshape(flat), v0[:16], v1[:16]).reshape(4, 4, 32, 512)
    up_q = jnp.concatenate([f32_sum(sum_q[1, :2], v0[16:]), sum_q[1, 2:]], axis=0)
    down_q = jnp.concatenate([sum_q[3, :2], f32_sum(sum_q[3, 2:], v1[16:])], axis=0)
    up, down = jnp.stack([sum_k[1], up_q]), jnp.stack([sum_k[3], down_q])
    up, down, far = shift(up, "y", 1), shift(down, "y", 3), shift(sum_k[2], "y", 2)
    sum_v = spread(sum_v, "x")
    sum_k = f32_sum(sum_k[0], up[0], down[0], far)
    sum_q = f32_sum(sum_q[0], up[1], down[1])
    summed = spread(jnp.concatenate([sum_q, sum_k, sum_v], axis=-1), "z")
    came = swap(jnp.where(late, summed[:16], summed[16:]))
    return (attn_out[None], input_grad[None], *assembled(core, summed, came))


def solution(mesh):
    finer = Mesh(mesh.devices.reshape(4, 4, 2, mesh.shape["dp"]), ("y", "x", "c", "z"))
    return jax.shard_map(
        per_device,
        mesh=finer,
        in_specs=(P("z", CTX, None), P(), P(), P(), P("z", CTX, None)),
        out_specs=(
            P("z", CTX, None),
            P("z", CTX, None),
            P(CTX_DP, None),
            P(CTX_DP, None),
            P(CTX_DP, None),
        ),
        check_vma=False,
    )
```

```python
import jax
import jax.numpy as jnp
from jax import lax
from jax.experimental import pallas as pl
from jax.experimental.pallas import tpu as pltpu
from jax.sharding import Mesh
from jax.sharding import PartitionSpec as P

DH = 128
TOK = 512
EPS = 1e-05
CTX = ("y", "x", "c")
CTX_DP = ("y", "x", "c", "z")
BF = jnp.bfloat16
F32 = jnp.float32
MB = 1 << 20


def dot(a, b, ca=1, cb=0):
    return lax.dot_general(a, b, (((ca,), (cb,)), ((), ())), preferred_element_type=F32)


def causal(x, turned=False):
    rows = lax.broadcasted_iota(jnp.int32, x.shape, 0)
    cols = lax.broadcasted_iota(jnp.int32, x.shape, 1)
    keep = rows <= cols if turned else rows >= cols
    return jnp.where(keep, x, 0.0).astype(BF)


def head(h):
    if isinstance(h, int):
        return slice(h * DH, (h + 1) * DH)
    return pl.ds(pl.multiple_of(h * DH, DH), DH)


def each_head(body):
    for h in range(4):
        body(h)


def looped_head(body):
    def step(h, carry):
        body(h)
        return carry

    lax.fori_loop(0, 4, step, 0)


def call(kernel, core, grid, ins, outs, flops, moved, limit=20):
    return pl.pallas_call(
        kernel,
        out_shape=[jax.ShapeDtypeStruct(s, d) for s, d, _, _ in outs],
        grid_spec=pltpu.PrefetchScalarGridSpec(
            num_scalar_prefetch=1,
            grid=(grid,),
            in_specs=[pl.BlockSpec(b, m) for _, b, m in ins],
            out_specs=[pl.BlockSpec(b, m) for _, _, b, m in outs],
        ),
        compiler_params=pltpu.CompilerParams(
            dimension_semantics=("arbitrary",), vmem_limit_bytes=limit * MB
        ),
        cost_estimate=pl.CostEstimate(flops=flops, bytes_accessed=moved, transcendentals=0),
    )(core, *[a for a, _, _ in ins])


def local(kernel, core, ins, outs, hbm_in=0, hbm_out=0, scratch=()):
    vmem, hbm = pl.BlockSpec(memory_space=pltpu.VMEM), pl.BlockSpec(memory_space=pltpu.HBM)
    return pl.pallas_call(
        kernel,
        out_shape=[jax.ShapeDtypeStruct(s, d) for s, d in outs],
        in_specs=[pl.BlockSpec(memory_space=pltpu.SMEM)]
        + [vmem] * (len(ins) - hbm_in)
        + [hbm] * hbm_in,
        out_specs=[vmem] * (len(outs) - hbm_out) + [hbm] * hbm_out,
        scratch_shapes=list(scratch),
        compiler_params=pltpu.CompilerParams(vmem_limit_bytes=20 * MB),
        cost_estimate=pl.CostEstimate(flops=1000000, bytes_accessed=1000, transcendentals=0),
    )(core, *ins)


def whole(j, c):
    return (0, 0)


def tall(j, c):
    return (j, 0)


def wide(j, c):
    return (0, j)


def mine(j, c):
    return (0, c[0] * 2 + j)


def in_hbm(*arrays):
    return [pltpu.with_memory_space_constraint(t, pltpu.HBM) for t in arrays]


def half_of(which):
    return pl.ds(pl.multiple_of(which * 512, 512), 512)


def project_own(core, tok, wk, wv):
    def kernel(c, t, b, d, k, v, s, bh, dh, tv, sems):
        copies = [[], [], []]
        for i in range(4):
            rows, part = pl.ds(i * 512, 512), pl.ds(i * 128, 128)
            copies[0].append(pltpu.make_async_copy(t.at[part], tv.at[part], sems.at[0, i]))
            for n, (src, dst) in enumerate(((b, bh), (d, dh))):
                half = src.at[rows, half_of(c[0])]
                copies[n + 1].append(pltpu.make_async_copy(half, dst.at[rows], sems.at[n + 1, i]))
        for copy in sum(copies, []):
            copy.start()
        for copy in copies[0]:
            copy.wait()
        for n, (w, out) in enumerate(((bh, k), (dh, v))):
            for copy in copies[n + 1]:
                copy.wait()
            out[...] = dot(tv[...], w[...]).astype(BF)
        for h in range(4):
            s[head(h), :] = dot(k[:, head(h)], v[:, head(h)], 0, 0).astype(BF)

    row, weight = ((TOK, 512), BF), ((2048, 512), BF)
    return local(
        kernel,
        core,
        in_hbm(tok, wk, wv),
        [row] * 2 + [((512, DH), BF)] + [weight] * 2,
        hbm_in=3,
        scratch=[pltpu.VMEM((TOK, 2048), BF), pltpu.SemaphoreType.DMA((3, 4))],
    )


def project_partner(core, tok, wk, wv, state, wq):
    def kernel(c, t, b, d, so, a, k, v, s, total, ah, sem):
        copy = pltpu.make_async_copy(a.at[:, half_of(c[0])], ah, sem)
        copy.start()
        k[...] = dot(t[...], b[...]).astype(BF)
        v[...] = dot(t[...], d[...]).astype(BF)
        for h in range(4):
            st = dot(k[:, head(h)], v[:, head(h)], 0, 0).astype(BF)
            s[head(h), :] = st
            total[head(h), :] = (st.astype(F32) + so[head(h), :].astype(F32)).astype(BF)
        copy.wait()

    row = ((TOK, 512), BF)
    return local(
        kernel,
        core,
        [tok, wk, wv, state, *in_hbm(wq)],
        [row] * 2 + [((512, DH), BF)] * 2 + [((2048, 512), BF)],
        hbm_in=1,
        scratch=[pltpu.SemaphoreType.DMA],
    )


LOW = slice(0, 256)
HIGH = slice(256, 512)


def forward_pairs(q, k, v):
    s00 = causal(dot(q[LOW], k[LOW], 1, 1))
    s10 = dot(q[HIGH], k[LOW], 1, 1).astype(BF)
    s11 = causal(dot(q[HIGH], k[HIGH], 1, 1))
    return dot(s00, v[LOW]), dot(s10, v[LOW]) + dot(s11, v[HIGH])


def backward_pairs(q, k, x):
    s00 = causal(dot(k[LOW], q[LOW], 1, 1), True)
    s01 = dot(k[LOW], q[HIGH], 1, 1).astype(BF)
    s11 = causal(dot(k[HIGH], q[HIGH], 1, 1), True)
    return dot(s00, x[LOW]) + dot(s01, x[HIGH]), dot(s11, x[HIGH])


def masked_sum(refs, at, reverse):
    total = None
    for r, d in zip(refs, (1, 3, 2)):
        passed = at + (4 - d) < 4 if reverse else at >= d
        piece = r[...].astype(F32) * jnp.where(passed, 1.0, 0.0)
        total = piece if total is None else total + piece
    return total


def within(core, tok, wq, k, v, cot=None):
    fetch = cot is not None

    def kernel(c, t, a, ko, vo, *refs):
        copies = []
        if fetch:
            ct, qo, out, mine_ct, other_ct, sems = refs
            copies = [
                pltpu.make_async_copy(ct.at[:, half_of(1 - c[0])], other_ct, sems.at[0]),
                pltpu.make_async_copy(ct.at[:, half_of(c[0])], mine_ct, sems.at[1]),
            ]
        else:
            qo, out = refs
        for copy in copies:
            copy.start()
        qo[...] = dot(t[...], a[...]).astype(BF)

        @looped_head
        def _(h):
            low, high = forward_pairs(qo[:, head(h)], ko[:, head(h)], vo[:, head(h)])
            out[:256, head(h)] = low
            out[256:, head(h)] = high

        for copy in copies:
            copy.wait()

    row = ((TOK, 512), BF)
    return local(
        kernel,
        core,
        [tok, wq, k, v] + (in_hbm(cot) if fetch else []),
        [row, ((TOK, 512), F32)] + [row] * (2 if fetch else 0),
        hbm_in=1 if fetch else 0,
        scratch=[pltpu.SemaphoreType.DMA((2,))] if fetch else [],
    )


def turned(core, tok_o, tok_p):
    def kernel(c, to, tp, out):
        out[:, :TOK] = to[...].T
        out[:, TOK:] = tp[...].T

    return call(
        kernel,
        core,
        4,
        [(tok_o, (TOK, 512), wide), (tok_p, (TOK, 512), wide)],
        [((2048, 2 * TOK), BF, (512, 2 * TOK), tall)],
        1000000,
        8 * MB,
    )[0]


def normed(core, i_o, i_p, q_o, q_p, state_o, state_p, along_x, along_y, cot, cot_p):
    def kernel(c, io, ip, qo, qp, so, sp, x1, x3, x2, y1, y3, y2, co, cp, *outs):
        ao, ap, g, po, pp, bo, bp, total = outs
        before = masked_sum((x1, x3, x2), c[2], False) + masked_sum((y1, y3, y2), c[1], False)
        late = c[0].astype(F32)
        po[...] = (before + sp[...].astype(F32) * late).astype(BF)
        pp[...] = (before + so[...].astype(F32) * (1.0 - late)).astype(BF)

        @each_head
        def _(h):
            backs = []
            for n, (it, q, p, a, b) in enumerate(((io, qo, po, ao, bo), (ip, qp, pp, ap, bp))):
                rows = slice(n * TOK, n * TOK + TOK)
                qh = q[:, head(h)]
                mixed = it[:, head(h)] + dot(qh, p[head(h), :])
                inverse = lax.rsqrt(jnp.mean(mixed * mixed, axis=-1, keepdims=True) + EPS)
                nm = mixed * inverse
                up = (co if n == 0 else cp)[:, head(h)].astype(F32)
                a[:, head(h)] = nm.astype(BF)
                gm = ((up - nm * jnp.mean(up * nm, axis=-1, keepdims=True)) * inverse).astype(BF)
                g[rows, head(h)] = gm
                back = dot(qh, gm, 0, 0).astype(BF)
                b[head(h), :] = back
                backs.append(back.astype(F32))
            total[head(h), :] = (backs[0] + backs[1]).astype(BF)

    state = ((512, DH), BF)
    return local(
        kernel,
        core,
        [i_o, i_p, q_o, q_p, state_o, state_p, *along_x, *along_y, cot, cot_p],
        [((TOK, 512), BF)] * 2 + [((2 * TOK, 512), BF)] + [state] * 5,
    )


def grad_q_of(core, k_o, k_p, v_o, v_p, g, p_o, p_p):
    def kernel(c, ko, kp, vo, vp, gr, po, pp, dq):
        @each_head
        def _(h):
            for n, (k, v, p) in enumerate(((ko, vo, po), (kp, vp, pp))):
                gh = gr[n * TOK : n * TOK + TOK, head(h)]
                past = dot(gh, p[head(h), :], 1, 1)
                low, high = forward_pairs(gh, v[:, head(h)], k[:, head(h)])
                dq[n * TOK : n * TOK + 256, head(h)] = (low + past[LOW]).astype(BF)
                dq[n * TOK + 256 : n * TOK + 512, head(h)] = (high + past[HIGH]).astype(BF)

    return local(
        kernel,
        core,
        [k_o, k_p, v_o, v_p, g, p_o, p_p],
        [((2 * TOK, 512), BF)],
    )[0]


def grads_within(core, q_o, q_p, k_o, k_p, v_o, v_p, g):
    def kernel(c, qo, qp, ko, kp, vo, vp, gr, dk, dv):
        @each_head
        def _(h):
            for n, (q, k, v) in enumerate(((qo, ko, vo), (qp, kp, vp))):
                qh, kh, vh = q[:, head(h)], k[:, head(h)], v[:, head(h)]
                gh = gr[n * TOK : n * TOK + TOK, head(h)]
                for left, right, x, out in ((gh, vh, qh, dk), (qh, kh, gh, dv)):
                    low, high = backward_pairs(left, right, x)
                    out[n * TOK : n * TOK + 256, head(h)] = low
                    out[n * TOK + 256 : n * TOK + 512, head(h)] = high

    return local(
        kernel,
        core,
        [q_o, q_p, k_o, k_p, v_o, v_p, g],
        [((2 * TOK, 512), F32)] * 2,
    )


def grads_after(core, k_o, k_p, v_o, v_p, dk, dv, back_o, back_p, along_x, along_y):
    def kernel(c, ko, kp, vo, vp, ak, av, bo, bp, x1, x3, x2, y1, y3, y2, ok, ov):
        after = masked_sum((x1, x3, x2), c[2], True) + masked_sum((y1, y3, y2), c[1], True)
        late = c[0].astype(F32)
        s_o = (after + bp[...].astype(F32) * (1.0 - late)).astype(BF)
        s_p = (after + bo[...].astype(F32) * late).astype(BF)
        for n, (k, v, s) in enumerate(((ko, vo, s_o), (kp, vp, s_p))):
            rows = slice(n * TOK, n * TOK + TOK)
            for h in range(4):
                sh = s[head(h), :]
                ok[rows, head(h)] = (ak[rows, head(h)] + dot(v[:, head(h)], sh, 1, 1)).astype(BF)
                ov[rows, head(h)] = (av[rows, head(h)] + dot(k[:, head(h)], sh)).astype(BF)

    return local(
        kernel,
        core,
        [k_o, k_p, v_o, v_p, dk, dv, back_o, back_p, *along_x, *along_y],
        [((2 * TOK, 512), BF)] * 2,
    )


def weight_grad(core, tt, jobs):
    n = len(jobs)

    def kernel(c, t, *refs):
        for m, (_, axis, step) in enumerate(jobs):
            g, out = refs[m], refs[n + m]
            if axis == "x":
                rows = t[:, (c[2] + step) % 4]
            elif axis == "y":
                rows = t[(c[1] + step) % 4]
            part = dot(rows.reshape(512, 2 * TOK), g[...]).astype(BF)
            for a in range(4):
                near = (a - c[1] + 4) % 4 if axis == "x" else (a - c[2] + 4) % 4
                for core_at in range(2):
                    for z in range(4):
                        row = a * 128 + core_at * 64 + z * 16
                        here = slice(core_at * 16, core_at * 16 + 16)
                        out[near, (z - c[3] + 4) % 4, here, :] = part[row : row + 16, :]

    return local(
        kernel,
        core,
        [tt.reshape(4, 4, 128, 2 * TOK)] + [g for g, _, _ in jobs],
        [((4, 4, 32, 512), BF)] * n,
    )


def weight_grad_all(core, tt, grad):
    def kernel(c, t, g, out):
        def at_y(y, carry):
            part = dot(t[y].reshape(512, 2 * TOK), g[...]).astype(BF)
            dy = (y - c[1] + 4) % 4
            for x in range(4):
                dx = (x - c[2] + 4) % 4
                for core_at in range(2):
                    for z in range(4):
                        row = x * 128 + core_at * 64 + z * 16
                        here = slice(core_at * 16, core_at * 16 + 16)
                        out[dx, dy, (z - c[3] + 4) % 4, here, :] = part[row : row + 16, :]
            return carry

        lax.fori_loop(0, 4, at_y, 0)

    return local(
        kernel,
        core,
        [tt.reshape(4, 4, 128, 2 * TOK), grad],
        [((4, 4, 4, 32, 512), BF)],
    )[0]


def joined_heads(core, own, received):
    def kernel(c, o, r, out, sems):
        copies = [
            pltpu.make_async_copy(o, out.at[:, half_of(c[0])], sems.at[0]),
            pltpu.make_async_copy(r, out.at[:, half_of(1 - c[0])], sems.at[1]),
        ]
        for copy in copies:
            copy.start()
        for copy in copies:
            copy.wait()

    return local(
        kernel,
        core,
        [own, received],
        [((TOK, 1024), BF)],
        hbm_out=1,
        scratch=[pltpu.SemaphoreType.DMA((2,))],
    )[0]


def assembled(core, summed, came):
    def kernel(c, qkv, r, *outs):
        scale = 65536.0**-0.5
        mine = pl.ds(pl.multiple_of(c[0] * 16, 16), 16)
        here = pl.ds(pl.multiple_of(c[0] * 512, 512), 512)
        there = pl.ds(pl.multiple_of((1 - c[0]) * 512, 512), 512)
        for m, out in enumerate(outs):
            out[:, here] = qkv[mine, m * 512 : m * 512 + 512].astype(F32) * scale
            out[:, there] = r[:, m * 512 : m * 512 + 512].astype(F32) * scale

    return local(kernel, core, [summed, came], [((16, 1024), F32)] * 3)


def input_part(core, slot, grads, weights, received=None):
    final = received is not None

    def kernel(c, *refs):
        rows = slice(slot * TOK, slot * TOK + TOK)
        out = refs[7] if final else refs[6]
        def columns(j, carry):
            at = pl.ds(pl.multiple_of(j * 512, 512), 512)
            total = dot(refs[0][rows, :], refs[3][at, :], 1, 1)
            total = total + dot(refs[1][rows, :], refs[4][at, :], 1, 1)
            total = total + dot(refs[2][rows, :], refs[5][at, :], 1, 1)
            if final:
                held, sems = refs[8:]
                held[:, at] = (total + refs[6][:, at].astype(F32)).astype(BF)
                pltpu.make_async_copy(held.at[:, at], out.at[:, at], sems.at[j]).start()
            else:
                out[:, at] = total.astype(BF)
            return carry

        lax.fori_loop(0, 4, columns, 0)
        if final:
            held, sems = refs[8:]
            for j in range(4):
                at = pl.ds(j * 512, 512)
                pltpu.make_async_copy(held.at[:, at], out.at[:, at], sems.at[j]).wait()

    return local(
        kernel,
        core,
        [*grads, *weights] + ([received] if final else []),
        [((TOK, 2048), BF)],
        hbm_out=1 if final else 0,
        scratch=[pltpu.VMEM((TOK, 2048), BF), pltpu.SemaphoreType.DMA((4,))] if final else [],
    )[0]


def shift(v, axis, d):
    n = lax.axis_size(axis)
    return lax.ppermute(v, axis, [(i, (i + d) % n) for i in range(n)])


def swap(v):
    return lax.ppermute(v, "c", [(0, 1), (1, 0)])


def pieces(v, axis):
    return [shift(v, axis, d) for d in (1, 3, 2)]


def together(*values):
    return lax.optimization_barrier(values)


def f32_sum(*parts):
    total = parts[0].astype(F32)
    for p in parts[1:]:
        total = total + p.astype(F32)
    return total.astype(BF)


def ring_out(far, axis):
    return shift(far[:2], axis, 1), shift(far[2:], axis, 3)


def ring_near(up, down, came, axis):
    from_left, from_right = came
    up = jnp.concatenate([f32_sum(up[:2], from_left), up[2:]], axis=0)
    down = jnp.concatenate([down[:2], f32_sum(down[2:], from_right)], axis=0)
    return shift(up, axis, 1), shift(down, axis, 3)


def spread(blocks, axis):
    return f32_sum(blocks[0], *[shift(blocks[d], axis, d) for d in (2, 1, 3)])


def per_device(tokens, w_query, w_key, w_value, cotangent):
    c = lax.axis_index("c")
    core = jnp.stack([lax.axis_index(a) for a in ("c", "y", "x", "z")]).astype(jnp.int32)
    tok_o = tokens[0]
    tok_p = swap(tok_o)
    late = c == 1

    k_o, v_o, state_o, w_k, w_v = project_own(core, tok_o, w_key, w_value)
    k_p, v_p, state_p, total, w_q = project_partner(core, tok_p, w_k, w_v, state_o, w_query)
    weights = (w_q, w_k, w_v)
    along_x = pieces(total, "x")
    q_o, i_o, cot, cot_s = within(core, tok_o, w_q, k_o, v_o, cotangent[0])
    row, i_o, q_o, tok_t, cot_s, k_p = together(
        f32_sum(total, *along_x), i_o, q_o, tok_o, cot_s, k_p
    )
    along_y = pieces(row, "y")
    cot_p = swap(cot_s)
    q_p, i_p = within(core, tok_p, w_q, k_p, v_p)
    tt = turned(core, tok_t, tok_p)
    *along_y, tt, cot_p, q_p, i_p = together(*along_y, tt, cot_p, q_p, i_p)
    a_o, a_p, g, p_o, p_p, back_o, back_p, total = normed(
        core, i_o, i_p, q_o, q_p, state_o, state_p, along_x, along_y, cot, cot_p
    )
    along_x = pieces(total, "x")
    a_r = swap(a_p)
    dq = grad_q_of(core, k_o, k_p, v_o, v_p, g, p_o, p_p)
    part_q = weight_grad_all(core, tt, dq)
    row, part_q, g, a_r = together(f32_sum(total, *along_x), part_q, g, a_r)
    along_y = pieces(row, "y")
    came_q = ring_out(part_q[2], "x")
    dk, dv = grads_within(core, q_o, q_p, k_o, k_p, v_o, v_p, g)
    *along_y, dk, dv, c0, c1 = together(*along_y, dk, dv, *came_q)
    last_q = ring_near(part_q[1], part_q[3], (c0, c1), "x")
    dk, dv = grads_after(
        core, k_o, k_p, v_o, v_p, dk, dv, back_o, back_p, along_x, along_y
    )
    far_k, far_v = weight_grad(core, tt, [(dk, "x", 2), (dv, "y", 2)])
    far_k, far_v, dk, dv = together(far_k, far_v, dk, dv)
    came_k, came_v = ring_out(far_k, "x"), shift(far_v, "y", 1)
    near = weight_grad(core, tt, [(dk, "x", 1), (dk, "x", 3), (dv, "y", 1), (dv, "y", 3)])
    here_k, here_v = weight_grad(core, tt, [(dk, "x", 0), (dv, "y", 0)])
    ig_p = input_part(core, 1, (dq, dk, dv), weights)
    *near, dk, dv, here_k, here_v, ig_p, a_o, k0, k1, came_v, q0, q1 = together(
        *near, dk, dv, here_k, here_v, ig_p, a_o, *came_k, came_v, *last_q
    )
    last_k = ring_near(near[0], near[1], (k0, k1), "x")
    sum_q = f32_sum(part_q[0], q0, q1)
    flat = (16, 32, 512)
    up = jnp.concatenate([f32_sum(near[2], came_v).reshape(flat), sum_q[2, :2]], axis=0)
    down = jnp.concatenate([near[3].reshape(flat), sum_q[2, 2:]], axis=0)
    last_v = [shift(up, "y", 1), shift(down, "y", 3)]
    ig_r = swap(ig_p)
    attn_out = joined_heads(core, a_o, a_r)
    input_grad = input_part(core, 0, (dq, dk, dv), weights, ig_r)
    sum_q, input_grad, attn_out, k0, k1, v0, v1 = together(
        sum_q, input_grad, attn_out, *last_k, *last_v
    )
    sum_k = f32_sum(here_k, k0, k1)
    sum_v = f32_sum(here_v.reshape(flat), v0[:16], v1[:16]).reshape(4, 4, 32, 512)
    up_q = jnp.concatenate([f32_sum(sum_q[1, :2], v0[16:]), sum_q[1, 2:]], axis=0)
    down_q = jnp.concatenate([sum_q[3, :2], f32_sum(sum_q[3, 2:], v1[16:])], axis=0)
    up, down = jnp.stack([sum_k[1], up_q]), jnp.stack([sum_k[3], down_q])
    up, down, far = shift(up, "y", 1), shift(down, "y", 3), shift(sum_k[2], "y", 2)
    far_v, right = shift(sum_v[2], "x", 2), shift(sum_v[3], "x", 3)
    right, last_v = together(right, sum_v[1])
    sum_v = f32_sum(sum_v[0], far_v, right, shift(last_v, "x", 1))
    sum_k = f32_sum(sum_k[0], up[0], down[0], far)
    sum_q = f32_sum(sum_q[0], up[1], down[1])
    summed = spread(jnp.concatenate([sum_q, sum_k, sum_v], axis=-1), "z")
    came = swap(jnp.where(late, summed[:16], summed[16:]))
    return (attn_out[None], input_grad[None], *assembled(core, summed, came))


def solution(mesh):
    finer = Mesh(mesh.devices.reshape(4, 4, 2, mesh.shape["dp"]), ("y", "x", "c", "z"))
    return jax.shard_map(
        per_device,
        mesh=finer,
        in_specs=(P("z", CTX, None), P(), P(), P(), P("z", CTX, None)),
        out_specs=(
            P("z", CTX, None),
            P("z", CTX, None),
            P(CTX_DP, None),
            P(CTX_DP, None),
            P(CTX_DP, None),
        ),
        check_vma=False,
    )
```

```python
import jax
import jax.numpy as jnp
from jax import lax
from jax.experimental import pallas as pl
from jax.experimental.pallas import tpu as pltpu
from jax.sharding import Mesh
from jax.sharding import PartitionSpec as P

DH = 128
TOK = 512
EPS = 1e-05
CTX = ("y", "x", "c")
CTX_DP = ("y", "x", "c", "z")
BF = jnp.bfloat16
F32 = jnp.float32
MB = 1 << 20
LOW = slice(0, 256)
HIGH = slice(256, 512)


def dot(a, b, ca=1, cb=0):
    return lax.dot_general(a, b, (((ca,), (cb,)), ((), ())), preferred_element_type=F32)


def causal(x, turned=False):
    rows = lax.broadcasted_iota(jnp.int32, x.shape, 0)
    cols = lax.broadcasted_iota(jnp.int32, x.shape, 1)
    keep = rows <= cols if turned else rows >= cols
    return jnp.where(keep, x, 0.0).astype(BF)


def head(h):
    if isinstance(h, int):
        return slice(h * DH, (h + 1) * DH)
    return pl.ds(pl.multiple_of(h * DH, DH), DH)


def each_head(body):
    for h in range(4):
        body(h)


def looped_head(body):
    def step(h, carry):
        body(h)
        return carry

    lax.fori_loop(0, 4, step, 0)


def call(kernel, core, grid, ins, outs, flops, moved, limit=20):
    return pl.pallas_call(
        kernel,
        out_shape=[jax.ShapeDtypeStruct(s, d) for s, d, _, _ in outs],
        grid_spec=pltpu.PrefetchScalarGridSpec(
            num_scalar_prefetch=1,
            grid=(grid,),
            in_specs=[pl.BlockSpec(b, m) for _, b, m in ins],
            out_specs=[pl.BlockSpec(b, m) for _, _, b, m in outs],
        ),
        compiler_params=pltpu.CompilerParams(
            dimension_semantics=("arbitrary",), vmem_limit_bytes=limit * MB
        ),
        cost_estimate=pl.CostEstimate(flops=flops, bytes_accessed=moved, transcendentals=0),
    )(core, *[a for a, _, _ in ins])


def local(kernel, core, ins, outs, hbm_in=0, hbm_out=0, scratch=()):
    vmem, hbm = pl.BlockSpec(memory_space=pltpu.VMEM), pl.BlockSpec(memory_space=pltpu.HBM)
    return pl.pallas_call(
        kernel,
        out_shape=[jax.ShapeDtypeStruct(s, d) for s, d in outs],
        in_specs=[pl.BlockSpec(memory_space=pltpu.SMEM)]
        + [vmem] * (len(ins) - hbm_in)
        + [hbm] * hbm_in,
        out_specs=[vmem] * (len(outs) - hbm_out) + [hbm] * hbm_out,
        scratch_shapes=list(scratch),
        compiler_params=pltpu.CompilerParams(vmem_limit_bytes=20 * MB),
        cost_estimate=pl.CostEstimate(flops=1000000, bytes_accessed=1000, transcendentals=0),
    )(core, *ins)


def whole(j, c):
    return (0, 0)


def tall(j, c):
    return (j, 0)


def wide(j, c):
    return (0, j)


def mine(j, c):
    return (0, c[0] * 2 + j)


def in_hbm(*arrays):
    return [pltpu.with_memory_space_constraint(t, pltpu.HBM) for t in arrays]


def half_of(which):
    return pl.ds(pl.multiple_of(which * 512, 512), 512)


def project_own(core, tok, wk, wv):
    def kernel(c, t, b, d, k, v, s, low, bh, dh, tv, sems):
        copies = [[], [], []]
        for i in range(4):
            rows, part = pl.ds(i * 512, 512), pl.ds(i * 128, 128)
            copies[0].append(pltpu.make_async_copy(t.at[part], tv.at[part], sems.at[0, i]))
            for n, (src, dst) in enumerate(((b, bh), (d, dh))):
                half = src.at[rows, half_of(c[0])]
                copies[n + 1].append(pltpu.make_async_copy(half, dst.at[rows], sems.at[n + 1, i]))
        for copy in sum(copies, []):
            copy.start()
        for copy in copies[0]:
            copy.wait()
        for n, (w, out) in enumerate(((bh, k), (dh, v))):
            for copy in copies[n + 1]:
                copy.wait()
            out[...] = dot(tv[...], w[...]).astype(BF)
        for h in range(4):
            first = dot(k[LOW, head(h)], v[LOW, head(h)], 0, 0)
            low[head(h), :] = first.astype(BF)
            s[head(h), :] = (first + dot(k[HIGH, head(h)], v[HIGH, head(h)], 0, 0)).astype(BF)

    row, weight = ((TOK, 512), BF), ((2048, 512), BF)
    return local(
        kernel,
        core,
        in_hbm(tok, wk, wv),
        [row] * 2 + [((512, DH), BF)] * 2 + [weight] * 2,
        hbm_in=3,
        scratch=[pltpu.VMEM((TOK, 2048), BF), pltpu.SemaphoreType.DMA((3, 4))],
    )


def project_partner(core, tok, wk, wv, state, wq):
    def kernel(c, t, b, d, so, a, k, v, s, low, total, ah, sem):
        copy = pltpu.make_async_copy(a.at[:, half_of(c[0])], ah, sem)
        copy.start()
        k[...] = dot(t[...], b[...]).astype(BF)
        v[...] = dot(t[...], d[...]).astype(BF)
        for h in range(4):
            first = dot(k[LOW, head(h)], v[LOW, head(h)], 0, 0)
            low[head(h), :] = first.astype(BF)
            st = (first + dot(k[HIGH, head(h)], v[HIGH, head(h)], 0, 0)).astype(BF)
            s[head(h), :] = st
            total[head(h), :] = (st.astype(F32) + so[head(h), :].astype(F32)).astype(BF)
        copy.wait()

    row = ((TOK, 512), BF)
    return local(
        kernel,
        core,
        [tok, wk, wv, state, *in_hbm(wq)],
        [row] * 2 + [((512, DH), BF)] * 3 + [((2048, 512), BF)],
        hbm_in=1,
        scratch=[pltpu.SemaphoreType.DMA],
    )


HALVES = (LOW, HIGH)


def diagonal(q, k, x):
    return [dot(causal(dot(q[r], k[r], 1, 1)), x[r]) for r in HALVES]


def diagonal_turned(q, k, x):
    return [dot(causal(dot(k[r], q[r], 1, 1), True), x[r]) for r in HALVES]


def masked_sum(refs, at, reverse):
    total = None
    for r, d in zip(refs, (1, 3, 2)):
        passed = at + (4 - d) < 4 if reverse else at >= d
        piece = r[...].astype(F32) * jnp.where(passed, 1.0, 0.0)
        total = piece if total is None else total + piece
    return total


def within(core, tok, wq, k, v, cot=None):
    fetch = cot is not None

    def kernel(c, t, a, ko, vo, *refs):
        copies = []
        if fetch:
            ct, qo, out, mine_ct, other_ct, sems = refs
            copies = [
                pltpu.make_async_copy(ct.at[:, half_of(1 - c[0])], other_ct, sems.at[0]),
                pltpu.make_async_copy(ct.at[:, half_of(c[0])], mine_ct, sems.at[1]),
            ]
        else:
            qo, out = refs
        for copy in copies:
            copy.start()
        qo[...] = dot(t[...], a[...]).astype(BF)

        @each_head
        def _(h):
            low, high = diagonal(qo[:, head(h)], ko[:, head(h)], vo[:, head(h)])
            out[:256, head(h)] = low
            out[256:, head(h)] = high

        for copy in copies:
            copy.wait()

    row = ((TOK, 512), BF)
    return local(
        kernel,
        core,
        [tok, wq, k, v] + (in_hbm(cot) if fetch else []),
        [row, ((TOK, 512), F32)] + [row] * (2 if fetch else 0),
        hbm_in=1 if fetch else 0,
        scratch=[pltpu.SemaphoreType.DMA((2,))] if fetch else [],
    )


def turned(core, tok_o, tok_p):
    def kernel(c, to, tp, out):
        out[:, :TOK] = to[...].T
        out[:, TOK:] = tp[...].T

    return call(
        kernel,
        core,
        4,
        [(tok_o, (TOK, 512), wide), (tok_p, (TOK, 512), wide)],
        [((2048, 2 * TOK), BF, (512, 2 * TOK), tall)],
        1000000,
        8 * MB,
    )[0]


def normed(core, i_o, i_p, q_o, q_p, states, lows, along_x, along_y, cot, cot_p):
    def kernel(c, io, ip, qo, qp, so, sp, lo, lp, x1, x3, x2, y1, y3, y2, co, cp, *outs):
        ao, ap, g, po, pp, ho, hp, bo, bp, eo, ep, total = outs
        before = masked_sum((x1, x3, x2), c[2], False) + masked_sum((y1, y3, y2), c[1], False)
        late = c[0].astype(F32)
        base_o = before + sp[...].astype(F32) * late
        base_p = before + so[...].astype(F32) * (1.0 - late)
        po[...] = base_o.astype(BF)
        pp[...] = base_p.astype(BF)
        ho[...] = (base_o + lo[...].astype(F32)).astype(BF)
        hp[...] = (base_p + lp[...].astype(F32)).astype(BF)

        @each_head
        def _(h):
            both = None
            for n, (it, q, p, up_h, a, ct, b, e) in enumerate(
                ((io, qo, po, ho, ao, co, bo, eo), (ip, qp, pp, hp, ap, cp, bp, ep))
            ):
                back = None
                for r, prefix in zip(HALVES, (p, up_h)):
                    qh = q[r, head(h)]
                    mixed = it[r, head(h)] + dot(qh, prefix[head(h), :])
                    inverse = lax.rsqrt(jnp.mean(mixed * mixed, axis=-1, keepdims=True) + EPS)
                    nm = mixed * inverse
                    up = ct[r, head(h)].astype(F32)
                    a[r, head(h)] = nm.astype(BF)
                    mean = jnp.mean(up * nm, axis=-1, keepdims=True)
                    gm = ((up - nm * mean) * inverse).astype(BF)
                    g[n * TOK + r.start : n * TOK + r.stop, head(h)] = gm
                    part = dot(qh, gm, 0, 0)
                    if r is HIGH:
                        e[head(h), :] = part.astype(BF)
                    back = part if back is None else back + part
                back = back.astype(BF)
                b[head(h), :] = back
                both = back.astype(F32) if both is None else both + back.astype(F32)
            total[head(h), :] = both.astype(BF)

    state = ((512, DH), BF)
    return local(
        kernel,
        core,
        [i_o, i_p, q_o, q_p, *states, *lows, *along_x, *along_y, cot, cot_p],
        [((TOK, 512), BF)] * 2 + [((2 * TOK, 512), BF)] + [state] * 9,
    )


def grad_q_of(core, k_o, k_p, v_o, v_p, g, p_o, p_p, h_o, h_p):
    def kernel(c, ko, kp, vo, vp, gr, po, pp, ho, hp, dq):
        @each_head
        def _(h):
            for n, (k, v, p, up) in enumerate(((ko, vo, po, ho), (kp, vp, pp, hp))):
                gh = gr[n * TOK : n * TOK + TOK, head(h)]
                parts = diagonal(gh, v[:, head(h)], k[:, head(h)])
                for r, part, prefix in zip(HALVES, parts, (p, up)):
                    past = dot(gh[r], prefix[head(h), :], 1, 1)
                    dq[n * TOK + r.start : n * TOK + r.stop, head(h)] = (part + past).astype(BF)

    return local(
        kernel,
        core,
        [k_o, k_p, v_o, v_p, g, p_o, p_p, h_o, h_p],
        [((2 * TOK, 512), BF)],
    )[0]


def grads_within(core, q_o, q_p, k_o, k_p, v_o, v_p, g):
    def kernel(c, qo, qp, ko, kp, vo, vp, gr, dk, dv):
        @each_head
        def _(h):
            for n, (q, k, v) in enumerate(((qo, ko, vo), (qp, kp, vp))):
                qh, kh, vh = q[:, head(h)], k[:, head(h)], v[:, head(h)]
                gh = gr[n * TOK : n * TOK + TOK, head(h)]
                for left, right, x, out in ((gh, vh, qh, dk), (qh, kh, gh, dv)):
                    low, high = diagonal_turned(left, right, x)
                    out[n * TOK : n * TOK + 256, head(h)] = low
                    out[n * TOK + 256 : n * TOK + 512, head(h)] = high

    return local(
        kernel,
        core,
        [q_o, q_p, k_o, k_p, v_o, v_p, g],
        [((2 * TOK, 512), F32)] * 2,
    )


def grads_after(core, k_o, k_p, v_o, v_p, dk, dv, backs, ends, along_x, along_y):
    def kernel(c, ko, kp, vo, vp, ak, av, bo, bp, eo, ep, x1, x3, x2, y1, y3, y2, ok, ov):
        after = masked_sum((x1, x3, x2), c[2], True) + masked_sum((y1, y3, y2), c[1], True)
        late = c[0].astype(F32)
        s_o = after + bp[...].astype(F32) * (1.0 - late)
        s_p = after + bo[...].astype(F32) * late
        for n, (k, v, s, e) in enumerate(((ko, vo, s_o, eo), (kp, vp, s_p, ep))):
            low = (s + e[...].astype(F32)).astype(BF)
            for r, suffix in zip(HALVES, (low, s.astype(BF))):
                rows = slice(n * TOK + r.start, n * TOK + r.stop)
                for h in range(4):
                    sh = suffix[head(h), :]
                    kh, vh = k[r, head(h)], v[r, head(h)]
                    ok[rows, head(h)] = (ak[rows, head(h)] + dot(vh, sh, 1, 1)).astype(BF)
                    ov[rows, head(h)] = (av[rows, head(h)] + dot(kh, sh)).astype(BF)

    return local(
        kernel,
        core,
        [k_o, k_p, v_o, v_p, dk, dv, *backs, *ends, *along_x, *along_y],
        [((2 * TOK, 512), BF)] * 2,
    )


def weight_grad(core, tt, jobs):
    n = len(jobs)

    def kernel(c, t, *refs):
        for m, (_, axis, step) in enumerate(jobs):
            g, out = refs[m], refs[n + m]
            if axis == "x":
                rows = t[:, (c[2] + step) % 4]
            elif axis == "y":
                rows = t[(c[1] + step) % 4]
            part = dot(rows.reshape(512, 2 * TOK), g[...]).astype(BF)
            for a in range(4):
                near = (a - c[1] + 4) % 4 if axis == "x" else (a - c[2] + 4) % 4
                for core_at in range(2):
                    for z in range(4):
                        row = a * 128 + core_at * 64 + z * 16
                        here = slice(core_at * 16, core_at * 16 + 16)
                        out[near, (z - c[3] + 4) % 4, here, :] = part[row : row + 16, :]

    return local(
        kernel,
        core,
        [tt.reshape(4, 4, 128, 2 * TOK)] + [g for g, _, _ in jobs],
        [((4, 4, 32, 512), BF)] * n,
    )


def weight_grad_all(core, tt, grad):
    def kernel(c, t, g, out):
        def at_y(y, carry):
            part = dot(t[y].reshape(512, 2 * TOK), g[...]).astype(BF)
            dy = (y - c[1] + 4) % 4
            for x in range(4):
                dx = (x - c[2] + 4) % 4
                for core_at in range(2):
                    for z in range(4):
                        row = x * 128 + core_at * 64 + z * 16
                        here = slice(core_at * 16, core_at * 16 + 16)
                        out[dx, dy, (z - c[3] + 4) % 4, here, :] = part[row : row + 16, :]
            return carry

        for y in range(4):
            at_y(y, 0)

    return local(
        kernel,
        core,
        [tt.reshape(4, 4, 128, 2 * TOK), grad],
        [((4, 4, 4, 32, 512), BF)],
    )[0]


def joined_heads(core, own, received):
    def kernel(c, o, r, out, sems):
        copies = [
            pltpu.make_async_copy(o, out.at[:, half_of(c[0])], sems.at[0]),
            pltpu.make_async_copy(r, out.at[:, half_of(1 - c[0])], sems.at[1]),
        ]
        for copy in copies:
            copy.start()
        for copy in copies:
            copy.wait()

    return local(
        kernel,
        core,
        [own, received],
        [((TOK, 1024), BF)],
        hbm_out=1,
        scratch=[pltpu.SemaphoreType.DMA((2,))],
    )[0]


def assembled(core, summed, came):
    def kernel(c, qkv, r, *outs):
        scale = 65536.0**-0.5
        mine = pl.ds(pl.multiple_of(c[0] * 16, 16), 16)
        here = pl.ds(pl.multiple_of(c[0] * 512, 512), 512)
        there = pl.ds(pl.multiple_of((1 - c[0]) * 512, 512), 512)
        for m, out in enumerate(outs):
            out[:, here] = qkv[mine, m * 512 : m * 512 + 512].astype(F32) * scale
            out[:, there] = r[:, m * 512 : m * 512 + 512].astype(F32) * scale

    return local(kernel, core, [summed, came], [((16, 1024), F32)] * 3)


def input_part(core, slot, grads, weights, received=None):
    final = received is not None

    def kernel(c, *refs):
        rows = slice(slot * TOK, slot * TOK + TOK)
        out = refs[7] if final else refs[6]
        def columns(j, carry):
            at = pl.ds(pl.multiple_of(j * 512, 512), 512)
            total = dot(refs[0][rows, :], refs[3][at, :], 1, 1)
            total = total + dot(refs[1][rows, :], refs[4][at, :], 1, 1)
            total = total + dot(refs[2][rows, :], refs[5][at, :], 1, 1)
            if final:
                held, sems = refs[8:]
                held[:, at] = (total + refs[6][:, at].astype(F32)).astype(BF)
                pltpu.make_async_copy(held.at[:, at], out.at[:, at], sems.at[j]).start()
            else:
                out[:, at] = total.astype(BF)
            return carry

        lax.fori_loop(0, 4, columns, 0)
        if final:
            held, sems = refs[8:]
            for j in range(4):
                at = pl.ds(j * 512, 512)
                pltpu.make_async_copy(held.at[:, at], out.at[:, at], sems.at[j]).wait()

    return local(
        kernel,
        core,
        [*grads, *weights] + ([received] if final else []),
        [((TOK, 2048), BF)],
        hbm_out=1 if final else 0,
        scratch=[pltpu.VMEM((TOK, 2048), BF), pltpu.SemaphoreType.DMA((4,))] if final else [],
    )[0]


def shift(v, axis, d):
    n = lax.axis_size(axis)
    return lax.ppermute(v, axis, [(i, (i + d) % n) for i in range(n)])


def swap(v):
    return lax.ppermute(v, "c", [(0, 1), (1, 0)])


def pieces(v, axis):
    return [shift(v, axis, d) for d in (1, 3, 2)]


def together(*values):
    return lax.optimization_barrier(values)


def f32_sum(*parts):
    total = parts[0].astype(F32)
    for p in parts[1:]:
        total = total + p.astype(F32)
    return total.astype(BF)


def ring_out(far, axis):
    return shift(far[:2], axis, 1), shift(far[2:], axis, 3)


def ring_near(up, down, came, axis):
    from_left, from_right = came
    up = jnp.concatenate([f32_sum(up[:2], from_left), up[2:]], axis=0)
    down = jnp.concatenate([down[:2], f32_sum(down[2:], from_right)], axis=0)
    return shift(up, axis, 1), shift(down, axis, 3)


def spread(blocks, axis):
    return f32_sum(blocks[0], *[shift(blocks[d], axis, d) for d in (2, 1, 3)])


def per_device(tokens, w_query, w_key, w_value, cotangent):
    c = lax.axis_index("c")
    core = jnp.stack([lax.axis_index(a) for a in ("c", "y", "x", "z")]).astype(jnp.int32)
    tok_o = tokens[0]
    tok_p = swap(tok_o)
    late = c == 1

    k_o, v_o, state_o, low_o, w_k, w_v = project_own(core, tok_o, w_key, w_value)
    k_p, v_p, state_p, low_p, total, w_q = project_partner(
        core, tok_p, w_k, w_v, state_o, w_query
    )
    weights = (w_q, w_k, w_v)
    along_x = pieces(total, "x")
    q_o, i_o, cot, cot_s = within(core, tok_o, w_q, k_o, v_o, cotangent[0])
    row, i_o, q_o, tok_t, cot_s, k_p = together(
        f32_sum(total, *along_x), i_o, q_o, tok_o, cot_s, k_p
    )
    along_y = pieces(row, "y")
    cot_p = swap(cot_s)
    q_p, i_p = within(core, tok_p, w_q, k_p, v_p)
    tt = turned(core, tok_t, tok_p)
    *along_y, tt, cot_p, q_p, i_p = together(*along_y, tt, cot_p, q_p, i_p)
    states, lows = (state_o, state_p), (low_o, low_p)
    a_o, a_p, g, p_o, p_p, h_o, h_p, back_o, back_p, end_o, end_p, total = normed(
        core, i_o, i_p, q_o, q_p, states, lows, along_x, along_y, cot, cot_p
    )
    along_x = pieces(total, "x")
    a_r = swap(a_p)
    dq = grad_q_of(core, k_o, k_p, v_o, v_p, g, p_o, p_p, h_o, h_p)
    part_q = weight_grad_all(core, tt, dq)
    row, part_q, g, a_r = together(f32_sum(total, *along_x), part_q, g, a_r)
    along_y = pieces(row, "y")
    came_q = ring_out(part_q[2], "x")
    dk, dv = grads_within(core, q_o, q_p, k_o, k_p, v_o, v_p, g)
    *along_y, dk, dv, c0, c1 = together(*along_y, dk, dv, *came_q)
    last_q = ring_near(part_q[1], part_q[3], (c0, c1), "x")
    dk, dv = grads_after(
        core, k_o, k_p, v_o, v_p, dk, dv, (back_o, back_p), (end_o, end_p), along_x, along_y
    )
    far_k, far_v = weight_grad(core, tt, [(dk, "x", 2), (dv, "y", 2)])
    far_k, far_v, dk, dv = together(far_k, far_v, dk, dv)
    came_k, came_v = ring_out(far_k, "x"), shift(far_v, "y", 1)
    near = weight_grad(core, tt, [(dk, "x", 1), (dk, "x", 3), (dv, "y", 1), (dv, "y", 3)])
    here_k, here_v = weight_grad(core, tt, [(dk, "x", 0), (dv, "y", 0)])
    ig_p = input_part(core, 1, (dq, dk, dv), weights)
    *near, dk, dv, here_k, here_v, ig_p, a_o, k0, k1, came_v, q0, q1 = together(
        *near, dk, dv, here_k, here_v, ig_p, a_o, *came_k, came_v, *last_q
    )
    last_k = ring_near(near[0], near[1], (k0, k1), "x")
    sum_q = f32_sum(part_q[0], q0, q1)
    flat = (16, 32, 512)
    up = jnp.concatenate([f32_sum(near[2], came_v).reshape(flat), sum_q[2, :2]], axis=0)
    down = jnp.concatenate([near[3].reshape(flat), sum_q[2, 2:]], axis=0)
    last_v = [shift(up, "y", 1), shift(down, "y", 3)]
    ig_r = swap(ig_p)
    attn_out = joined_heads(core, a_o, a_r)
    input_grad = input_part(core, 0, (dq, dk, dv), weights, ig_r)
    sum_q, input_grad, attn_out, k0, k1, v0, v1 = together(
        sum_q, input_grad, attn_out, *last_k, *last_v
    )
    sum_k = f32_sum(here_k, k0, k1)
    sum_v = f32_sum(here_v.reshape(flat), v0[:16], v1[:16]).reshape(4, 4, 32, 512)
    up_q = jnp.concatenate([f32_sum(sum_q[1, :2], v0[16:]), sum_q[1, 2:]], axis=0)
    down_q = jnp.concatenate([sum_q[3, :2], f32_sum(sum_q[3, 2:], v1[16:])], axis=0)
    up, down = jnp.stack([sum_k[1], up_q]), jnp.stack([sum_k[3], down_q])
    up, down, far = shift(up, "y", 1), shift(down, "y", 3), shift(sum_k[2], "y", 2)
    far_v, right = shift(sum_v[2], "x", 2), shift(sum_v[3], "x", 3)
    right, last_v = together(right, sum_v[1])
    sum_v = f32_sum(sum_v[0], far_v, right, shift(last_v, "x", 1))
    sum_k = f32_sum(sum_k[0], up[0], down[0], far)
    sum_q = f32_sum(sum_q[0], up[1], down[1])
    summed = spread(jnp.concatenate([sum_q, sum_k, sum_v], axis=-1), "z")
    came = swap(jnp.where(late, summed[:16], summed[16:]))
    return (attn_out[None], input_grad[None], *assembled(core, summed, came))


def solution(mesh):
    finer = Mesh(mesh.devices.reshape(4, 4, 2, mesh.shape["dp"]), ("y", "x", "c", "z"))
    return jax.shard_map(
        per_device,
        mesh=finer,
        in_specs=(P("z", CTX, None), P(), P(), P(), P("z", CTX, None)),
        out_specs=(
            P("z", CTX, None),
            P("z", CTX, None),
            P(CTX_DP, None),
            P(CTX_DP, None),
            P(CTX_DP, None),
        ),
        check_vma=False,
    )
```

```python
import jax
import jax.numpy as jnp
from jax import lax
from jax.experimental import pallas as pl
from jax.experimental.pallas import tpu as pltpu
from jax.sharding import Mesh
from jax.sharding import PartitionSpec as P

DH = 128
TOK = 512
EPS = 1e-05
CTX = ("y", "x", "c")
CTX_DP = ("y", "x", "c", "z")
BF = jnp.bfloat16
F32 = jnp.float32
MB = 1 << 20


def dot(a, b, ca=1, cb=0):
    return lax.dot_general(a, b, (((ca,), (cb,)), ((), ())), preferred_element_type=F32)


def causal(x, turned=False):
    rows = lax.broadcasted_iota(jnp.int32, x.shape, 0)
    cols = lax.broadcasted_iota(jnp.int32, x.shape, 1)
    keep = rows <= cols if turned else rows >= cols
    return jnp.where(keep, x, 0.0).astype(BF)


def head(h):
    if isinstance(h, int):
        return slice(h * DH, (h + 1) * DH)
    return pl.ds(pl.multiple_of(h * DH, DH), DH)


def each_head(body):
    for h in range(4):
        body(h)


def looped_head(body):
    def step(h, carry):
        body(h)
        return carry

    lax.fori_loop(0, 4, step, 0)


def call(kernel, core, grid, ins, outs, flops, moved, limit=20):
    return pl.pallas_call(
        kernel,
        out_shape=[jax.ShapeDtypeStruct(s, d) for s, d, _, _ in outs],
        grid_spec=pltpu.PrefetchScalarGridSpec(
            num_scalar_prefetch=1,
            grid=(grid,),
            in_specs=[pl.BlockSpec(b, m) for _, b, m in ins],
            out_specs=[pl.BlockSpec(b, m) for _, _, b, m in outs],
        ),
        compiler_params=pltpu.CompilerParams(
            dimension_semantics=("arbitrary",), vmem_limit_bytes=limit * MB
        ),
        cost_estimate=pl.CostEstimate(flops=flops, bytes_accessed=moved, transcendentals=0),
    )(core, *[a for a, _, _ in ins])


def local(kernel, core, ins, outs, hbm_in=0, hbm_out=0, scratch=()):
    vmem, hbm = pl.BlockSpec(memory_space=pltpu.VMEM), pl.BlockSpec(memory_space=pltpu.HBM)
    return pl.pallas_call(
        kernel,
        out_shape=[jax.ShapeDtypeStruct(s, d) for s, d in outs],
        in_specs=[pl.BlockSpec(memory_space=pltpu.SMEM)]
        + [vmem] * (len(ins) - hbm_in)
        + [hbm] * hbm_in,
        out_specs=[vmem] * (len(outs) - hbm_out) + [hbm] * hbm_out,
        scratch_shapes=list(scratch),
        compiler_params=pltpu.CompilerParams(vmem_limit_bytes=20 * MB),
        cost_estimate=pl.CostEstimate(flops=1000000, bytes_accessed=1000, transcendentals=0),
    )(core, *ins)


def whole(j, c):
    return (0, 0)


def tall(j, c):
    return (j, 0)


def wide(j, c):
    return (0, j)


def mine(j, c):
    return (0, c[0] * 2 + j)


def in_hbm(*arrays):
    return [pltpu.with_memory_space_constraint(t, pltpu.HBM) for t in arrays]


def half_of(which):
    return pl.ds(pl.multiple_of(which * 512, 512), 512)


def project_own(core, tok, wk, wv):
    def kernel(c, t, b, d, k, v, s, bh, dh, tv, sems):
        copies = [[], [], []]
        for i in range(4):
            rows, part = pl.ds(i * 512, 512), pl.ds(i * 128, 128)
            copies[0].append(pltpu.make_async_copy(t.at[part], tv.at[part], sems.at[0, i]))
            for n, (src, dst) in enumerate(((b, bh), (d, dh))):
                half = src.at[rows, half_of(c[0])]
                copies[n + 1].append(pltpu.make_async_copy(half, dst.at[rows], sems.at[n + 1, i]))
        for copy in sum(copies, []):
            copy.start()
        for copy in copies[0]:
            copy.wait()
        for n, (w, out) in enumerate(((bh, k), (dh, v))):
            for copy in copies[n + 1]:
                copy.wait()
            out[...] = dot(tv[...], w[...]).astype(BF)
        for h in range(4):
            s[head(h), :] = dot(k[:, head(h)], v[:, head(h)], 0, 0).astype(BF)

    row, weight = ((TOK, 512), BF), ((2048, 512), BF)
    return local(
        kernel,
        core,
        in_hbm(tok, wk, wv),
        [row] * 2 + [((512, DH), BF)] + [weight] * 2,
        hbm_in=3,
        scratch=[pltpu.VMEM((TOK, 2048), BF), pltpu.SemaphoreType.DMA((3, 4))],
    )


def project_partner(core, tok, wk, wv, state, wq):
    def kernel(c, t, b, d, so, a, k, v, s, total, ah, sem):
        copy = pltpu.make_async_copy(a.at[:, half_of(c[0])], ah, sem)
        copy.start()
        k[...] = dot(t[...], b[...]).astype(BF)
        v[...] = dot(t[...], d[...]).astype(BF)
        for h in range(4):
            st = dot(k[:, head(h)], v[:, head(h)], 0, 0).astype(BF)
            s[head(h), :] = st
            total[head(h), :] = (st.astype(F32) + so[head(h), :].astype(F32)).astype(BF)
        copy.wait()

    row = ((TOK, 512), BF)
    return local(
        kernel,
        core,
        [tok, wk, wv, state, *in_hbm(wq)],
        [row] * 2 + [((512, DH), BF)] * 2 + [((2048, 512), BF)],
        hbm_in=1,
        scratch=[pltpu.SemaphoreType.DMA],
    )


LOW = slice(0, 256)
HIGH = slice(256, 512)


HALVES = (LOW, HIGH)


def diagonal(q, k, x):
    return [dot(causal(dot(q[r], k[r], 1, 1)), x[r]) for r in HALVES]


def diagonal_turned(q, k, x):
    return [dot(causal(dot(k[r], q[r], 1, 1), True), x[r]) for r in HALVES]


def outer(a, b, r):
    return dot(a[r], b[r], 0, 0)


def masked_sum(refs, at, reverse):
    total = None
    for r, d in zip(refs, (1, 3, 2)):
        passed = at + (4 - d) < 4 if reverse else at >= d
        piece = r[...].astype(F32) * jnp.where(passed, 1.0, 0.0)
        total = piece if total is None else total + piece
    return total


def within(core, tok, wq, k, v, cot=None):
    fetch = cot is not None

    def kernel(c, t, a, ko, vo, *refs):
        copies = []
        if fetch:
            ct, qo, out, first, mine_ct, other_ct, sems = refs
            copies = [
                pltpu.make_async_copy(ct.at[:, half_of(1 - c[0])], other_ct, sems.at[0]),
                pltpu.make_async_copy(ct.at[:, half_of(c[0])], mine_ct, sems.at[1]),
            ]
        else:
            qo, out, first = refs
        for copy in copies:
            copy.start()
        qo[...] = dot(t[...], a[...]).astype(BF)

        @each_head
        def _(h):
            qh, kh, vh = qo[:, head(h)], ko[:, head(h)], vo[:, head(h)]
            low, high = diagonal(qh, kh, vh)
            state = outer(kh, vh, LOW).astype(BF)
            first[head(h), :] = state
            out[:256, head(h)] = low
            out[256:, head(h)] = high + dot(qh[HIGH], state)

        for copy in copies:
            copy.wait()

    row = ((TOK, 512), BF)
    return local(
        kernel,
        core,
        [tok, wq, k, v] + (in_hbm(cot) if fetch else []),
        [row, ((TOK, 512), F32), ((512, DH), BF)] + [row] * (2 if fetch else 0),
        hbm_in=1 if fetch else 0,
        scratch=[pltpu.SemaphoreType.DMA((2,))] if fetch else [],
    )


def turned(core, tok_o, tok_p):
    def kernel(c, to, tp, out):
        out[:, :TOK] = to[...].T
        out[:, TOK:] = tp[...].T

    return call(
        kernel,
        core,
        4,
        [(tok_o, (TOK, 512), wide), (tok_p, (TOK, 512), wide)],
        [((2048, 2 * TOK), BF, (512, 2 * TOK), tall)],
        1000000,
        8 * MB,
    )[0]


def normed(core, i_o, i_p, q_o, q_p, state_o, state_p, along_x, along_y, cot, cot_p):
    def kernel(c, io, ip, qo, qp, so, sp, x1, x3, x2, y1, y3, y2, co, cp, *outs):
        ao, ap, g, po, pp, bo, bp, total = outs
        before = masked_sum((x1, x3, x2), c[2], False) + masked_sum((y1, y3, y2), c[1], False)
        late = c[0].astype(F32)
        po[...] = (before + sp[...].astype(F32) * late).astype(BF)
        pp[...] = (before + so[...].astype(F32) * (1.0 - late)).astype(BF)

        @each_head
        def _(h):
            backs = []
            for n, (it, q, p, a, b) in enumerate(((io, qo, po, ao, bo), (ip, qp, pp, ap, bp))):
                rows = slice(n * TOK, n * TOK + TOK)
                qh = q[:, head(h)]
                mixed = it[:, head(h)] + dot(qh, p[head(h), :])
                inverse = lax.rsqrt(jnp.mean(mixed * mixed, axis=-1, keepdims=True) + EPS)
                nm = mixed * inverse
                up = (co if n == 0 else cp)[:, head(h)].astype(F32)
                a[:, head(h)] = nm.astype(BF)
                gm = ((up - nm * jnp.mean(up * nm, axis=-1, keepdims=True)) * inverse).astype(BF)
                g[rows, head(h)] = gm
                back = dot(qh, gm, 0, 0).astype(BF)
                b[head(h), :] = back
                backs.append(back.astype(F32))
            total[head(h), :] = (backs[0] + backs[1]).astype(BF)

    state = ((512, DH), BF)
    return local(
        kernel,
        core,
        [i_o, i_p, q_o, q_p, state_o, state_p, *along_x, *along_y, cot, cot_p],
        [((TOK, 512), BF)] * 2 + [((2 * TOK, 512), BF)] + [state] * 5,
    )


def grad_q_of(core, k_o, k_p, v_o, v_p, g, p_o, p_p, low_o, low_p):
    def kernel(c, ko, kp, vo, vp, gr, po, pp, lo, lp, dq):
        @each_head
        def _(h):
            for n, (k, v, p, low) in enumerate(((ko, vo, po, lo), (kp, vp, pp, lp))):
                gh = gr[n * TOK : n * TOK + TOK, head(h)]
                prefix = p[head(h), :]
                later = (prefix.astype(F32) + low[head(h), :].astype(F32)).astype(BF)
                parts = diagonal(gh, v[:, head(h)], k[:, head(h)])
                for r, part, before in zip(HALVES, parts, (prefix, later)):
                    past = dot(gh[r], before, 1, 1)
                    dq[n * TOK + r.start : n * TOK + r.stop, head(h)] = (part + past).astype(BF)

    return local(
        kernel,
        core,
        [k_o, k_p, v_o, v_p, g, p_o, p_p, low_o, low_p],
        [((2 * TOK, 512), BF)],
    )[0]


def grads_within(core, q_o, q_p, k_o, k_p, v_o, v_p, g):
    def kernel(c, qo, qp, ko, kp, vo, vp, gr, dk, dv):
        @each_head
        def _(h):
            for n, (q, k, v) in enumerate(((qo, ko, vo), (qp, kp, vp))):
                qh, kh, vh = q[:, head(h)], k[:, head(h)], v[:, head(h)]
                gh = gr[n * TOK : n * TOK + TOK, head(h)]
                back = outer(qh, gh, HIGH).astype(BF)
                low, high = diagonal_turned(gh, vh, qh)
                dk[n * TOK : n * TOK + 256, head(h)] = low + dot(vh[LOW], back, 1, 1)
                dk[n * TOK + 256 : n * TOK + 512, head(h)] = high
                low, high = diagonal_turned(qh, kh, gh)
                dv[n * TOK : n * TOK + 256, head(h)] = low + dot(kh[LOW], back)
                dv[n * TOK + 256 : n * TOK + 512, head(h)] = high

    return local(
        kernel,
        core,
        [q_o, q_p, k_o, k_p, v_o, v_p, g],
        [((2 * TOK, 512), F32)] * 2,
    )


def grads_after(core, k_o, k_p, v_o, v_p, dk, dv, back_o, back_p, along_x, along_y):
    def kernel(c, ko, kp, vo, vp, ak, av, bo, bp, x1, x3, x2, y1, y3, y2, ok, ov):
        after = masked_sum((x1, x3, x2), c[2], True) + masked_sum((y1, y3, y2), c[1], True)
        late = c[0].astype(F32)
        s_o = (after + bp[...].astype(F32) * (1.0 - late)).astype(BF)
        s_p = (after + bo[...].astype(F32) * late).astype(BF)
        for n, (k, v, s) in enumerate(((ko, vo, s_o), (kp, vp, s_p))):
            rows = slice(n * TOK, n * TOK + TOK)
            for h in range(4):
                sh = s[head(h), :]
                ok[rows, head(h)] = (ak[rows, head(h)] + dot(v[:, head(h)], sh, 1, 1)).astype(BF)
                ov[rows, head(h)] = (av[rows, head(h)] + dot(k[:, head(h)], sh)).astype(BF)

    return local(
        kernel,
        core,
        [k_o, k_p, v_o, v_p, dk, dv, back_o, back_p, *along_x, *along_y],
        [((2 * TOK, 512), BF)] * 2,
    )


def weight_grad(core, tt, jobs):
    n = len(jobs)

    def kernel(c, t, *refs):
        for m, (_, axis, step) in enumerate(jobs):
            g, out = refs[m], refs[n + m]
            if axis == "x":
                rows = t[:, (c[2] + step) % 4]
            elif axis == "y":
                rows = t[(c[1] + step) % 4]
            part = dot(rows.reshape(512, 2 * TOK), g[...]).astype(BF)
            for a in range(4):
                near = (a - c[1] + 4) % 4 if axis == "x" else (a - c[2] + 4) % 4
                for core_at in range(2):
                    for z in range(4):
                        row = a * 128 + core_at * 64 + z * 16
                        here = slice(core_at * 16, core_at * 16 + 16)
                        out[near, (z - c[3] + 4) % 4, here, :] = part[row : row + 16, :]

    return local(
        kernel,
        core,
        [tt.reshape(4, 4, 128, 2 * TOK)] + [g for g, _, _ in jobs],
        [((4, 4, 32, 512), BF)] * n,
    )


def weight_grad_all(core, tt, grad):
    def kernel(c, t, g, out):
        def at_y(y, carry):
            part = dot(t[y].reshape(512, 2 * TOK), g[...]).astype(BF)
            dy = (y - c[1] + 4) % 4
            for x in range(4):
                dx = (x - c[2] + 4) % 4
                for core_at in range(2):
                    for z in range(4):
                        row = x * 128 + core_at * 64 + z * 16
                        here = slice(core_at * 16, core_at * 16 + 16)
                        out[dx, dy, (z - c[3] + 4) % 4, here, :] = part[row : row + 16, :]
            return carry

        lax.fori_loop(0, 4, at_y, 0)

    return local(
        kernel,
        core,
        [tt.reshape(4, 4, 128, 2 * TOK), grad],
        [((4, 4, 4, 32, 512), BF)],
    )[0]


def joined_heads(core, own, received):
    def kernel(c, o, r, out, sems):
        copies = [
            pltpu.make_async_copy(o, out.at[:, half_of(c[0])], sems.at[0]),
            pltpu.make_async_copy(r, out.at[:, half_of(1 - c[0])], sems.at[1]),
        ]
        for copy in copies:
            copy.start()
        for copy in copies:
            copy.wait()

    return local(
        kernel,
        core,
        [own, received],
        [((TOK, 1024), BF)],
        hbm_out=1,
        scratch=[pltpu.SemaphoreType.DMA((2,))],
    )[0]


def assembled(core, summed, came):
    def kernel(c, qkv, r, *outs):
        scale = 65536.0**-0.5
        mine = pl.ds(pl.multiple_of(c[0] * 16, 16), 16)
        here = pl.ds(pl.multiple_of(c[0] * 512, 512), 512)
        there = pl.ds(pl.multiple_of((1 - c[0]) * 512, 512), 512)
        for m, out in enumerate(outs):
            out[:, here] = qkv[mine, m * 512 : m * 512 + 512].astype(F32) * scale
            out[:, there] = r[:, m * 512 : m * 512 + 512].astype(F32) * scale

    return local(kernel, core, [summed, came], [((16, 1024), F32)] * 3)


def input_part(core, slot, grads, weights, received=None):
    final = received is not None

    def kernel(c, *refs):
        rows = slice(slot * TOK, slot * TOK + TOK)
        out = refs[7] if final else refs[6]
        def columns(j, carry):
            at = pl.ds(pl.multiple_of(j * 512, 512), 512)
            total = dot(refs[0][rows, :], refs[3][at, :], 1, 1)
            total = total + dot(refs[1][rows, :], refs[4][at, :], 1, 1)
            total = total + dot(refs[2][rows, :], refs[5][at, :], 1, 1)
            if final:
                held, sems = refs[8:]
                held[:, at] = (total + refs[6][:, at].astype(F32)).astype(BF)
                pltpu.make_async_copy(held.at[:, at], out.at[:, at], sems.at[j]).start()
            else:
                out[:, at] = total.astype(BF)
            return carry

        lax.fori_loop(0, 4, columns, 0)
        if final:
            held, sems = refs[8:]
            for j in range(4):
                at = pl.ds(j * 512, 512)
                pltpu.make_async_copy(held.at[:, at], out.at[:, at], sems.at[j]).wait()

    return local(
        kernel,
        core,
        [*grads, *weights] + ([received] if final else []),
        [((TOK, 2048), BF)],
        hbm_out=1 if final else 0,
        scratch=[pltpu.VMEM((TOK, 2048), BF), pltpu.SemaphoreType.DMA((4,))] if final else [],
    )[0]


def shift(v, axis, d):
    n = lax.axis_size(axis)
    return lax.ppermute(v, axis, [(i, (i + d) % n) for i in range(n)])


def swap(v):
    return lax.ppermute(v, "c", [(0, 1), (1, 0)])


def pieces(v, axis):
    return [shift(v, axis, d) for d in (1, 3, 2)]


def together(*values):
    return lax.optimization_barrier(values)


def f32_sum(*parts):
    total = parts[0].astype(F32)
    for p in parts[1:]:
        total = total + p.astype(F32)
    return total.astype(BF)


def ring_out(far, axis):
    return shift(far[:2], axis, 1), shift(far[2:], axis, 3)


def ring_near(up, down, came, axis):
    from_left, from_right = came
    up = jnp.concatenate([f32_sum(up[:2], from_left), up[2:]], axis=0)
    down = jnp.concatenate([down[:2], f32_sum(down[2:], from_right)], axis=0)
    return shift(up, axis, 1), shift(down, axis, 3)


def spread(blocks, axis):
    return f32_sum(blocks[0], *[shift(blocks[d], axis, d) for d in (2, 1, 3)])


def per_device(tokens, w_query, w_key, w_value, cotangent):
    c = lax.axis_index("c")
    core = jnp.stack([lax.axis_index(a) for a in ("c", "y", "x", "z")]).astype(jnp.int32)
    tok_o = tokens[0]
    tok_p = swap(tok_o)
    late = c == 1

    k_o, v_o, state_o, w_k, w_v = project_own(core, tok_o, w_key, w_value)
    k_p, v_p, state_p, total, w_q = project_partner(core, tok_p, w_k, w_v, state_o, w_query)
    weights = (w_q, w_k, w_v)
    along_x = pieces(total, "x")
    q_o, i_o, low_o, cot, cot_s = within(core, tok_o, w_q, k_o, v_o, cotangent[0])
    row, i_o, q_o, tok_t, cot_s, k_p = together(
        f32_sum(total, *along_x), i_o, q_o, tok_o, cot_s, k_p
    )
    along_y = pieces(row, "y")
    cot_p = swap(cot_s)
    q_p, i_p, low_p = within(core, tok_p, w_q, k_p, v_p)
    tt = turned(core, tok_t, tok_p)
    *along_y, tt, cot_p, q_p, i_p = together(*along_y, tt, cot_p, q_p, i_p)
    a_o, a_p, g, p_o, p_p, back_o, back_p, total = normed(
        core, i_o, i_p, q_o, q_p, state_o, state_p, along_x, along_y, cot, cot_p
    )
    along_x = pieces(total, "x")
    a_r = swap(a_p)
    dq = grad_q_of(core, k_o, k_p, v_o, v_p, g, p_o, p_p, low_o, low_p)
    part_q = weight_grad_all(core, tt, dq)
    row, part_q, g, a_r = together(f32_sum(total, *along_x), part_q, g, a_r)
    along_y = pieces(row, "y")
    came_q = ring_out(part_q[2], "x")
    dk, dv = grads_within(core, q_o, q_p, k_o, k_p, v_o, v_p, g)
    *along_y, dk, dv, c0, c1 = together(*along_y, dk, dv, *came_q)
    last_q = ring_near(part_q[1], part_q[3], (c0, c1), "x")
    dk, dv = grads_after(
        core, k_o, k_p, v_o, v_p, dk, dv, back_o, back_p, along_x, along_y
    )
    far_k, far_v = weight_grad(core, tt, [(dk, "x", 2), (dv, "y", 2)])
    far_k, far_v, dk, dv = together(far_k, far_v, dk, dv)
    came_k, came_v = ring_out(far_k, "x"), shift(far_v, "y", 1)
    near = weight_grad(core, tt, [(dk, "x", 1), (dk, "x", 3), (dv, "y", 1), (dv, "y", 3)])
    here_k, here_v = weight_grad(core, tt, [(dk, "x", 0), (dv, "y", 0)])
    ig_p = input_part(core, 1, (dq, dk, dv), weights)
    *near, dk, dv, here_k, here_v, ig_p, a_o, k0, k1, came_v, q0, q1 = together(
        *near, dk, dv, here_k, here_v, ig_p, a_o, *came_k, came_v, *last_q
    )
    last_k = ring_near(near[0], near[1], (k0, k1), "x")
    sum_q = f32_sum(part_q[0], q0, q1)
    flat = (16, 32, 512)
    up = jnp.concatenate([f32_sum(near[2], came_v).reshape(flat), sum_q[2, :2]], axis=0)
    down = jnp.concatenate([near[3].reshape(flat), sum_q[2, 2:]], axis=0)
    last_v = [shift(up, "y", 1), shift(down, "y", 3)]
    ig_r = swap(ig_p)
    attn_out = joined_heads(core, a_o, a_r)
    input_grad = input_part(core, 0, (dq, dk, dv), weights, ig_r)
    sum_q, input_grad, attn_out, k0, k1, v0, v1 = together(
        sum_q, input_grad, attn_out, *last_k, *last_v
    )
    sum_k = f32_sum(here_k, k0, k1)
    sum_v = f32_sum(here_v.reshape(flat), v0[:16], v1[:16]).reshape(4, 4, 32, 512)
    up_q = jnp.concatenate([f32_sum(sum_q[1, :2], v0[16:]), sum_q[1, 2:]], axis=0)
    down_q = jnp.concatenate([sum_q[3, :2], f32_sum(sum_q[3, 2:], v1[16:])], axis=0)
    up, down = jnp.stack([sum_k[1], up_q]), jnp.stack([sum_k[3], down_q])
    up, down, far = shift(up, "y", 1), shift(down, "y", 3), shift(sum_k[2], "y", 2)
    far_v, right = shift(sum_v[2], "x", 2), shift(sum_v[3], "x", 3)
    right, last_v = together(right, sum_v[1])
    sum_v = f32_sum(sum_v[0], far_v, right, shift(last_v, "x", 1))
    sum_k = f32_sum(sum_k[0], up[0], down[0], far)
    sum_q = f32_sum(sum_q[0], up[1], down[1])
    summed = spread(jnp.concatenate([sum_q, sum_k, sum_v], axis=-1), "z")
    came = swap(jnp.where(late, summed[:16], summed[16:]))
    return (attn_out[None], input_grad[None], *assembled(core, summed, came))


def solution(mesh):
    finer = Mesh(mesh.devices.reshape(4, 4, 2, mesh.shape["dp"]), ("y", "x", "c", "z"))
    return jax.shard_map(
        per_device,
        mesh=finer,
        in_specs=(P("z", CTX, None), P(), P(), P(), P("z", CTX, None)),
        out_specs=(
            P("z", CTX, None),
            P("z", CTX, None),
            P(CTX_DP, None),
            P(CTX_DP, None),
            P(CTX_DP, None),
        ),
        check_vma=False,
    )
```

```python
import jax
import jax.numpy as jnp
from jax import lax
from jax.experimental import pallas as pl
from jax.experimental.pallas import tpu as pltpu
from jax.sharding import Mesh
from jax.sharding import PartitionSpec as P

DH = 128
TOK = 512
EPS = 1e-05
CTX = ("y", "x", "c")
CTX_DP = ("y", "x", "c", "z")
BF = jnp.bfloat16
F32 = jnp.float32
MB = 1 << 20


def dot(a, b, ca=1, cb=0):
    return lax.dot_general(a, b, (((ca,), (cb,)), ((), ())), preferred_element_type=F32)


def causal(x, turned=False):
    rows = lax.broadcasted_iota(jnp.int32, x.shape, 0)
    cols = lax.broadcasted_iota(jnp.int32, x.shape, 1)
    keep = rows <= cols if turned else rows >= cols
    return jnp.where(keep, x, 0.0).astype(BF)


def head(h):
    if isinstance(h, int):
        return slice(h * DH, (h + 1) * DH)
    return pl.ds(pl.multiple_of(h * DH, DH), DH)


def each_head(body):
    for h in range(4):
        body(h)


def looped_head(body):
    def step(h, carry):
        body(h)
        return carry

    lax.fori_loop(0, 4, step, 0)


def call(kernel, core, grid, ins, outs, flops, moved, limit=20):
    return pl.pallas_call(
        kernel,
        out_shape=[jax.ShapeDtypeStruct(s, d) for s, d, _, _ in outs],
        grid_spec=pltpu.PrefetchScalarGridSpec(
            num_scalar_prefetch=1,
            grid=(grid,),
            in_specs=[pl.BlockSpec(b, m) for _, b, m in ins],
            out_specs=[pl.BlockSpec(b, m) for _, _, b, m in outs],
        ),
        compiler_params=pltpu.CompilerParams(
            dimension_semantics=("arbitrary",), vmem_limit_bytes=limit * MB
        ),
        cost_estimate=pl.CostEstimate(flops=flops, bytes_accessed=moved, transcendentals=0),
    )(core, *[a for a, _, _ in ins])


def local(kernel, core, ins, outs, hbm_in=0, hbm_out=0, scratch=()):
    vmem, hbm = pl.BlockSpec(memory_space=pltpu.VMEM), pl.BlockSpec(memory_space=pltpu.HBM)
    return pl.pallas_call(
        kernel,
        out_shape=[jax.ShapeDtypeStruct(s, d) for s, d in outs],
        in_specs=[pl.BlockSpec(memory_space=pltpu.SMEM)]
        + [vmem] * (len(ins) - hbm_in)
        + [hbm] * hbm_in,
        out_specs=[vmem] * (len(outs) - hbm_out) + [hbm] * hbm_out,
        scratch_shapes=list(scratch),
        compiler_params=pltpu.CompilerParams(vmem_limit_bytes=20 * MB),
        cost_estimate=pl.CostEstimate(flops=1000000, bytes_accessed=1000, transcendentals=0),
    )(core, *ins)


def whole(j, c):
    return (0, 0)


def tall(j, c):
    return (j, 0)


def wide(j, c):
    return (0, j)


def mine(j, c):
    return (0, c[0] * 2 + j)


def in_hbm(*arrays):
    return [pltpu.with_memory_space_constraint(t, pltpu.HBM) for t in arrays]


def half_of(which):
    return pl.ds(pl.multiple_of(which * 512, 512), 512)


def project_own(core, tok, wk, wv):
    def kernel(c, t, b, d, k, v, s, bh, dh, tv, sems):
        copies = [[], [], []]
        for i in range(4):
            rows, part = pl.ds(i * 512, 512), pl.ds(i * 128, 128)
            copies[0].append(pltpu.make_async_copy(t.at[part], tv.at[part], sems.at[0, i]))
            for n, (src, dst) in enumerate(((b, bh), (d, dh))):
                half = src.at[rows, half_of(c[0])]
                copies[n + 1].append(pltpu.make_async_copy(half, dst.at[rows], sems.at[n + 1, i]))
        for copy in sum(copies, []):
            copy.start()
        for copy in copies[0]:
            copy.wait()
        for n, (w, out) in enumerate(((bh, k), (dh, v))):
            for copy in copies[n + 1]:
                copy.wait()
            out[...] = dot(tv[...], w[...]).astype(BF)
        for h in range(4):
            s[head(h), :] = dot(k[:, head(h)], v[:, head(h)], 0, 0).astype(BF)

    row, weight = ((TOK, 512), BF), ((2048, 512), BF)
    return local(
        kernel,
        core,
        in_hbm(tok, wk, wv),
        [row] * 2 + [((512, DH), BF)] + [weight] * 2,
        hbm_in=3,
        scratch=[pltpu.VMEM((TOK, 2048), BF), pltpu.SemaphoreType.DMA((3, 4))],
    )


def project_partner(core, tok, wk, wv, state, wq):
    def kernel(c, t, b, d, so, a, k, v, s, total, ah, sem):
        copy = pltpu.make_async_copy(a.at[:, half_of(c[0])], ah, sem)
        copy.start()
        k[...] = dot(t[...], b[...]).astype(BF)
        v[...] = dot(t[...], d[...]).astype(BF)
        for h in range(4):
            st = dot(k[:, head(h)], v[:, head(h)], 0, 0).astype(BF)
            s[head(h), :] = st
            total[head(h), :] = (st.astype(F32) + so[head(h), :].astype(F32)).astype(BF)
        copy.wait()

    row = ((TOK, 512), BF)
    return local(
        kernel,
        core,
        [tok, wk, wv, state, *in_hbm(wq)],
        [row] * 2 + [((512, DH), BF)] * 2 + [((2048, 512), BF)],
        hbm_in=1,
        scratch=[pltpu.SemaphoreType.DMA],
    )


LOW = slice(0, 256)
HIGH = slice(256, 512)


HALVES = (LOW, HIGH)


def diagonal(q, k, x):
    return [dot(causal(dot(q[r], k[r], 1, 1)), x[r]) for r in HALVES]


def diagonal_turned(q, k, x):
    return [dot(causal(dot(k[r], q[r], 1, 1), True), x[r]) for r in HALVES]


def outer(a, b, r):
    return dot(a[r], b[r], 0, 0)


def masked_sum(refs, at, reverse):
    total = None
    for r, d in zip(refs, (1, 3, 2)):
        passed = at + (4 - d) < 4 if reverse else at >= d
        piece = r[...].astype(F32) * jnp.where(passed, 1.0, 0.0)
        total = piece if total is None else total + piece
    return total


def within(core, tok, wq, k, v, cot=None):
    fetch = cot is not None

    def kernel(c, t, a, ko, vo, *refs):
        copies = []
        if fetch:
            ct, qo, out, first, mine_ct, other_ct, sems = refs
            copies = [
                pltpu.make_async_copy(ct.at[:, half_of(1 - c[0])], other_ct, sems.at[0]),
                pltpu.make_async_copy(ct.at[:, half_of(c[0])], mine_ct, sems.at[1]),
            ]
        else:
            qo, out, first = refs
        for copy in copies:
            copy.start()
        qo[...] = dot(t[...], a[...]).astype(BF)

        @each_head
        def _(h):
            qh, kh, vh = qo[:, head(h)], ko[:, head(h)], vo[:, head(h)]
            low, high = diagonal(qh, kh, vh)
            state = outer(kh, vh, LOW).astype(BF)
            first[head(h), :] = state
            out[:256, head(h)] = low
            out[256:, head(h)] = high + dot(qh[HIGH], state)

        for copy in copies:
            copy.wait()

    row = ((TOK, 512), BF)
    return local(
        kernel,
        core,
        [tok, wq, k, v] + (in_hbm(cot) if fetch else []),
        [row, ((TOK, 512), F32), ((512, DH), BF)] + [row] * (2 if fetch else 0),
        hbm_in=1 if fetch else 0,
        scratch=[pltpu.SemaphoreType.DMA((2,))] if fetch else [],
    )


def turned(core, tok_o, tok_p):
    def kernel(c, to, tp, out):
        out[:, :TOK] = to[...].T
        out[:, TOK:] = tp[...].T

    return call(
        kernel,
        core,
        4,
        [(tok_o, (TOK, 512), wide), (tok_p, (TOK, 512), wide)],
        [((2048, 2 * TOK), BF, (512, 2 * TOK), tall)],
        1000000,
        8 * MB,
    )[0]


def normed(core, i_o, i_p, q_o, q_p, state_o, state_p, along_x, along_y, cot, cot_p):
    def kernel(c, io, ip, qo, qp, so, sp, x1, x3, x2, y1, y3, y2, co, cp, *outs):
        ao, ap, g, po, pp, bo, bp, total = outs
        before = masked_sum((x1, x3, x2), c[2], False) + masked_sum((y1, y3, y2), c[1], False)
        late = c[0].astype(F32)
        po[...] = (before + sp[...].astype(F32) * late).astype(BF)
        pp[...] = (before + so[...].astype(F32) * (1.0 - late)).astype(BF)

        @each_head
        def _(h):
            backs = []
            for n, (it, q, p, a, b) in enumerate(((io, qo, po, ao, bo), (ip, qp, pp, ap, bp))):
                rows = slice(n * TOK, n * TOK + TOK)
                qh = q[:, head(h)]
                mixed = it[:, head(h)] + dot(qh, p[head(h), :])
                inverse = lax.rsqrt(jnp.mean(mixed * mixed, axis=-1, keepdims=True) + EPS)
                nm = mixed * inverse
                up = (co if n == 0 else cp)[:, head(h)].astype(F32)
                a[:, head(h)] = nm.astype(BF)
                gm = ((up - nm * jnp.mean(up * nm, axis=-1, keepdims=True)) * inverse).astype(BF)
                g[rows, head(h)] = gm
                back = dot(qh, gm, 0, 0).astype(BF)
                b[head(h), :] = back
                backs.append(back.astype(F32))
            total[head(h), :] = (backs[0] + backs[1]).astype(BF)

    state = ((512, DH), BF)
    return local(
        kernel,
        core,
        [i_o, i_p, q_o, q_p, state_o, state_p, *along_x, *along_y, cot, cot_p],
        [((TOK, 512), BF)] * 2 + [((2 * TOK, 512), BF)] + [state] * 5,
    )


def grad_q_of(core, k_o, k_p, v_o, v_p, g, p_o, p_p, low_o, low_p):
    def kernel(c, ko, kp, vo, vp, gr, po, pp, lo, lp, dq):
        @each_head
        def _(h):
            for n, (k, v, p, low) in enumerate(((ko, vo, po, lo), (kp, vp, pp, lp))):
                gh = gr[n * TOK : n * TOK + TOK, head(h)]
                prefix = p[head(h), :]
                later = (prefix.astype(F32) + low[head(h), :].astype(F32)).astype(BF)
                parts = diagonal(gh, v[:, head(h)], k[:, head(h)])
                for r, part, before in zip(HALVES, parts, (prefix, later)):
                    past = dot(gh[r], before, 1, 1)
                    dq[n * TOK + r.start : n * TOK + r.stop, head(h)] = (part + past).astype(BF)

    return local(
        kernel,
        core,
        [k_o, k_p, v_o, v_p, g, p_o, p_p, low_o, low_p],
        [((2 * TOK, 512), BF)],
    )[0]


def grads_within(core, q_o, q_p, k_o, k_p, v_o, v_p, g):
    def kernel(c, qo, qp, ko, kp, vo, vp, gr, dk, dv):
        @each_head
        def _(h):
            for n, (q, k, v) in enumerate(((qo, ko, vo), (qp, kp, vp))):
                qh, kh, vh = q[:, head(h)], k[:, head(h)], v[:, head(h)]
                gh = gr[n * TOK : n * TOK + TOK, head(h)]
                back = outer(qh, gh, HIGH).astype(BF)
                low, high = diagonal_turned(gh, vh, qh)
                dk[n * TOK : n * TOK + 256, head(h)] = low + dot(vh[LOW], back, 1, 1)
                dk[n * TOK + 256 : n * TOK + 512, head(h)] = high
                low, high = diagonal_turned(qh, kh, gh)
                dv[n * TOK : n * TOK + 256, head(h)] = low + dot(kh[LOW], back)
                dv[n * TOK + 256 : n * TOK + 512, head(h)] = high

    return local(
        kernel,
        core,
        [q_o, q_p, k_o, k_p, v_o, v_p, g],
        [((2 * TOK, 512), F32)] * 2,
    )


def grads_after(core, k_o, k_p, v_o, v_p, dk, dv, back_o, back_p, along_x, along_y):
    def kernel(c, ko, kp, vo, vp, ak, av, bo, bp, x1, x3, x2, y1, y3, y2, ok, ov):
        after = masked_sum((x1, x3, x2), c[2], True) + masked_sum((y1, y3, y2), c[1], True)
        late = c[0].astype(F32)
        s_o = (after + bp[...].astype(F32) * (1.0 - late)).astype(BF)
        s_p = (after + bo[...].astype(F32) * late).astype(BF)
        for n, (k, v, s) in enumerate(((ko, vo, s_o), (kp, vp, s_p))):
            rows = slice(n * TOK, n * TOK + TOK)
            for h in range(4):
                sh = s[head(h), :]
                ok[rows, head(h)] = (ak[rows, head(h)] + dot(v[:, head(h)], sh, 1, 1)).astype(BF)
                ov[rows, head(h)] = (av[rows, head(h)] + dot(k[:, head(h)], sh)).astype(BF)

    return local(
        kernel,
        core,
        [k_o, k_p, v_o, v_p, dk, dv, back_o, back_p, *along_x, *along_y],
        [((2 * TOK, 512), BF)] * 2,
    )


def weight_grad(core, tt, jobs):
    n = len(jobs)

    def kernel(c, t, *refs):
        for m, (_, axis, step) in enumerate(jobs):
            g, out = refs[m], refs[n + m]
            if axis == "x":
                rows = t[:, (c[2] + step) % 4]
            elif axis == "y":
                rows = t[(c[1] + step) % 4]
            part = dot(rows.reshape(512, 2 * TOK), g[...]).astype(BF)
            for a in range(4):
                near = (a - c[1] + 4) % 4 if axis == "x" else (a - c[2] + 4) % 4
                for core_at in range(2):
                    for z in range(4):
                        row = a * 128 + core_at * 64 + z * 16
                        here = slice(core_at * 16, core_at * 16 + 16)
                        out[near, (z - c[3] + 4) % 4, here, :] = part[row : row + 16, :]

    return local(
        kernel,
        core,
        [tt.reshape(4, 4, 128, 2 * TOK)] + [g for g, _, _ in jobs],
        [((4, 4, 32, 512), BF)] * n,
    )


def weight_grad_all(core, tt, grad):
    def kernel(c, t, g, out):
        def at_y(y, carry):
            part = dot(t[y].reshape(512, 2 * TOK), g[...]).astype(BF)
            dy = (y - c[1] + 4) % 4
            for x in range(4):
                dx = (x - c[2] + 4) % 4
                for core_at in range(2):
                    for z in range(4):
                        row = x * 128 + core_at * 64 + z * 16
                        here = slice(core_at * 16, core_at * 16 + 16)
                        out[dx, dy, (z - c[3] + 4) % 4, here, :] = part[row : row + 16, :]
            return carry

        lax.fori_loop(0, 4, at_y, 0)

    return local(
        kernel,
        core,
        [tt.reshape(4, 4, 128, 2 * TOK), grad],
        [((4, 4, 4, 32, 512), BF)],
    )[0]


def joined_heads(core, own, received):
    def kernel(c, o, r, out, sems):
        copies = [
            pltpu.make_async_copy(o, out.at[:, half_of(c[0])], sems.at[0]),
            pltpu.make_async_copy(r, out.at[:, half_of(1 - c[0])], sems.at[1]),
        ]
        for copy in copies:
            copy.start()
        for copy in copies:
            copy.wait()

    return local(
        kernel,
        core,
        [own, received],
        [((TOK, 1024), BF)],
        hbm_out=1,
        scratch=[pltpu.SemaphoreType.DMA((2,))],
    )[0]


def assembled(core, summed, came):
    def kernel(c, qkv, r, *outs):
        scale = 65536.0**-0.5
        mine = pl.ds(pl.multiple_of(c[0] * 16, 16), 16)
        here = pl.ds(pl.multiple_of(c[0] * 512, 512), 512)
        there = pl.ds(pl.multiple_of((1 - c[0]) * 512, 512), 512)
        for m, out in enumerate(outs):
            out[:, here] = qkv[mine, m * 512 : m * 512 + 512].astype(F32) * scale
            out[:, there] = r[:, m * 512 : m * 512 + 512].astype(F32) * scale

    return local(kernel, core, [summed, came], [((16, 1024), F32)] * 3)


def input_part(core, slot, grads, weights, received=None):
    final = received is not None

    def kernel(c, *refs):
        rows = slice(slot * TOK, slot * TOK + TOK)
        out = refs[7] if final else refs[6]
        def columns(j, carry):
            at = pl.ds(pl.multiple_of(j * 512, 512), 512)
            total = dot(refs[0][rows, :], refs[3][at, :], 1, 1)
            total = total + dot(refs[1][rows, :], refs[4][at, :], 1, 1)
            total = total + dot(refs[2][rows, :], refs[5][at, :], 1, 1)
            if final:
                held, sems = refs[8:]
                held[:, at] = (total + refs[6][:, at].astype(F32)).astype(BF)
                pltpu.make_async_copy(held.at[:, at], out.at[:, at], sems.at[j]).start()
            else:
                out[:, at] = total.astype(BF)
            return carry

        lax.fori_loop(0, 4, columns, 0)
        if final:
            held, sems = refs[8:]
            for j in range(4):
                at = pl.ds(j * 512, 512)
                pltpu.make_async_copy(held.at[:, at], out.at[:, at], sems.at[j]).wait()

    return local(
        kernel,
        core,
        [*grads, *weights] + ([received] if final else []),
        [((TOK, 2048), BF)],
        hbm_out=1 if final else 0,
        scratch=[pltpu.VMEM((TOK, 2048), BF), pltpu.SemaphoreType.DMA((4,))] if final else [],
    )[0]


def shift(v, axis, d):
    n = lax.axis_size(axis)
    return lax.ppermute(v, axis, [(i, (i + d) % n) for i in range(n)])


def swap(v):
    return lax.ppermute(v, "c", [(0, 1), (1, 0)])


def pieces(v, axis):
    return [shift(v, axis, d) for d in (1, 3, 2)]


def together(*values):
    return lax.optimization_barrier(values)


def f32_sum(*parts):
    total = parts[0].astype(F32)
    for p in parts[1:]:
        total = total + p.astype(F32)
    return total.astype(BF)


def ring_out(far, axis):
    return shift(far[:2], axis, 1), shift(far[2:], axis, 3)


def ring_near(up, down, came, axis):
    from_left, from_right = came
    up = jnp.concatenate([f32_sum(up[:2], from_left), up[2:]], axis=0)
    down = jnp.concatenate([down[:2], f32_sum(down[2:], from_right)], axis=0)
    return shift(up, axis, 1), shift(down, axis, 3)


def spread(blocks, axis):
    return f32_sum(blocks[0], *[shift(blocks[d], axis, d) for d in (2, 1, 3)])


def per_device(tokens, w_query, w_key, w_value, cotangent):
    c = lax.axis_index("c")
    core = jnp.stack([lax.axis_index(a) for a in ("c", "y", "x", "z")]).astype(jnp.int32)
    tok_o = tokens[0]
    tok_p = swap(tok_o)
    late = c == 1

    k_o, v_o, state_o, w_k, w_v = project_own(core, tok_o, w_key, w_value)
    k_p, v_p, state_p, total, w_q = project_partner(core, tok_p, w_k, w_v, state_o, w_query)
    weights = (w_q, w_k, w_v)
    along_x = pieces(total, "x")
    q_o, i_o, low_o, cot, cot_s = within(core, tok_o, w_q, k_o, v_o, cotangent[0])
    row, i_o, q_o, tok_t, cot_s, k_p = together(
        f32_sum(total, *along_x), i_o, q_o, tok_o, cot_s, k_p
    )
    along_y = pieces(row, "y")
    cot_p = swap(cot_s)
    q_p, i_p, low_p = within(core, tok_p, w_q, k_p, v_p)
    tt = turned(core, tok_t, tok_p)
    *along_y, tt, cot_p, q_p, i_p = together(*along_y, tt, cot_p, q_p, i_p)
    a_o, a_p, g, p_o, p_p, back_o, back_p, total = normed(
        core, i_o, i_p, q_o, q_p, state_o, state_p, along_x, along_y, cot, cot_p
    )
    along_x = pieces(total, "x")
    a_r = swap(a_p)
    dq = grad_q_of(core, k_o, k_p, v_o, v_p, g, p_o, p_p, low_o, low_p)
    part_q = weight_grad_all(core, tt, dq)
    row, part_q, g, a_r = together(f32_sum(total, *along_x), part_q, g, a_r)
    along_y = pieces(row, "y")
    came_q = ring_out(part_q[2], "x")
    dk, dv = grads_within(core, q_o, q_p, k_o, k_p, v_o, v_p, g)
    *along_y, dk, dv, c0, c1 = together(*along_y, dk, dv, *came_q)
    last_q = ring_near(part_q[1], part_q[3], (c0, c1), "x")
    dk, dv = grads_after(
        core, k_o, k_p, v_o, v_p, dk, dv, back_o, back_p, along_x, along_y
    )
    far_k, far_v = weight_grad(core, tt, [(dk, "x", 2), (dv, "y", 2)])
    far_k, far_v, dk, dv = together(far_k, far_v, dk, dv)
    came_k, came_v = ring_out(far_k, "x"), shift(far_v, "y", 1)
    near = weight_grad(core, tt, [(dk, "x", 1), (dk, "x", 3), (dv, "y", 1), (dv, "y", 3)])
    ig_p = input_part(core, 1, (dq, dk, dv), weights)
    *near, dk, dv, ig_p, a_o, k0, k1, came_v, q0, q1 = together(
        *near, dk, dv, ig_p, a_o, *came_k, came_v, *last_q
    )
    last_k = ring_near(near[0], near[1], (k0, k1), "x")
    sum_q = f32_sum(part_q[0], q0, q1)
    flat = (16, 32, 512)
    up = jnp.concatenate([f32_sum(near[2], came_v).reshape(flat), sum_q[2, :2]], axis=0)
    down = jnp.concatenate([near[3].reshape(flat), sum_q[2, 2:]], axis=0)
    last_v = [shift(up, "y", 1), shift(down, "y", 3)]
    ig_r = swap(ig_p)
    here_k, here_v = weight_grad(core, tt, [(dk, "x", 0), (dv, "y", 0)])
    attn_out = joined_heads(core, a_o, a_r)
    input_grad = input_part(core, 0, (dq, dk, dv), weights, ig_r)
    sum_q, here_k, here_v, input_grad, attn_out, k0, k1, v0, v1 = together(
        sum_q, here_k, here_v, input_grad, attn_out, *last_k, *last_v
    )
    sum_k = f32_sum(here_k, k0, k1)
    sum_v = f32_sum(here_v.reshape(flat), v0[:16], v1[:16]).reshape(4, 4, 32, 512)
    up_q = jnp.concatenate([f32_sum(sum_q[1, :2], v0[16:]), sum_q[1, 2:]], axis=0)
    down_q = jnp.concatenate([sum_q[3, :2], f32_sum(sum_q[3, 2:], v1[16:])], axis=0)
    up, down = jnp.stack([sum_k[1], up_q]), jnp.stack([sum_k[3], down_q])
    up, down, far = shift(up, "y", 1), shift(down, "y", 3), shift(sum_k[2], "y", 2)
    far_v, right = shift(sum_v[2], "x", 2), shift(sum_v[3], "x", 3)
    right, last_v = together(right, sum_v[1])
    sum_v = f32_sum(sum_v[0], far_v, right, shift(last_v, "x", 1))
    sum_k = f32_sum(sum_k[0], up[0], down[0], far)
    sum_q = f32_sum(sum_q[0], up[1], down[1])
    summed = spread(jnp.concatenate([sum_q, sum_k, sum_v], axis=-1), "z")
    came = swap(jnp.where(late, summed[:16], summed[16:]))
    return (attn_out[None], input_grad[None], *assembled(core, summed, came))


def solution(mesh):
    finer = Mesh(mesh.devices.reshape(4, 4, 2, mesh.shape["dp"]), ("y", "x", "c", "z"))
    return jax.shard_map(
        per_device,
        mesh=finer,
        in_specs=(P("z", CTX, None), P(), P(), P(), P("z", CTX, None)),
        out_specs=(
            P("z", CTX, None),
            P("z", CTX, None),
            P(CTX_DP, None),
            P(CTX_DP, None),
            P(CTX_DP, None),
        ),
        check_vma=False,
    )
```
